32 devices in a mesh: fsdp: 16 (over z, x, core), seq: 2 (over y).
Axes of the slice: x: 2, y: 2, z: 4, core: 2. Of those that a mesh axis runs over, the one named last changes fastest.
Arguments:
- tokens: bfloat16 [8192, 1024], P(('fsdp', 'seq')), may hold values from -6 to 6
- cotangent: bfloat16 [8192, 1024], P(('fsdp', 'seq')), may hold values from -6 to 6
- doc_ids: int32 [8192], replicated, may hold values from 0 to 7, never falling along the last dimension, each value on 1 to 4096 neighbouring positions
- norm_gain: float32 [1024], replicated, may hold values from 0.7 to 6.5
- in_weight: float32 [1024, 4384], P(('fsdp', 'seq'))
- conv_params: float32 [5, 2304], replicated, may hold values from -0.5 to 0.5
- head_params: float32 [3, 32], replicated, may hold values from -6 to 2
- out_gain: float32 [2048], replicated, may hold values from 0.7 to 6.5
- out_weight: float32 [2048, 1024], P(('fsdp', 'seq'))
- norm_first: float32 [1024], replicated, may hold values from -20 to 20
- norm_second: float32 [1024], replicated, may hold values from 0.49152 to 8.192
- in_first: float32 [1024, 4384], P(('fsdp', 'seq')), may hold values from -32 to 32
- in_second: float32 [1024, 4384], P(('fsdp', 'seq')), may hold values from 1.024 to 16.384
- conv_first: float32 [5, 2304], replicated, may hold values from -24 to 24
- conv_second: float32 [5, 2304], replicated, may hold values from 0.65536 to 10.6496
- head_first: float32 [3, 32], replicated, may hold values from -64 to 64
- head_second: float32 [3, 32], replicated, may hold values from 4.096 to 65.536
- gain_first: float32 [2048], replicated, may hold values from -20 to 20
- gain_second: float32 [2048], replicated, may hold values from 0.49152 to 8.192
- out_first: float32 [2048, 1024], P(('fsdp', 'seq')), may hold values from -128 to 128
- out_second: float32 [2048, 1024], P(('fsdp', 'seq')), may hold values from 16.384 to 262.144
Outputs:
- mixed: bfloat16 [8192, 1024], P(('fsdp', 'seq'))
- grad_tokens: float32 [8192, 1024], P(('fsdp', 'seq'))
- new_norm_first: float32 [1024], replicated
- new_norm_second: float32 [1024], replicated
- new_norm_gain: float32 [1024], replicated
- new_in_first: float32 [1024, 4384], P(('fsdp', 'seq'))
- new_in_second: float32 [1024, 4384], P(('fsdp', 'seq'))
- new_in_weight: float32 [1024, 4384], P(('fsdp', 'seq'))
- new_conv_first: float32 [5, 2304], replicated
- new_conv_second: float32 [5, 2304], replicated
- new_conv_params: float32 [5, 2304], replicated
- new_head_first: float32 [3, 32], replicated
- new_head_second: float32 [3, 32], replicated
- new_head_params: float32 [3, 32], replicated
- new_gain_first: float32 [2048], replicated
- new_gain_second: float32 [2048], replicated
- new_out_gain: float32 [2048], replicated
- new_out_first: float32 [2048, 1024], P(('fsdp', 'seq'))
- new_out_second: float32 [2048, 1024], P(('fsdp', 'seq'))
- new_out_weight: float32 [2048, 1024], P(('fsdp', 'seq'))
The draws below stay inside these ranges and needn't reach their ends.
Inputs may be any that keep to these rules, and one draw needn't show every extreme that they name: `doc_ids`: document numbers never fall along the stream; each document has 1 to 4096 tokens and one has exactly 4096.
All inputs are finite; a program needn't handle non-finite values.
Results may differ from the reference program's by a relative error of at most 0.0031.
The reference program's roundings to bfloat16 on the way count: a program that leaves them out, or rounds other values in their place, can miss the bound.
Values may be sent and summed in bfloat16 or wider, within the bound.
A program may use at most 128 MiB of HBM per device.

```python
import math
import jax
import jax.numpy as jnp
import numpy as np
from jax import lax

D = 1024
HEADS = 32
HEAD_DIM = 64
NSTATE = 128
CONV = 4
SPAN = 256
STEP = 10
INNER = 2048
CHANNELS = 2304
PROJ = 4384
TOKENS = 8192
DOC_MAX = 4096
SEGS = 8
N_SEQ = 2


def rising_gain(key, entries, climb, spread):
    position = jnp.arange(entries, dtype=jnp.float32) / entries
    return (1.0 + climb * position) * jax.random.uniform(key, (entries,), jnp.float32, 1.0 - spread, 1.0 + spread)


def draw_norm_gain(key, part):
    key = jax.random.fold_in(key, 11)
    return rising_gain(key, D, 2.0, 0.2)


def draw_out_gain(key, part):
    key = jax.random.fold_in(key, 12)
    return rising_gain(key, INNER, 2.0, 0.2)


def draw_in_weight(key, part):
    key = jax.random.fold_in(key, 13)
    position = jnp.arange(D, dtype=jnp.float32) / D
    noise = jnp.clip(jax.random.normal(key, (D, PROJ), jnp.float32), -5.0, 5.0)
    ramp = 0.6 + 1.2 * position
    return noise * ramp[:, None] * (0.5 / math.sqrt(D))


def draw_out_weight(key, part):
    key = jax.random.fold_in(key, 14)
    position = jnp.arange(INNER, dtype=jnp.float32) / INNER
    noise = jnp.clip(jax.random.normal(key, (INNER, D), jnp.float32), -5.0, 5.0)
    ramp = 0.6 + 1.2 * position
    return noise * ramp[:, None] * (0.4 / math.sqrt(INNER))


def draw_head_params(key, part):
    key = jax.random.fold_in(key, 17)
    subkeys = jax.random.split(key, 3)
    bias_row = jax.random.uniform(subkeys[0], (HEADS,), jnp.float32, -6.0, -3.0)
    rate_row = jax.random.uniform(subkeys[1], (HEADS,), jnp.float32, -5.0, 2.0)
    skip_row = jax.random.uniform(subkeys[2], (HEADS,), jnp.float32, 0.5, 1.5)
    return jnp.stack([bias_row, rate_row, skip_row])


def level_of(stream_key, dims, shards, smallest, top_value):
    loudness, own = 1.0, jax.random.fold_in(stream_key, 6)
    for axis_at, parts in shards:
        heights = jnp.exp(jax.random.uniform(jax.random.fold_in(own, axis_at), (parts,), jnp.float32, smallest / len(shards), top_value / len(shards)))
        loudness = loudness * jnp.repeat(heights, dims[axis_at] // parts).reshape([-1 if axis == axis_at else 1 for axis in range(len(dims))])
    return loudness


def length_profile(amount, total, bound, slope):
    weights = [(1 << 20) // math.isqrt(standing ** slope) + 1 for standing in range(2, amount + 1)]
    spare, holding = total - bound - (amount - 1), [1] * (amount - 1)
    while spare > 0:
        free = [i for i in range(amount - 1) if holding[i] < bound]
        pool, left = sum([weights[i] for i in free]), spare
        for i in free:
            more = min(bound - holding[i], max(1, left * weights[i] // pool), spare)
            holding[i] = holding[i] + more
            spare = spare - more
    return np.array([bound] + holding)


def ragged(own_key, number_of, total, reach, lean):
    if number_of == 2:
        one = jax.random.randint(own_key, (), max(1, total - reach), min(reach, total - 1) + 1)
        return jnp.stack([one, total - one])
    lengths = jnp.asarray(length_profile(number_of, total, reach, lean), jnp.int32)
    twos = (number_of - 1) // 2
    giver, taker = lengths[1:1 + 2 * twos:2], lengths[2:2 + 2 * twos:2]
    margin = jnp.minimum(giver - 1, reach - taker)
    moved = jax.random.randint(jax.random.fold_in(own_key, 1), (twos,), 0, 1 << 20) % (margin + 1)
    lengths = lengths.at[1:1 + 2 * twos:2].set(giver - moved).at[2:2 + 2 * twos:2].set(taker + moved)
    return lengths[jax.random.permutation(jax.random.fold_in(own_key, 2), number_of)]


def normal_values(key, extent, scale, most, cuts=(), kind=jnp.bfloat16):
    drawn = scale * jax.random.normal(key, extent, jnp.float32)
    if cuts:
        drawn = drawn * level_of(key, extent, cuts, -0.22, 0.18)
    return jnp.clip(drawn, -most, most).astype(kind)


def setup_inputs(seed: int = 0) -> dict:
    seeds = jax.random.split(jax.random.key(seed), 22)
    return {
        "tokens": normal_values(seeds[0], (TOKENS, D), 1.0, 6.0, ((0, 32),)),
        "cotangent": normal_values(seeds[1], (TOKENS, D), 1.0, 6.0, ((0, 32),)),
        "doc_ids": jnp.searchsorted(jnp.cumsum(ragged(seeds[2], SEGS, TOKENS, DOC_MAX, 0)), jnp.arange(TOKENS), side="right").astype(jnp.int32),
        "norm_gain": draw_norm_gain(jax.random.fold_in(seeds[21], 71), 0),
        "in_weight": draw_in_weight(jax.random.fold_in(seeds[21], 71), 0),
        "conv_params": jnp.clip(jax.random.uniform(seeds[5], (CONV + 1, CHANNELS), jnp.float32, -0.5, 0.5), -0.5, 0.5),
        "head_params": draw_head_params(jax.random.fold_in(seeds[21], 71), 0),
        "out_gain": draw_out_gain(jax.random.fold_in(seeds[21], 71), 0),
        "out_weight": draw_out_weight(jax.random.fold_in(seeds[21], 71), 0),
        "norm_first": normal_values(seeds[9], (D,), (0.039 * TOKENS ** 0.5), 20.0, (), jnp.float32),
        "norm_second": jnp.clip(jnp.exp(jax.random.uniform(seeds[10], (D,), jnp.float32, math.log(0.49152), math.log(8.192))), 0.49152, 8.192),
        "in_first": normal_values(seeds[11], (D, PROJ), (0.055 * TOKENS ** 0.5), 32.0, ((0, 32),), jnp.float32),
        "in_second": jnp.clip(jnp.exp(math.log(16.384) - 2.7725887 * jax.random.uniform(seeds[12], (D, PROJ), jnp.float32) ** level_of(seeds[12], (D, PROJ), ((0, 32),), -0.2, 0.2)), 1.024, 16.384),
        "conv_first": normal_values(seeds[13], (CONV + 1, CHANNELS), (0.044 * TOKENS ** 0.5), 24.0, (), jnp.float32),
        "conv_second": jnp.clip(jnp.exp(jax.random.uniform(seeds[14], (CONV + 1, CHANNELS), jnp.float32, math.log(0.65536), math.log(10.6496))), 0.65536, 10.6496),
        "head_first": normal_values(seeds[15], (3, HEADS), (0.11 * TOKENS ** 0.5), 64.0, (), jnp.float32),
        "head_second": jnp.clip(jnp.exp(jax.random.uniform(seeds[16], (3, HEADS), jnp.float32, math.log(4.096), math.log(65.536))), 4.096, 65.536),
        "gain_first": normal_values(seeds[17], (INNER,), (0.039 * TOKENS ** 0.5), 20.0, (), jnp.float32),
        "gain_second": jnp.clip(jnp.exp(jax.random.uniform(seeds[18], (INNER,), jnp.float32, math.log(0.49152), math.log(8.192))), 0.49152, 8.192),
        "out_first": normal_values(seeds[19], (INNER, D), (0.22 * TOKENS ** 0.5), 128.0, ((0, 32),), jnp.float32),
        "out_second": jnp.clip(jnp.exp(math.log(262.144) - 2.7725887 * jax.random.uniform(seeds[20], (INNER, D), jnp.float32) ** level_of(seeds[20], (INNER, D), ((0, 32),), -0.2, 0.2)), 16.384, 262.144),
    }


EPS_NORM = 1e-05
BETA_ONE = 0.9
BETA_TWO = 0.999
ADAM_EPS = 1e-06
DECAY = 0.01
RATE = 0.5
PRECISE = lax.Precision.HIGHEST

@jax.custom_vjp
def low(v):
    return lax.optimization_barrier(v.astype(jnp.bfloat16)).astype(jnp.float32)

@jax.custom_vjp
def low_back(v):
    return v

def low_keep(v):
    return (low(v), None)

def low_pass(kept, grad):
    return (grad,)

def back_keep(v):
    return (v, None)

def back_low(kept, grad):
    return (low(grad),)
low.defvjp(low_keep, low_pass)
low_back.defvjp(back_keep, back_low)

def product(left, right):
    return jnp.dot(left, right, precision=PRECISE, preferred_element_type=jnp.float32)

def convolve(extended, doc_window, kernel):
    rows_out = extended.shape[-2] - (CONV - 1)
    doc_now = doc_window[CONV - 1:]
    result = kernel[CONV] + jnp.zeros(extended[..., CONV - 1:, :].shape, jnp.float32)
    for offset in range(CONV):
        first_row = CONV - 1 - offset
        matched = (doc_window[first_row:first_row + rows_out] == doc_now)[:, None]
        result = result + jnp.where(matched, extended[..., first_row:first_row + rows_out, :] * kernel[offset], 0.0)
    return result

def span_masks(step_sizes, doc_span, doc_before, decay_rate):
    rows_in = doc_span.shape[0]
    cumulative = jnp.cumsum(step_sizes * decay_rate, axis=0)
    by_head = jnp.transpose(cumulative)
    below_diag = jnp.tril(jnp.ones((rows_in, rows_in), dtype=bool))
    matched = (doc_span[:, None] == doc_span[None, :]) & below_diag
    weights = jnp.where(matched[None], jnp.exp(jnp.minimum(by_head[:, :, None] - by_head[:, None, :], 0.0)), 0.0)
    rising = jnp.exp(cumulative) * (doc_span == doc_before).astype(jnp.float32)[:, None]
    ending = jnp.exp(cumulative[-1][None, :] - cumulative) * (doc_span == doc_span[-1]).astype(jnp.float32)[:, None]
    return (weights, rising, ending)

def ssd_span(inner_heads, write_heads, read_heads, step_sizes, doc_span, doc_before, decay_rate, skip_gain, states):
    weights, rising, ending = span_masks(step_sizes, doc_span, doc_before, decay_rate)
    scores = jnp.einsum('ihn,jhn->hij', read_heads, write_heads, precision=PRECISE)
    scaled = step_sizes[:, :, None] * inner_heads
    within = jnp.einsum('hij,jhp->ihp', scores * weights, scaled, precision=PRECISE)
    carried = jnp.einsum('ihn,hnp->ihp', read_heads, states, precision=PRECISE) * rising[:, :, None]
    output = within + carried + skip_gain[None, :, None] * inner_heads
    new_states = rising[-1][:, None, None] * states + jnp.einsum('jhn,jhp->hnp', write_heads, ending[:, :, None] * scaled, precision=PRECISE)
    return (output, new_states)

def layer_forward(params, token_vals, doc_ids):
    norm_gain, in_weight, conv_params, head_params, out_gain, out_weight = params
    in_low = low(in_weight)
    out_low = low(out_weight)
    doc_padded = jnp.concatenate([jnp.full((CONV - 1,), -1, dtype=jnp.int32), doc_ids.astype(jnp.int32)])
    heads_group = HEADS // N_SEQ
    step_bias = head_params[0]
    decay_rate = -jnp.exp(head_params[1])
    skip_gain = head_params[2]
    kernel_inner = conv_params[:, :INNER]
    kernel_state = conv_params[:, INNER:]

    def span_step(carried, pieces):
        states, tail_inner, tail_state = carried
        block_rows, position = pieces
        doc_window = lax.dynamic_slice(doc_padded, (position * SPAN,), (SPAN + CONV - 1,))
        doc_now = doc_window[CONV - 1:]
        inv_rms = lax.rsqrt(lax.optimization_barrier(jnp.mean(block_rows * block_rows, axis=1, keepdims=True)) + EPS_NORM)
        normed = low(block_rows * inv_rms * norm_gain)
        projected = low(low_back(product(normed, in_low)))
        gate_vals = projected[:, :INNER]
        inner_raw = projected[:, INNER:2 * INNER]
        state_proj = projected[:, 2 * INNER:2 * INNER + 2 * NSTATE]
        step_raw = projected[:, 2 * INNER + 2 * NSTATE:]
        inner_ext = jnp.concatenate([tail_inner, inner_raw], axis=0)
        copies = low_back(jnp.broadcast_to(state_proj[None], (N_SEQ, SPAN, 2 * NSTATE)))
        state_ext = jnp.concatenate([tail_state, copies], axis=1)
        inner_conv = low(jax.nn.silu(convolve(inner_ext, doc_window, kernel_inner)))
        state_conv = low(jax.nn.silu(convolve(state_ext, doc_window, kernel_state)))
        write_heads = jnp.repeat(jnp.transpose(state_conv[:, :, :NSTATE], (1, 0, 2)), heads_group, axis=1)
        read_heads = jnp.repeat(jnp.transpose(state_conv[:, :, NSTATE:], (1, 0, 2)), heads_group, axis=1)
        step_sizes = jax.nn.softplus(step_raw + step_bias)
        doc_before = doc_window[CONV - 2]
        inner_heads = inner_conv.reshape(SPAN, HEADS, HEAD_DIM)
        ssd_out, new_states = ssd_span(inner_heads, write_heads, read_heads, step_sizes, doc_now, doc_before, decay_rate, skip_gain, states)
        y_low = low(low_back(ssd_out.reshape(SPAN, INNER)))
        gated = y_low * jax.nn.silu(gate_vals)
        inv_gated = lax.rsqrt(lax.optimization_barrier(jnp.mean(gated * gated, axis=1, keepdims=True)) + EPS_NORM)
        normed_out = low(gated * inv_gated * out_gain)
        mixed_rows = block_rows + product(normed_out, out_low)
        return ((new_states, inner_ext[SPAN:], state_ext[:, SPAN:]), mixed_rows)
    span_count = TOKENS // SPAN
    blocks = token_vals.reshape(span_count, SPAN, D)
    start_carry = (jnp.zeros((HEADS, NSTATE, HEAD_DIM), jnp.float32), jnp.zeros((CONV - 1, INNER), jnp.float32), jnp.zeros((N_SEQ, CONV - 1, 2 * NSTATE), jnp.float32))
    unused, outputs = lax.scan(jax.checkpoint(span_step), start_carry, (blocks, jnp.arange(span_count, dtype=jnp.int32)))
    return outputs.reshape(TOKENS, D)

def lamb_update(weight, grad, first, second):
    first_new = BETA_ONE * first + (1.0 - BETA_ONE) * grad
    second_new = BETA_TWO * second + (1.0 - BETA_TWO) * grad * grad
    update = first_new / (1.0 - BETA_ONE ** STEP) / (jnp.sqrt(second_new / (1.0 - BETA_TWO ** STEP)) + ADAM_EPS) + DECAY * weight
    ratio = jnp.sqrt(jnp.sum(weight * weight)) / (jnp.sqrt(jnp.sum(update * update)) + ADAM_EPS)
    return (first_new, second_new, weight - RATE * ratio * update)

def reference(tokens, cotangent, doc_ids, norm_gain, in_weight, conv_params, head_params, out_gain, out_weight, norm_first, norm_second, in_first, in_second, conv_first, conv_second, head_first, head_second, gain_first, gain_second, out_first, out_second):
    params = (norm_gain, in_weight, conv_params, head_params, out_gain, out_weight)

    def forward(weights_all, inputs_all):
        return layer_forward(weights_all, inputs_all, doc_ids)
    mixed, pullback = jax.vjp(forward, params, tokens.astype(jnp.float32))
    grads, grad_tokens = pullback(cotangent.astype(jnp.float32))
    norm_f, norm_s, norm_w = lamb_update(norm_gain, grads[0], norm_first, norm_second)
    in_f, in_s, in_w = lamb_update(in_weight, grads[1], in_first, in_second)
    conv_f, conv_s, conv_w = lamb_update(conv_params, grads[2], conv_first, conv_second)
    head_f, head_s, head_w = lamb_update(head_params, grads[3], head_first, head_second)
    gain_f, gain_s, gain_w = lamb_update(out_gain, grads[4], gain_first, gain_second)
    out_f, out_s, out_w = lamb_update(out_weight, grads[5], out_first, out_second)
    return (mixed.astype(jnp.bfloat16), grad_tokens, norm_f, norm_s, norm_w, in_f, in_s, in_w, conv_f, conv_s, conv_w, head_f, head_s, head_w, gain_f, gain_s, gain_w, out_f, out_s, out_w)
```

```python
import functools

import jax
import jax.numpy as jnp
from jax import lax
from jax.experimental import pallas as pl
from jax.experimental.pallas import tpu as pltpu
from jax.sharding import Mesh, PartitionSpec as P

HEADS = 32
HEAD_DIM = 64
NSTATE = 128
CONV = 4
SPAN = 256
STEP = 10
INNER = 2048
D = 1024

EPS_NORM = 1e-05
BETA_ONE = 0.9
BETA_TWO = 0.999
ADAM_EPS = 1e-06
DECAY = 0.01
RATE = 0.5

PLANE = 8
HERE = HEADS // PLANE
WIDE = HERE * HEAD_DIM
STATES = 2 * NSTATE
LOCAL = WIDE + STATES
PACK = NSTATE + 8
MAIN = 2 * WIDE
SHARED = STATES + 128
SMALL = 24
TP = ("sub", "seq")
ALL = ("grp", "sub", "seq")

f32 = jnp.float32
bf16 = jnp.bfloat16


def dot(a, b, ca=1, cb=0):
    return lax.dot_general(a, b, (((ca,), (cb,)), ((), ())), preferred_element_type=f32)


def split2(x):
    high = x.astype(bf16)
    return high, (x - high.astype(f32)).astype(bf16)


def split3(x):
    high = x.astype(bf16)
    rest = x - high.astype(f32)
    mid = rest.astype(bf16)
    return high, mid, (rest - mid.astype(f32)).astype(bf16)


def exact_left(a, b, ca=1, cb=0):
    high, low = split2(b)
    return dot(a, high, ca, cb) + dot(a, low, ca, cb)


def exact_right(a, b, ca=1, cb=0):
    high, low = split2(a)
    return dot(high, b, ca, cb) + dot(low, b, ca, cb)


def both_split(a, b, ca=1, cb=0):
    ah, al = split2(a)
    bh, bl = split2(b)
    return dot(ah, bh, ca, cb) + dot(al, bh, ca, cb) + dot(ah, bl, ca, cb)


def running(mask, x):
    a, b, c = split3(x)
    return dot(mask, a) + dot(mask, b) + dot(mask, c)


def spread(cols):
    lane = lax.broadcasted_iota(jnp.int32, (cols.shape[0], 128), 1)
    halves = [
        jnp.where(lane < HEAD_DIM, cols[:, 2 * i : 2 * i + 1], cols[:, 2 * i + 1 : 2 * i + 2])
        for i in range(HERE // 2)
    ]
    return jnp.concatenate(halves, axis=1)


def head_sum(x):
    row = lax.broadcasted_iota(jnp.int32, (WIDE, 128), 0)
    lane = lax.broadcasted_iota(jnp.int32, (WIDE, 128), 1)
    pick = (row // HEAD_DIM == lane).astype(bf16)
    return exact_right(x, pick)


def sigmoid(x):
    return 1.0 / (1.0 + jnp.exp(-x))


def half_tanh(x):
    return 0.5 * jnp.tanh(0.5 * x) + 0.5


def silu(x):
    return x * half_tanh(x)


def silu_slope(x):
    s = half_tanh(x)
    return s * (1.0 + x * (1.0 - s))


def lower(rows):
    i = lax.broadcasted_iota(jnp.int32, (rows, rows), 0)
    j = lax.broadcasted_iota(jnp.int32, (rows, rows), 1)
    return j <= i


def head_mask(x, h):
    lane = lax.broadcasted_iota(jnp.int32, x.shape, 1)
    return jnp.where(lane // HEAD_DIM == h, x, jnp.zeros_like(x))


def pack_kernel(wi_ref, wo_ref, main_ref, shared_ref, out_ref):
    weight = wi_ref[...].astype(bf16)
    for base in (0, 1):
        for t in range(PLANE):
            lanes = slice(HEAD_DIM * (t % 2), HEAD_DIM * (t % 2 + 1))
            for half in range(HERE // 2):
                tiles = []
                for i in (2 * half, 2 * half + 1):
                    at = base * INNER + i * PLANE * HEAD_DIM + t // 2 * 128
                    tiles.append(weight[:, at : at + 128][:, lanes])
                at = base * WIDE + 128 * half
                main_ref[t, :, at : at + 128] = jnp.concatenate(tiles, axis=1)
    shared_ref[...] = jnp.zeros_like(shared_ref)
    shared_ref[:, : STATES + HEADS] = weight[:, 2 * INNER :]
    out_ref[...] = wo_ref[...].astype(bf16)


def prepare(
    group, place, conv_ref, head_ref, gain_ref,
    conv_out, bias_out, rate_out, skip_out, gain_out, pick_out, before_out, behind_out,
):
    pair = jnp.where(place >= 2, 1, 0) + jnp.where(place >= 4, 1, 0) + jnp.where(place >= 6, 1, 0)
    odd = place - 2 * pair == 1

    def half(x):
        return jnp.where(odd, x[:, HEAD_DIM:], x[:, :HEAD_DIM])

    def four(get):
        halves = [half(get(i)) for i in range(HERE)]
        return [jnp.concatenate(halves[2 * i : 2 * i + 2], axis=1) for i in range(HERE // 2)]

    conv_out[...] = jnp.zeros_like(conv_out)
    columns = lambda i: conv_ref[:, pl.ds(pl.multiple_of(i * PLANE * HEAD_DIM + pair * 128, 128), 128)]
    for i, tile in enumerate(four(columns)):
        conv_out[0 : CONV + 1, 128 * i : 128 * (i + 1)] = tile
    conv_out[0 : CONV + 1, WIDE:] = conv_ref[:, INNER:]
    for i, tile in enumerate(four(lambda i: gain_ref[pl.ds(i * PLANE // 2 + pair, 1), :])):
        gain_out[:, 128 * i : 128 * (i + 1)] = tile
    head = lax.broadcasted_iota(jnp.int32, (3, HEADS), 1)
    lane = lax.broadcasted_iota(jnp.int32, (3, 128), 1)
    mine = jnp.zeros((3, 128), f32)
    for i in range(HERE):
        one = jnp.sum(jnp.where(head == PLANE * i + place, head_ref[...], 0.0), axis=1, keepdims=True)
        mine = mine + jnp.where(lane == i, one, 0.0)
    bias_out[...] = mine[0:1]
    rate_out[...] = jnp.where(lane[0:1] < HERE, -jnp.exp(mine[1:2]), 0.0)
    skip_out[...] = spread(jnp.broadcast_to(mine[2:3], (8, 128)))[0:1]
    row = lax.broadcasted_iota(jnp.int32, (128, 128), 0)
    column = lax.broadcasted_iota(jnp.int32, (128, 128), 1)
    pick_out[...] = jnp.where((row == PLANE * column + place) & (row < HEADS), 1.0, 0.0).astype(bf16)
    rank = lax.broadcasted_iota(jnp.int32, before_out.shape, 0)
    before_out[...] = (rank < group).astype(f32)
    behind_out[...] = (rank > group).astype(f32)


def flags_of(z, docs, flags, doc_rows):
    lines = PLANE * SPAN // 128
    lane = lax.broadcasted_iota(jnp.int32, (1, 128), 1)
    total = docs.shape[0]
    first = z * lines

    def line(i):
        at = first + i
        inside = jnp.clip(at, 0, total - 1)
        got = docs[pl.ds(inside, 1), :].astype(f32)
        return jnp.where(at < 0, -1.0, jnp.where(at >= total, -2.0, got))

    rows = [line(i) for i in range(-1, lines + 1)]
    for i in range(lines + 1):
        now, last = rows[i + 1], rows[i]
        same = []
        for k in range(1, CONV):
            moved = jnp.where(lane < k, pltpu.roll(last, k, 1), pltpu.roll(now, k, 1))
            same.append((moved == now).astype(f32))
        span = min(i, lines - 1) // 2
        rise = (now == rows[2 * span][:, 127:128]).astype(f32)
        tail = (now == rows[2 * span + 2][:, 127:128]).astype(f32)
        both = jnp.concatenate([*same, rise, tail, now, now * 0.0, now * 0.0], axis=0).T
        if i < lines:
            flags[128 * i : 128 * (i + 1), :] = both
            doc_rows[i // 2, :, 128 * (i % 2) : 128 * (i % 2 + 1)] = now
        else:
            flags[128 * i : 128 * i + 8, :] = both[0:8, :]


def prep_kernel(at_ref, *refs):
    prepare(at_ref[0], at_ref[1], *refs)


def normalize(rows, gain):
    vals = rows.astype(f32)
    inv = lax.rsqrt(jnp.mean(vals * vals, axis=1, keepdims=True) + EPS_NORM)
    return (vals * inv * gain).astype(bf16)


def first_begin(halo_ref, ng_ref, wm_ref, ws_ref, edge_ref, ext, state, decay):
    before = normalize(halo_ref[...], ng_ref[...])
    inner = dot(before, wm_ref[:, WIDE : 2 * WIDE]).astype(bf16).astype(f32)
    shared = dot(before, ws_ref[:, :STATES]).astype(bf16).astype(f32)
    rows = jnp.concatenate([inner, shared], axis=1)[8:16]
    ext[SPAN : SPAN + 8, :] = rows
    edge_ref[...] = rows
    state[...] = jnp.zeros_like(state)
    decay[...] = jnp.ones_like(decay)


def first_phase(
    span, x_ref, halo_ref, ng_ref, wm_ref, ws_ref, pick_ref, conv_ref, bias_ref, rate_ref, fl_ref,
    normed_ref, gate_ref, chan_ref, pre_ref, act_ref, dt_ref, cum_ref, held_ref, pref_ref, edge_ref,
    ext, state, decay, end_ref, act_all, dt_all, cum_all,
):
    ext[0:8, :] = ext[SPAN : SPAN + 8, :]
    normed = normalize(x_ref[...], ng_ref[...])
    normed_ref[...] = normed
    main = dot(normed, wm_ref[...]).astype(bf16)
    shared = dot(normed, ws_ref[...]).astype(bf16)
    gate_ref[...] = main[:, :WIDE]
    chan = jnp.concatenate([main[:, WIDE:], shared[:, :STATES]], axis=1)
    chan_ref[...] = chan
    ext[8 : SPAN + 8, :] = chan.astype(f32)
    flags = fl_ref[...]
    pre = conv_ref[4:5, :] + ext[8 : SPAN + 8, :] * conv_ref[0:1, :]
    for k in range(1, CONV):
        moved = ext[8 - k : SPAN + 8 - k, :] * conv_ref[k : k + 1, :]
        pre = pre + jnp.where(flags[:, k - 1 : k] > 0.5, moved, 0.0)
    pre_ref[...] = pre
    act = silu(pre).astype(bf16)
    act_ref[...] = act
    act_all[span] = act
    step = dot(shared[:, STATES:], pick_ref[...]) + bias_ref[...]
    dt = jnp.maximum(step, 0.0) + jnp.log1p(jnp.exp(-jnp.abs(step)))
    lane = lax.broadcasted_iota(jnp.int32, dt.shape, 1)
    both = jnp.where(lane < HEAD_DIM, dt, pltpu.roll(sigmoid(step), HEAD_DIM, 1))
    dt_ref[...] = both
    dt_all[span] = both
    cum = running(lower(SPAN).astype(bf16), dt * rate_ref[...])
    cum_ref[...] = cum
    cum_all[span] = cum
    last = cum[SPAN - 1 : SPAN, :]
    ending = jnp.where(flags[:, 4:5] > 0.5, jnp.exp(last - cum), 0.0)
    inner = act[:, :WIDE]
    write = act[:, WIDE : WIDE + NSTATE]
    added = exact_left(write, spread(ending * dt) * inner.astype(f32), 0, 0)
    held = state[...]
    held_ref[0] = held
    pref_ref[0] = decay[...]
    closing = jnp.where(flags[SPAN - 1 : SPAN, 3:4] > 0.5, jnp.exp(last), 0.0)
    fade = spread(jnp.broadcast_to(closing, (8, 128)))
    held = fade[0:1, :] * held + added
    state[...] = held
    decay[...] = decay[...] * fade
    end_ref[0:NSTATE, :] = held
    end_ref[NSTATE:, :] = decay[...]


def carry_chain(ends_ref, ahead_ref, out_ref, reverse):
    out_ref[...] = jnp.zeros_like(out_ref)
    groups = ends_ref.shape[0]

    @pl.loop(0, groups)
    def _(step):
        g = groups - 1 - step if reverse else step
        one = ends_ref[g]
        on = ahead_ref[g] > 0.5
        held = out_ref[...]
        out_ref[...] = jnp.where(on, one[NSTATE : NSTATE + 1, :] * held + one[0:NSTATE, :], held)


def within_phase(span, fl_ref, row_ref, skip_ref, y_ref, act_all, dt_all, cum_all):
    act = act_all[span]
    inner = act[:, :WIDE]
    cum = cum_all[span]
    cum_t = cum.T
    dt_t = dt_all[span].T
    scores = dot(act[:, WIDE + NSTATE :], act[:, WIDE : WIDE + NSTATE], 1, 1)
    matched = (fl_ref[:, 5:6] == row_ref[0]) & lower(SPAN)
    y = skip_ref[...] * inner.astype(f32)
    for h in range(HERE):
        fade = jnp.exp(jnp.minimum(cum[:, h : h + 1] - cum_t[h : h + 1, :], 0.0))
        mixing = jnp.where(matched, fade, 0.0) * scores * dt_t[h : h + 1, :]
        y = y + exact_right(mixing, head_mask(inner, h))
    y_ref[...] = y


def second_kernel(
    read_ref, cum_ref, fl_ref, held_ref, pref_ref, inc_ref, part_ref, gate_ref, cot_ref, wo_ref, og_ref,
    y_ref, gno_ref, sums_ref,
):
    entering = held_ref[0] + pref_ref[0][0:1, :] * inc_ref[...]
    rising = jnp.where(fl_ref[:, 3:4] > 0.5, jnp.exp(cum_ref[...]), 0.0)
    y_low = (part_ref[...] + spread(rising) * exact_left(read_ref[...], entering)).astype(bf16)
    y_ref[...] = y_low
    gated = y_low.astype(f32) * silu(gate_ref[...].astype(f32))
    gno = dot(cot_ref[...], wo_ref[...], 1, 1)
    gno_ref[...] = gno
    squares = jnp.sum(gated * gated, axis=1, keepdims=True)
    along = jnp.sum(gno * og_ref[...] * gated, axis=1, keepdims=True)
    lane = lax.broadcasted_iota(jnp.int32, (SPAN, 128), 1)
    both = jnp.where(lane == 0, squares, jnp.where(lane == 1, along, 0.0))
    sums_ref[0] = both.T[0:2, :]


def third_begin(gog_ref, gskip_ref, gout_ref, ggw_ref, state, decay):
    for ref in (gog_ref, gskip_ref, gout_ref, ggw_ref, state):
        ref[...] = jnp.zeros_like(ref)
    decay[...] = jnp.ones_like(decay)


def third_first(
    at, y_ref, gate_ref, gno_ref, sums_ref, act_ref, cum_ref, fl_ref, og_ref,
    gy_ref, gg_ref, behind_ref, suff_ref, start_ref, gog_ref, gskip_ref,
    state, decay, no_all, gg_all,
):
    span = no_all.shape[0] - 1 - at
    act = act_ref[...]
    inner = act[:, :WIDE].astype(f32)
    read = act[:, WIDE + NSTATE :]
    flags = fl_ref[...]
    totals = jnp.sum(sums_ref[...], axis=0)
    inv_row = lax.rsqrt(totals[0:1, :] / INNER + EPS_NORM)
    mean_row = inv_row * totals[1:2, :] / INNER
    cols = jnp.concatenate([inv_row, mean_row, jnp.zeros((6, SPAN), f32)], axis=0).T
    inv = cols[:, 0:1]
    mean = cols[:, 1:2]
    y = y_ref[...].astype(f32)
    gate = gate_ref[...].astype(f32)
    gate_act = silu(gate)
    unit = y * gate_act * inv
    gno = gno_ref[...]
    no_all[span] = (unit * og_ref[...]).astype(bf16)
    grad_gated = inv * (gno * og_ref[...] - unit * mean)
    gy = (grad_gated * gate_act).astype(bf16)
    gy_ref[...] = gy
    ggate = (grad_gated * y * silu_slope(gate)).astype(bf16)
    gg_ref[...] = ggate
    gg_all[span] = ggate
    gyf = gy.astype(f32)
    gog_ref[...] += jnp.sum(gno * unit, axis=0, keepdims=True)
    gskip_ref[...] += jnp.sum(inner * gyf, axis=0, keepdims=True)
    rising = jnp.where(flags[:, 3:4] > 0.5, jnp.exp(cum_ref[...]), 0.0)
    wide = spread(rising)
    pulled = exact_left(read, wide * gyf, 0, 0)
    held = state[...]
    behind_ref[0] = held
    suff_ref[0] = decay[...]
    fade = wide[SPAN - 1 : SPAN, :]
    held = fade * held + pulled
    state[...] = held
    decay[...] = decay[...] * fade
    start_ref[0:NSTATE, :] = held
    start_ref[NSTATE:, :] = decay[...]


def third_second(span, place, cot_ref, wo_ref, normed_ref, mix_ref, gout_ref, ggw_ref, no_all, gg_all):
    mix_ref[...] = dot(no_all[place], wo_ref[...])
    gout_ref[...] += dot(no_all[span], cot_ref[...], 0, 0)
    ggw_ref[...] += dot(gg_all[span], normed_ref[...], 0, 0)


def fourth_kernel(
    at, act_ref, dt_ref, cum_ref, fl_ref, row_ref, held_ref, pref_ref, inc_ref, behind_ref, suff_ref,
    ends_ref, ahead_ref, gy_ref, pre_ref, skip_ref, rate_ref,
    gpre_ref, gst_ref, gstep_ref, hsum_ref,
    out_ref,
):
    @pl.when(at == 0)
    def _():
        hsum_ref[...] = jnp.zeros_like(hsum_ref)
        carry_chain(ends_ref, ahead_ref, out_ref, True)

    act = act_ref[...]
    inner = act[:, :WIDE]
    innerf = inner.astype(f32)
    write = act[:, WIDE : WIDE + NSTATE]
    read = act[:, WIDE + NSTATE :]
    flags = fl_ref[...]
    cum = cum_ref[...]
    dt = dt_ref[...]
    gy = gy_ref[...]
    gyf = gy.astype(f32)
    cum_t = cum.T
    entering = held_ref[0] + pref_ref[0][0:1, :] * inc_ref[...]
    leaving = behind_ref[0] + suff_ref[0][0:1, :] * out_ref[...]
    last = cum[SPAN - 1 : SPAN, :]
    rising = jnp.where(flags[:, 3:4] > 0.5, jnp.exp(cum), 0.0)
    ending = jnp.where(flags[:, 4:5] > 0.5, jnp.exp(last - cum), 0.0)
    scores = dot(write, read, 1, 1)
    i = lax.broadcasted_iota(jnp.int32, (SPAN, SPAN), 0)
    j = lax.broadcasted_iota(jnp.int32, (SPAN, SPAN), 1)
    matched = (flags[:, 5:6] == row_ref[0]) & (i <= j)
    lane = lax.broadcasted_iota(jnp.int32, (SPAN, 128), 1)
    from_state = exact_left(write, leaving)
    grad_scaled = spread(ending) * from_state
    grad_scores = jnp.zeros((SPAN, SPAN), f32)
    rows_of = []
    cols_of = jnp.zeros((SPAN, 128), f32)
    for h in range(HERE):
        fade = jnp.exp(jnp.minimum(cum_t[h : h + 1, :] - cum[:, h : h + 1], 0.0))
        weights = jnp.where(matched, fade, 0.0)
        grad_scaled = grad_scaled + exact_right(weights * scores, head_mask(gy, h))
        part = dot(head_mask(inner, h), gy, 1, 1) * weights * dt[:, h : h + 1]
        grad_scores = grad_scores + part
        logs = part * scores
        rows_of.append(jnp.sum(logs, axis=0, keepdims=True))
        cols_of = cols_of + jnp.where(lane == h, jnp.sum(logs, axis=1, keepdims=True), 0.0)
    rows_of.append(jnp.zeros((128 - HERE, SPAN), f32))
    grad_cum = jnp.concatenate(rows_of, axis=0).T - cols_of
    high, low = split2(grad_scores)
    grad_write = dot(high, read) + dot(low, read)
    grad_read = dot(high, write, 0, 0) + dot(low, write, 0, 0)
    read_state = exact_left(read, entering)
    grad_read = grad_read + both_split(spread(rising) * gyf, entering, 1, 1)
    grad_write = grad_write + both_split(spread(ending * dt) * innerf, leaving, 1, 1)
    tail = head_sum(innerf * from_state) * dt * ending
    grad_cum = grad_cum + head_sum(gyf * read_state) * rising - tail
    crossing = jnp.sum(entering * leaving, axis=0, keepdims=True)
    crossing = head_sum(jnp.broadcast_to(crossing, (8, WIDE)))[0:1, :] * rising[SPAN - 1 : SPAN, :]
    end_term = jnp.sum(tail, axis=0, keepdims=True) + crossing
    row = lax.broadcasted_iota(jnp.int32, (SPAN, 128), 0)
    grad_cum = grad_cum + jnp.where(row == SPAN - 1, end_term, 0.0)
    grad_log = running((i <= j).astype(bf16), grad_cum)
    grad_steps = grad_log * rate_ref[...] + head_sum(innerf * grad_scaled)
    grad_step_raw = jnp.where(lane < HERE, grad_steps * pltpu.roll(dt, HEAD_DIM, 1), 0.0)
    gstep_ref[...] = grad_step_raw.T[0:8, :]
    grad_rate = jnp.where(lane < HERE, grad_log * dt, 0.0)
    hsum_ref[0:1, :] += jnp.sum(grad_step_raw, axis=0, keepdims=True)
    hsum_ref[1:2, :] += jnp.sum(grad_rate, axis=0, keepdims=True)
    grad_inner = spread(dt) * grad_scaled + skip_ref[...] * gyf
    slope = silu_slope(pre_ref[...])
    gpre_ref[...] = grad_inner * slope[:, :WIDE]
    gst_ref[...] = jnp.concatenate([grad_write, grad_read], axis=1) * slope[:, WIDE:]


def conv_back(gpre, flags, chan_ext, conv_ref, masked):
    rows = gpre.shape[0] - 8
    total = gpre[0:rows, :] * conv_ref[0:1, :]
    sums = [jnp.sum(gpre[0:rows, :] * chan_ext[8 : rows + 8, :], axis=0, keepdims=True)]
    for k in range(1, CONV):
        masked[...] = jnp.where(flags[:, k - 1 : k] > 0.5, gpre, 0.0)
        total = total + masked[k : rows + k, :] * conv_ref[k : k + 1, :]
        sums.append(jnp.sum(masked[0:rows, :] * chan_ext[8 - k : rows + 8 - k, :], axis=0, keepdims=True))
    sums.append(jnp.sum(gpre[0:rows, :], axis=0, keepdims=True))
    sums.append(jnp.zeros((3, gpre.shape[1]), f32))
    return total, jnp.concatenate(sums, axis=0)


def fifth_begin(gstate_ref, gog_ref, gskip_ref, hsum_ref, giw_ref, small_ref):
    giw_ref[...] = jnp.zeros_like(giw_ref)
    small_ref[...] = jnp.zeros_like(small_ref)
    small_ref[8:16, :] = gstate_ref[...]
    small_ref[16:17, :] = gog_ref[...]
    small_ref[17:18, :] = gskip_ref[...]
    small_ref[18:19, 0:128] = hsum_ref[0:1, :]
    small_ref[18:19, 128:256] = hsum_ref[1:2, :]


def fifth_product(gg_ref, ginner, wm_ref):
    return dot(gg_ref[...], wm_ref[:, :WIDE], 1, 1) + dot(ginner, wm_ref[:, WIDE:], 1, 1)


def fifth_kernel(
    span, spans, gpre_ref, after_ref, fl_ref, chan_ref, edge_ref, conv_ref, normed_ref,
    ginner_ref, giw_ref, small_ref,
    chan_ext, gext, masked,
):
    start = pl.multiple_of(span * SPAN, SPAN)

    @pl.when(span == 0)
    def _():
        chan_ext[0:8, :] = edge_ref[:, :WIDE]

    @pl.when(span > 0)
    def _():
        chan_ext[0:8, :] = chan_ref[pl.ds(pl.multiple_of(start - 16, 16), 16), :WIDE].astype(f32)[8:16, :]

    chan_ext[8 : SPAN + 8, :] = chan_ref[pl.ds(start, SPAN), :WIDE].astype(f32)
    gext[0:SPAN, :] = gpre_ref[pl.ds(start, SPAN), :]

    @pl.when(span < spans - 1)
    def _():
        gext[SPAN : SPAN + 8, :] = gpre_ref[pl.ds(pl.multiple_of(start + SPAN, SPAN), 8), :]

    @pl.when(span == spans - 1)
    def _():
        gext[SPAN : SPAN + 8, :] = after_ref[...]

    total, sums = conv_back(gext[...], fl_ref[pl.ds(start, SPAN + 8), :], chan_ext, conv_ref, masked)
    ginner = total.astype(bf16)
    small_ref[0:8, :] += sums
    ginner_ref[...] = ginner
    giw_ref[...] += dot(ginner, normed_ref[...], 0, 0)


def sixth_kernel(count, *refs):
    sixth_body(refs[:count], *refs[count:])


def sixth_body(
    parts, tails_ref, steps_ref, fl_ref, chan_ref, edge_ref, conv_ref, x_ref, ng_ref,
    gs_ref, gconv_ref, gw_ref,
    gext, chan_ext, masked,
):
    place = lax.axis_index("sub") * lax.axis_size("seq") + lax.axis_index("seq")
    start = pl.multiple_of(place * SPAN, SPAN)
    total = jnp.sum(parts[0][...].astype(f32), axis=0)
    for part in parts[1:]:
        total = total + part[...]
    gext[0:SPAN, :] = total
    gext[SPAN : SPAN + 8, :] = jnp.sum(tails_ref[...], axis=0)
    chan_ext[8 : SPAN + 8, :] = chan_ref[pl.ds(start, SPAN), WIDE:].astype(f32)

    @pl.when(place == 0)
    def _():
        chan_ext[0:8, :] = edge_ref[:, WIDE:]

    @pl.when(place > 0)
    def _():
        chan_ext[0:8, :] = chan_ref[pl.ds(pl.multiple_of(start - 16, 16), 16), WIDE:].astype(f32)[8:16, :]

    conv = conv_ref.at[:, WIDE:]
    total, sums = conv_back(gext[...], fl_ref[pl.ds(start, SPAN + 8), :], chan_ext, conv, masked)
    gconv_ref[...] = sums
    steps = jnp.concatenate([steps_ref[:, i, :] for i in range(HERE)] + [jnp.zeros((128 - HEADS, SPAN), f32)], axis=0)
    grads = jnp.concatenate([total, steps.T], axis=1).astype(bf16)
    gs_ref[...] = grads
    vals = x_ref[...].astype(f32)
    inv = lax.rsqrt(jnp.mean(vals * vals, axis=1, keepdims=True) + EPS_NORM)
    gw_ref[...] = dot((vals * inv * ng_ref[...]).astype(bf16), grads, 0, 0)


def seventh_kernel(skip, count, many, *refs):
    refs = refs[skip:]
    parts, mixes, rest = refs[:count], refs[count : count + many], refs[count + many :]
    gs_ref, ws_ref, x_ref, cot_ref, ng_ref, mixed_ref, gt_ref, gain_ref = rest

    def add_all(total, refs):
        halves = [ref[...] for ref in refs if ref.shape[0] == SPAN // 2]
        if halves:
            total = total + jnp.concatenate(halves, axis=0).astype(f32)
        for ref in refs:
            if ref.shape[0] == SPAN // 2:
                continue
            if len(ref.shape) == 2:
                total = total + ref[...].astype(f32)
            else:
                for i in range(ref.shape[0]):
                    total = total + ref[i].astype(f32)
        return total

    vals = x_ref[...].astype(f32)
    mixed_ref[...] = add_all(vals, mixes).astype(bf16)
    grad = add_all(dot(gs_ref[...], ws_ref[...], 1, 1), parts)
    inv = lax.rsqrt(jnp.mean(vals * vals, axis=1, keepdims=True) + EPS_NORM)
    unit = vals * inv
    s = grad * ng_ref[...]
    gt_ref[...] = cot_ref[...].astype(f32) + inv * (s - unit * jnp.mean(s * unit, axis=1, keepdims=True))
    row = jnp.sum(grad * unit, axis=0, keepdims=True)
    for i in range(D // 128):
        gain_ref[i : i + 1, :] = row[:, 128 * i : 128 * (i + 1)]


def adam_terms(weight, grad, first, second):
    first_new = BETA_ONE * first + (1.0 - BETA_ONE) * grad
    second_new = BETA_TWO * second + (1.0 - BETA_TWO) * grad * grad
    update = (
        first_new / (1.0 - BETA_ONE**STEP) / (jnp.sqrt(second_new / (1.0 - BETA_TWO**STEP)) + ADAM_EPS)
        + DECAY * weight
    )
    return (first_new, second_new, update)


def square_sum(x):
    return jnp.sum(jnp.sum(x * x, axis=1, keepdims=True), axis=0, keepdims=True)


def lamb_apply(weight, update, weight_sq, update_sq):
    return weight - RATE * (jnp.sqrt(weight_sq) / (jnp.sqrt(update_sq) + ADAM_EPS)) * update


def two_heads(ref, rows, i, pair):
    cols = slice(HEAD_DIM * i, HEAD_DIM * (i + 1))
    return jnp.concatenate([ref[2 * pair, rows, cols], ref[2 * pair + 1, rows, cols]], axis=1)


def from_planes(z, own, near, far):
    first = jnp.where(z > 0, near[0], far[0].astype(f32))
    third = jnp.where(z < 3, near[1], far[2].astype(f32))
    return own + first + far[1].astype(f32) + third


def adam_kernel(count, gate_ref, inner_ref, shared_ref, gain_ref, wi_ref, mi_ref, vi_ref, wo_ref, mo_ref, vo_ref, *refs):
    outs, (mi_out, vi_out, ui_out, mo_out, vo_out, uo_out, sums_ref, grad) = refs[:count], refs[count:]
    for base, ref in ((0, gate_ref), (INNER, inner_ref)):
        for i in range(HERE):
            for pair in range(PLANE // 2):
                at = base + i * PLANE * HEAD_DIM + pair * 128
                grad[:, at : at + 128] = two_heads(ref, slice(None), i, pair)
    grad[:, 2 * INNER :] = jnp.sum(shared_ref[...], axis=0)[:, : STATES + HEADS]
    weight = wi_ref[...]
    mi_out[...], vi_out[...], update = adam_terms(weight, grad[...], mi_ref[...], vi_ref[...])
    ui_out[...] = update
    sums_ref[0:8, :] = gain_ref[...]
    sums_ref[8:16, :] = jnp.zeros((8, 128), f32)
    sums_ref[8:9, :] = jnp.broadcast_to(square_sum(weight), (1, 128))
    sums_ref[9:10, :] = jnp.broadcast_to(square_sum(update), (1, 128))
    if count > 1:
        z = lax.axis_index("grp")
        total = from_planes(z, outs[0][pl.ds(pl.multiple_of(z * HEAD_DIM, HEAD_DIM), HEAD_DIM), :], *outs[1:])
    else:
        total = outs[0][...]
    weight = wo_ref[...]
    mo_out[...], vo_out[...], update = adam_terms(weight, total, mo_ref[...], vo_ref[...])
    uo_out[...] = update
    sums_ref[10:11, :] = jnp.broadcast_to(square_sum(weight), (1, 128))
    sums_ref[11:12, :] = jnp.broadcast_to(square_sum(update), (1, 128))


def last_kernel(
    every_ref, small_ref, wi_ref, ui_ref, wo_ref, uo_ref,
    nw_ref, nm_ref, nv_ref, cw_ref, cm_ref, cv_ref, hw_ref, hm_ref, hv_ref, gw_ref, gm_ref, gv_ref,
    wi_out, wo_out, nm_out, nv_out, nw_out, cm_out, cv_out, cw_out, hm_out, hv_out, hw_out, gm_out, gv_out, gw_out,
    conv, gain,
):
    total = jnp.sum(every_ref[...], axis=0)
    wi_out[...] = lamb_apply(wi_ref[...], ui_ref[...], total[8:9, 0:1], total[9:10, 0:1])
    wo_out[...] = lamb_apply(wo_ref[...], uo_ref[...], total[10:11, 0:1], total[11:12, 0:1])

    def update(grad, weight_ref, first_ref, second_ref, first_out, second_out, weight_out):
        weight = weight_ref[...]
        first, second, step = adam_terms(weight, grad, first_ref[...], second_ref[...])
        first_out[...] = first
        second_out[...] = second
        weight_out[...] = lamb_apply(weight, step, square_sum(weight), square_sum(step))

    update(total[0:8], nw_ref, nm_ref, nv_ref, nm_out, nv_out, nw_out)
    for i in range(HERE):
        for pair in range(PLANE // 2):
            at = i * PLANE * HEAD_DIM + pair * 128
            conv[:, at : at + 128] = two_heads(small_ref, slice(0, 8), i, pair)
            gain[at // 128 : at // 128 + 1, :] = two_heads(small_ref, slice(16, 17), i, pair)
    conv[:, INNER:] = jnp.sum(small_ref[:, 8:16, :], axis=0)
    update(conv[0:5, :], cw_ref, cm_ref, cv_ref, cm_out, cv_out, cw_out)
    update(gain[...], gw_ref, gm_ref, gv_ref, gm_out, gv_out, gw_out)

    t = lax.broadcasted_iota(jnp.int32, (PLANE, 128), 0)
    lane = lax.broadcasted_iota(jnp.int32, (PLANE, 128), 1)

    def by_head(cols):
        row = jnp.zeros((PLANE, 128), f32)
        for i in range(HERE):
            row = row + jnp.where(lane == PLANE * i + t, cols[:, i : i + 1], 0.0)
        return jnp.sum(row, axis=0, keepdims=True)[:, :HEADS]

    steps = by_head(small_ref[:, 18, 0:128])
    rates = by_head(small_ref[:, 18, 128:256]) * -jnp.exp(hw_ref[1:2, :])
    skips = by_head(head_sum(small_ref[:, 17, :]))
    update(jnp.concatenate([steps, rates, skips], axis=0), hw_ref, hm_ref, hv_ref, hm_out, hv_out, hw_out)


def spec(block, index):
    return pl.BlockSpec(block, index)


def whole(*dims):
    return pl.BlockSpec(dims, lambda *_: (0,) * len(dims))


def shape(*dims, dtype=f32):
    return jax.ShapeDtypeStruct(dims, dtype)


ANY = pl.BlockSpec(memory_space=pl.ANY)
IN_VMEM = pl.BlockSpec(memory_space=pltpu.VMEM)
IN_HBM = pl.BlockSpec(memory_space=pltpu.HBM)
MIB = 1024 * 1024
VMEM_LIMIT = 60 * MIB
SMALL_LIMIT = 13 * MIB


def launch(kernel, name, steps, in_specs, ins, out_specs, outs, scratch=()):
    grid = {"grid": (steps,), "in_specs": list(in_specs), "out_specs": list(out_specs)} if steps else {}
    return pl.pallas_call(
        kernel,
        out_shape=list(outs),
        scratch_shapes=list(scratch),
        compiler_params=pltpu.CompilerParams(vmem_limit_bytes=VMEM_LIMIT),
        name=name,
        **grid,
    )(*ins)


class First:
    def __init__(self, spans, x, halo, gain, wm, ws, pick, conv, bias, rate, flags, doc_rows, skip, ahead):
        rows = spans * SPAN
        early = lambda s: jnp.minimum(s, spans - 1)
        late = lambda s: jnp.maximum(s - spans, 0)
        both = lambda s: jnp.where(s >= spans, s - spans, s)
        block = lambda cols, at=early: spec((SPAN, cols), lambda s: (at(s), 0))
        span3 = lambda a, b, at=early: spec((1, a, b), lambda s: (at(s), 0, 0))
        self.ins = [x, halo, gain, wm, ws, pick, conv, bias, rate, flags, doc_rows, skip, ahead]
        self.in_specs = [
            block(D), whole(16, D), whole(1, D), whole(D, MAIN), whole(D, SHARED), whole(128, 128), whole(8, LOCAL),
            whole(1, 128), whole(1, 128), block(8, both), span3(1, SPAN, late), whole(1, WIDE), whole(*ahead.shape),
        ]
        self.out_specs = [
            block(D), block(WIDE), block(LOCAL), block(LOCAL), block(LOCAL), block(128), block(128),
            span3(NSTATE, WIDE), span3(8, WIDE), whole(8, LOCAL), block(WIDE, late),
        ]
        self.outs = [
            shape(rows, D, dtype=bf16), shape(rows, WIDE, dtype=bf16), shape(rows, LOCAL, dtype=bf16), shape(rows, LOCAL),
            shape(rows, LOCAL, dtype=bf16), shape(rows, 128), shape(rows, 128),
            shape(spans, NSTATE, WIDE), shape(spans, 8, WIDE), shape(8, LOCAL), shape(rows, WIDE),
        ]
        self.scratch = [
            pltpu.VMEM((SPAN + 8, LOCAL), f32), pltpu.VMEM((NSTATE, WIDE), f32), pltpu.VMEM((8, WIDE), f32),
            pltpu.VMEM((PACK, WIDE), f32), pltpu.VMEM((spans, SPAN, LOCAL), bf16), pltpu.VMEM((spans, SPAN, 128), f32),
            pltpu.VMEM((spans, SPAN, 128), f32),
        ]


def first_steps(step, spans, ins, outs, scratch):
    @pl.when(step == 0)
    def _():
        first_begin(*ins[1:5], outs[9], *scratch[:3])

    @pl.when(step < spans)
    def _():
        first_phase(step, *ins[:10], *outs[:10], *scratch)

    @pl.when(step >= spans)
    def _():
        within_phase(step - spans, *ins[9:12], outs[10], *scratch[4:])


def first_plain(spans, *refs):
    ins, outs, end, scratch = refs[:13], refs[13:24], refs[24], refs[25:]
    step = pl.program_id(0)
    first_steps(step, spans, ins, outs, scratch)

    @pl.when(step == spans - 1)
    def _():
        end[...] = scratch[3][...]


class Second:
    def __init__(self, spans, act, cum, flags, held, pref, incoming, part, gate, cot, wo, gain):
        rows = spans * SPAN
        block = lambda cols: spec((SPAN, cols), lambda s: (s, 0))
        span3 = lambda a, b: spec((1, a, b), lambda s: (s, 0, 0))
        self.ins = [act, cum, flags, held, pref, incoming, part, gate, cot, wo, gain]
        self.in_specs = [
            spec((SPAN, NSTATE), lambda s: (s, (WIDE + NSTATE) // NSTATE)), block(128), block(8), span3(NSTATE, WIDE),
            span3(8, WIDE), whole(NSTATE, WIDE), block(WIDE), block(WIDE), block(D), whole(WIDE, D), whole(1, WIDE),
        ]
        self.out_specs = [block(WIDE), block(WIDE)]
        self.outs = [shape(rows, WIDE, dtype=bf16), shape(rows, WIDE)]
        self.scratch = []


class Third:
    def __init__(self, spans, y, gate, gno, sums, act, cum, flags, gain, cot, wo, normed):
        rows = spans * SPAN
        back = lambda s: jnp.maximum(spans - 1 - s, 0)
        after = lambda s: jnp.maximum(s - spans, 0)
        block = lambda cols: spec((SPAN, cols), lambda s: (back(s), 0))
        later = lambda cols: spec((SPAN, cols), lambda s: (after(s), 0))
        span3 = lambda a, b: spec((1, a, b), lambda s: (back(s), 0, 0))
        self.later = later
        self.ins = [y, gate, gno, sums, act, cum, flags, gain, cot, wo, normed]
        self.in_specs = [
            block(WIDE), block(WIDE), block(WIDE), spec((PLANE, pl.squeezed, 2, SPAN), lambda s: (0, back(s), 0, 0)),
            block(LOCAL), block(128), block(8), whole(1, WIDE), later(D), whole(WIDE, D), later(D),
        ]
        self.out_specs = [block(WIDE), block(WIDE), span3(NSTATE, WIDE), span3(8, WIDE), whole(1, WIDE), whole(1, WIDE),
                          whole(WIDE, D), whole(WIDE, D)]
        self.outs = [
            shape(rows, WIDE, dtype=bf16), shape(rows, WIDE, dtype=bf16), shape(spans, NSTATE, WIDE),
            shape(spans, 8, WIDE), shape(1, WIDE), shape(1, WIDE), shape(WIDE, D), shape(WIDE, D),
        ]
        keep = pltpu.VMEM((spans, SPAN, WIDE), bf16)
        self.scratch = [pltpu.VMEM((NSTATE, WIDE), f32), pltpu.VMEM((8, WIDE), f32), keep, keep]


def third_plain(spans, *refs):
    ins, (gy, gg, behind, suff, gog, gskip, gout, ggw, start, mix), scratch = refs[:11], refs[11:21], refs[21:]
    step = pl.program_id(0)

    @pl.when(step == 0)
    def _():
        third_begin(gog, gskip, gout, ggw, *scratch[:2])

    @pl.when(step < spans)
    def _():
        third_first(step, *ins[:8], gy, gg, behind, suff, start, gog, gskip, *scratch)

    @pl.when(step >= spans)
    def _():
        third_second(step - spans, step - spans, *ins[8:], mix, gout, ggw, *scratch[2:])


class Fourth:
    def __init__(
        self, spans, act, dt, cum, flags, doc_rows, held, pref, incoming, behind, suff, ends, after_us, gy, pre,
        skip, rate,
    ):
        rows = spans * SPAN
        groups = ends.shape[0]
        block = lambda cols: spec((SPAN, cols), lambda s: (s, 0))
        span3 = lambda a, b: spec((1, a, b), lambda s: (s, 0, 0))
        self.ins = [act, dt, cum, flags, doc_rows, held, pref, incoming, behind, suff, ends, after_us, gy, pre, skip, rate]
        self.in_specs = [
            block(LOCAL), block(128), block(128), block(8), span3(1, SPAN), span3(NSTATE, WIDE),
            span3(8, WIDE), whole(NSTATE, WIDE), span3(NSTATE, WIDE), span3(8, WIDE), whole(groups, PACK, WIDE),
            whole(groups, 1, WIDE), block(WIDE), block(LOCAL), whole(1, WIDE), whole(1, 128),
        ]
        self.out_specs = [block(WIDE), whole(8, 128)]
        self.outs = [shape(rows, WIDE), shape(8, 128)]
        self.scratch = [pltpu.VMEM((NSTATE, WIDE), f32)]


def fourth_plain(*refs):
    ins, (gpre, hsum, gst, gstep), scratch = refs[:16], refs[16:20], refs[20:]
    fourth_kernel(pl.program_id(0), *ins, gpre, gst, gstep, hsum, *scratch)


class Fifth:
    def __init__(self, spans, gpre, after, flags, chan, edge, conv, normed, gstate, gog, gskip, hsum, ggate, wm):
        rows = spans * SPAN
        block = lambda cols: spec((SPAN, cols), lambda s: (s, 0))
        self.ins = [gpre, after, flags, chan, edge, conv, normed, gstate, gog, gskip, hsum, ggate, wm]
        self.in_specs = [
            whole(rows, WIDE), whole(8, WIDE), whole(rows + 8, 8), whole(rows, LOCAL), whole(8, LOCAL), whole(8, WIDE),
            block(D), whole(8, STATES), whole(1, WIDE), whole(1, WIDE), whole(8, 128), block(WIDE), whole(D, MAIN),
        ]
        self.outs = []
        self.scratch = [pltpu.VMEM((SPAN + 8, WIDE), f32)] * 3


def fifth_plain(spans, *refs):
    step = pl.program_id(0)
    ins, (gp, giw, small), (*scratch, ginner) = refs[:13], refs[13:16], refs[16:]

    @pl.when(step == 0)
    def _():
        fifth_begin(*ins[7:11], giw, small)

    fifth_kernel(step, spans, *ins[:7], ginner, giw, small, *scratch)
    gp[...] = fifth_product(ins[11], ginner[...], ins[12])


def run_sixth(parts, tails, steps, flags, chan, edge, conv, x, gain):
    ins = [*parts, tails, steps, flags, chan, edge, conv, x, gain]
    return pl.pallas_call(
        functools.partial(sixth_kernel, len(parts)),
        in_specs=[IN_VMEM] * len(ins),
        out_shape=[shape(SPAN, SHARED, dtype=bf16), shape(8, STATES), shape(D, SHARED)],
        scratch_shapes=[pltpu.VMEM((SPAN + 8, STATES), f32)] * 3,
        compiler_params=pltpu.CompilerParams(vmem_limit_bytes=SMALL_LIMIT),
        name="conv_back_state",
    )(*ins)


def run_seventh(parts, mixes, gs, ws, x, cot, gain, spare):
    ins = [*spare, *parts, *mixes, gs, ws, x, cot, gain]
    return pl.pallas_call(
        functools.partial(seventh_kernel, len(spare), len(parts), len(mixes)),
        in_specs=[IN_VMEM] * len(ins),
        out_shape=[shape(SPAN, D, dtype=bf16), shape(SPAN, D), shape(D // 128, 128)],
        compiler_params=pltpu.CompilerParams(vmem_limit_bytes=SMALL_LIMIT),
        name="token_gradient",
    )(*ins)


def run_adam(gate, inner, shared, gain, wi, mi, vi, wo, mo, vo, grads_out):
    like = lambda a: shape(*a.shape)
    ins = [gate, inner, shared, gain, wi, mi, vi, wo, mo, vo, *grads_out]
    return pl.pallas_call(
        functools.partial(adam_kernel, len(grads_out)),
        in_specs=[IN_VMEM] * len(ins),
        out_shape=[like(wi), like(wi), like(wi), like(wo), like(wo), like(wo), shape(16, 128)],
        scratch_shapes=[pltpu.VMEM(wi.shape, f32)],
        compiler_params=pltpu.CompilerParams(vmem_limit_bytes=SMALL_LIMIT),
        name="adam_terms",
    )(*ins)


def run_prep(groups, at, conv, head, gain):
    return pl.pallas_call(
        prep_kernel,
        in_specs=[pl.BlockSpec(memory_space=pltpu.SMEM)] + [pl.BlockSpec(memory_space=pltpu.VMEM)] * 3,
        out_shape=[shape(8, LOCAL), shape(1, 128), shape(1, 128), shape(1, WIDE), shape(1, WIDE),
                   shape(128, 128, dtype=bf16), shape(groups, 1, WIDE), shape(groups, 1, WIDE)],
        compiler_params=pltpu.CompilerParams(vmem_limit_bytes=VMEM_LIMIT),
        name="prepare",
    )(at, conv, head, gain)


def run_last(every, small, big, params):
    like = lambda a: shape(*a.shape)
    outs = [like(big[0]), like(big[2])]
    for weight in params[::3]:
        outs += [like(weight)] * 3
    return pl.pallas_call(
        last_kernel,
        out_shape=outs,
        scratch_shapes=[pltpu.VMEM((8, INNER + STATES), f32), pltpu.VMEM((INNER // 128, 128), f32)],
        compiler_params=pltpu.CompilerParams(vmem_limit_bytes=SMALL_LIMIT),
        name="lamb_apply",
    )(every, small, *big, *params)


MESH = pl.DeviceIdType.MESH


def bits(place):
    x = jnp.where(place >= 4, 1, 0)
    rest = place - 4 * x
    c = jnp.where(rest >= 2, 1, 0)
    return x, c, rest - 2 * c


class Here:
    def __init__(self):
        self.z = lax.axis_index("grp")
        self.sub = lax.axis_index("sub")
        self.y = lax.axis_index("seq")
        self.x = jnp.where(self.sub >= 2, 1, 0)
        self.c = self.sub - 2 * self.x
        self.t = self.sub * 2 + self.y

    def mate(self, o, up=0):
        x = 1 - self.x if o & 4 else self.x
        c = 1 - self.c if o & 2 else self.c
        y = 1 - self.y if o & 1 else self.y
        sub = x * 2 + c
        return (self.onward(up), sub, y), sub * 2 + y

    def onward(self, up):
        z = self.z + up
        return jnp.where(z >= 4, z - 4, z) if up else self.z

    def plane(self, up):
        return (self.onward(up), self.sub, self.y), self.onward(up)


CHIPS = (5, 4, 1)
CORE = 2


def near(h):
    return [h.mate(o)[0] for o in range(1, 8)]


def same_core(h):
    return [h.mate(o)[0] for o in CHIPS]


def line(h):
    return [h.plane(up)[0] for up in range(1, 4)]


def call(devices):
    barrier = pltpu.get_barrier_semaphore()
    for device in devices:
        pl.semaphore_signal(barrier, inc=1, device_id=device, device_id_type=MESH)
    return barrier


def greet(devices):
    pl.semaphore_wait(call(devices), len(devices))


def rows_at(ref, at, size):
    return ref.at[pl.ds(pl.multiple_of(at * size, size), size)]


class Wires:
    def __init__(self, send, recv, local, started=False):
        self.send_sem, self.recv_sem, self.local_sem = send, recv, local
        self.sent, self.kept, self.started = [], [], started

    def make(self, src, dst, i, device, j=None):
        return pltpu.make_async_remote_copy(
            src_ref=src, dst_ref=dst, send_sem=self.send_sem.at[i], recv_sem=self.recv_sem.at[i if j is None else j],
            device_id=device, device_id_type=MESH,
        )

    def send(self, src, dst, i, device):
        copy = self.make(src, dst, i, device)
        if not self.started:
            copy.start()
        self.sent.append(copy)

    def arrived(self, dst, i, device):
        self.make(dst, dst, i, device).wait_recv()

    def keep(self, src, dst):
        copy = pltpu.make_async_copy(src, dst, self.local_sem.at[len(self.kept)])
        if not self.started:
            copy.start()
        self.kept.append(copy)
        return copy

    def finish(self):
        for copy in self.sent:
            copy.wait_send()


def wires(copies, kept):
    return [pltpu.SemaphoreType.DMA((copies,)), pltpu.SemaphoreType.DMA((copies,)), pltpu.SemaphoreType.DMA((kept,))]


def talk(kernel, number, name, outs, ins, scratch):
    return pl.pallas_call(
        kernel,
        in_specs=[IN_VMEM] * len(ins),
        out_specs=[IN_VMEM] * len(outs),
        out_shape=outs,
        scratch_shapes=scratch,
        compiler_params=pltpu.CompilerParams(collective_id=number, has_side_effects=True, vmem_limit_bytes=SMALL_LIMIT),
        name=name,
    )(*ins)


class Relay:
    def __init__(self, h, w, base, block):
        self.h, self.w, self.base, self.block = h, w, base, block

    def copies(self, hop):
        h = self.h
        above, below = h.plane(1)[0], h.plane(3)[0]
        up = self.w.make, jnp.maximum(h.z - hop + 1, 0), self.base + hop, above
        down = self.w.make, jnp.minimum(h.z + hop - 1, 3), self.base + 4 + hop, below
        yield (h.z < 3) & (h.z >= hop - 1), up, h.z >= hop, jnp.maximum(h.z - hop, 0), below
        yield (h.z > 0) & (h.z <= 4 - hop), down, h.z <= 3 - hop, jnp.minimum(h.z + hop, 3), above

    def first(self):
        for sends, (make, z, i, device), *_ in self.copies(1):

            @pl.when(sends)
            def _():
                make(self.block(z), self.block(z), i, device).start()

    def onward(self, hop):
        for _, (_, _, i, _), comes, z, device in self.copies(hop):

            @pl.when(comes)
            def _():
                self.w.arrived(self.block(z), i, device)

        if hop < 3:
            for sends, (make, z, i, device), *_ in self.copies(hop + 1):

                @pl.when(sends)
                def _():
                    make(self.block(z), self.block(z), i, device).start()

    def finish(self):
        for hop in range(1, 4):
            for sends, (make, z, i, device), *_ in self.copies(hop):

                @pl.when(sends)
                def _():
                    make(self.block(z), self.block(z), i, device).wait_send()


def start_kernel(wi_in, wo_in, tok, docs_in, conv_in, head_in, gain_in, norm_in, *refs):
    (wm, ws, x, halo), outputs, (flags, doc_rows, out_low, norm), refs = refs[:4], refs[4:12], refs[12:16], refs[16:]
    (wi, wo, docs, conv, head, gain, main, shared), sems = refs[:8], refs[8:]
    h = Here()
    w = Wires(*sems)
    near_x, near_y, mate = [h.mate(o)[0] for o in (4, 1, CORE)]
    friends = near(h) + line(h)
    barrier = call(friends)
    loads = [w.keep(wi_in, wi), w.keep(wo_in, wo)]
    loads += [w.keep(*pair) for pair in ((docs_in, docs), (conv_in, conv), (head_in, head), (gain_in, gain), (norm_in, norm))]
    own = w.keep(tok, rows_at(x, h.t, SPAN))
    loads[0].wait()
    loads[1].wait()
    pack_kernel(wi, wo, main, shared, out_low)
    pl.semaphore_wait(barrier, len(friends))

    in_rows = lambda place: wm.at[pl.ds(pl.multiple_of(h.z * SPAN + place * 32, 32), 32)]
    keep = [w.keep(main.at[h.t], in_rows(h.t)), w.keep(shared, ws.at[h.z, h.t])]
    for o in range(1, 8):
        device, place = h.mate(o)
        w.send(main.at[place], in_rows(h.t), o, device)
    for up in range(1, 4):
        w.send(shared, ws.at[h.z, h.t], 10 + up, h.plane(up)[0])
    block = lambda o: rows_at(x, h.mate(o)[1], SPAN)
    w.send(tok, block(0), 21, near_x)
    w.send(tok, block(0), 22, near_y)
    w.send(tok, block(0), 23, mate)
    for copy in loads[2:]:
        copy.wait()
    prepare(h.z, h.t, conv, head, gain, *outputs)
    flags_of(h.z, docs, flags, doc_rows)
    keep[0].wait()
    for o in range(1, 8):
        device, place = h.mate(o)
        w.arrived(in_rows(place), o, device)
    relay = Relay(h, w, 30, lambda z: rows_at(wm, z, SPAN))
    relay.first()
    keep[1].wait()
    for up in range(1, 4):
        device, z = h.plane(4 - up)
        w.arrived(ws.at[z, h.t], 10 + up, device)
    for i, o in enumerate(CHIPS):
        w.send(ws.at[:, h.t], ws.at[:, h.t], 40 + i, h.mate(o)[0])
    w.send(ws.at[:, h.t], ws.at[:, h.t], 43, mate)
    half = SPAN // 2
    upper, lower = pl.ds(0, half), pl.ds(half, half)
    relay.onward(1)
    w.arrived(block(4), 21, near_x)
    w.send(block(4).at[upper], block(4).at[upper], 20, near_y)
    w.send(block(4), block(4), 25, mate)
    w.arrived(block(1), 22, near_y)
    w.send(block(1).at[lower], block(1).at[lower], 27, near_x)
    w.send(block(1), block(1), 26, mate)
    for i, o in enumerate(CHIPS):
        device, place = h.mate(o)
        w.arrived(ws.at[:, place], 40 + i, device)
        w.send(ws.at[:, place], ws.at[:, place], 44 + i, mate)
    relay.onward(2)
    w.arrived(block(5).at[upper], 20, near_y)
    w.arrived(block(5).at[lower], 27, near_x)
    w.send(block(5), block(5), 24, mate)
    own.wait()
    w.arrived(block(CORE), 23, mate)
    w.arrived(ws.at[:, h.mate(CORE)[1]], 43, mate)
    for i, o in enumerate(CHIPS):
        w.arrived(block(o ^ CORE), 24 + i, mate)
    w.send(x.at[pl.ds(PLANE * SPAN - 16, 16)], halo, 50, h.plane(1)[0])
    for i, o in enumerate(CHIPS):
        w.arrived(ws.at[:, h.mate(o ^ CORE)[1]], 44 + i, mate)
    relay.onward(3)
    relay.finish()
    w.arrived(halo, 50, h.plane(3)[0])
    w.finish()


class Chain:
    def __init__(self, h, w, ends, low, lows, reverse):
        self.h, self.w, self.ends, self.low, self.lows = h, w, ends, low, lows
        self.hops = []
        for up in range(1, 4):
            ahead = 4 - up if reverse else up
            goes = h.z >= up if reverse else h.z < 4 - up
            comes = h.z < 4 - up if reverse else h.z >= up
            self.hops.append((up, goes, h.plane(ahead)[0], comes, *h.plane(4 - ahead)))

    def copy(self, up, device):
        z = self.h.z
        if up == 1:
            return self.w.make(self.ends.at[z], self.ends.at[z], up, device)
        return self.w.make(self.low, self.lows.at[z], up, device)

    def start(self):
        self.low[...] = self.ends[self.h.z].astype(bf16)
        for up, goes, device, *_ in self.hops:

            @pl.when(goes)
            def _():
                self.copy(up, device).start()

    def wait(self):
        for up, goes, device, comes, back, z in self.hops:

            @pl.when(comes)
            def _():
                self.w.arrived((self.lows if up > 1 else self.ends).at[z], up, back)
                if up > 1:
                    self.ends[z] = self.lows[z].astype(f32)

            @pl.when(goes)
            def _():
                self.copy(up, device).wait_send()


def first_direct(work, *refs):
    ins, (out, cot), refs = refs[:13], refs[13:15], refs[15:]
    outs, (inc, g, wo), refs = refs[:11], refs[11:14], refs[14:]
    (ext, state, decay, ends, low, lows), sems = refs[:6], refs[6:]
    h = Here()
    w = Wires(*sems)
    local = sems[2]
    mate, _ = h.mate(CORE)
    end = ends.at[h.z]
    spans = PLANE
    rows_of = [Rows(outs[i]) for i in (4, 5, 6)]

    greet(line(h) + same_core(h) + [mate])
    rows = [w.make(out, rows_at(wo, h.z, HEAD_DIM), 8 + up, h.plane(up)[0]) for up in range(1, 4)]
    block = lambda o: rows_at(g, h.mate(o)[1], SPAN)
    across = [w.make(cot, block(0), 4 + i, h.mate(o)[0]) for i, o in enumerate(CHIPS)]
    for copy in (*rows, *across):
        copy.start()
    loads = [pltpu.make_async_copy(cot, block(0), local.at[0]),
             pltpu.make_async_copy(out, rows_at(wo, h.z, HEAD_DIM), local.at[1])]
    for copy in loads:
        copy.start()
    first_begin(*ins[1:5], outs[9], ext, state, decay)

    @pl.loop(0, spans, unroll=2)
    def _(step):
        taken = views(work.in_specs[:10], ins, step)
        given = views(work.out_specs[:10], outs, step)
        first_phase(step, *taken, *given, ext, state, decay, end, *rows_of)

    chain = Chain(h, w, ends, low, lows, False)
    chain.start()
    over = [w.make(block(o), block(o), 12 + i, mate) for i, o in enumerate((*CHIPS, 0))]

    def within(span):
        taken = views(work.in_specs[9:12], ins[9:12], span + spans)
        within_phase(span, *taken, view(work.out_specs[10], outs[10], span + spans), *rows_of)

    pl.loop(0, spans // 2, unroll=2)(within)
    loads[0].wait()
    over[3].start()
    for i, o in enumerate(CHIPS):
        across[i].wait_send()
        w.arrived(block(o), 4 + i, h.mate(o)[0])
        over[i].start()
    pl.loop(spans // 2, spans, unroll=2)(within)
    for i, o in enumerate((*CHIPS, 0)):
        over[i].wait_send()
        w.arrived(block(o ^ CORE), 12 + i, mate)
    for up in range(1, 4):
        rows[up - 1].wait_send()
        w.arrived(rows_at(wo, h.onward(4 - up), HEAD_DIM), 8 + up, h.plane(4 - up)[0])
    loads[1].wait()
    chain.wait()
    carry_chain(ends, ins[12], inc, False)


def turn(step):
    h = Here()
    a, b, e = bits(7 - step)
    x, c, y = h.x + a - 2 * h.x * a, h.c + e - 2 * h.c * e, h.y + b - 2 * h.y * b
    return x * 4 + c * 2 + y


class Fold:
    def __init__(self, h, w, base, blocks, inbox, outbox, total, deliver):
        self.h, self.w, self.base, self.deliver = h, w, base, deliver
        self.blocks, self.inbox, self.outbox, self.total = blocks, inbox, outbox, total
        self.mate, _ = h.mate(CORE)
        self.slots = blocks.shape[0]

    def sent(self, i):
        self.w.make(self.inbox.at[i], self.inbox.at[i], self.base + i, self.mate).wait_send()

    def slot(self, step):
        for i in (2, 3):

            @pl.when(step == 2 * i)
            def _():
                self.sent(i - 2)

        return jnp.where(step >= 4, step - 4, step) if self.slots == 4 else step

    def add(self, pair, put):
        @pl.loop(0, SPAN, step=32)
        def _(row):
            rows = pl.ds(pl.multiple_of(row, 32), 32)
            put(rows, self.blocks[(2 * pair + 1) % self.slots, rows, :] + self.inbox[pair, rows, :])

    def settle(self, i):
        self.w.arrived(self.inbox.at[i], self.base + i, self.mate)
        self.add(i, put_in(self.outbox, i))
        self.deliver(i)

    def step(self, step, early=0):
        for i in range(4):

            @pl.when(step == 2 * i)
            def _():
                self.w.make(self.blocks.at[2 * i % self.slots], self.inbox.at[i], self.base + i, self.mate).start()
                if i > early:
                    self.settle(i - 1)

    def last(self):
        self.w.arrived(self.inbox.at[3], self.base + 3, self.mate)
        self.add(3, put_in(self.total))
        self.sent(2)
        self.sent(3)


class ToChips:
    def __init__(self, h, w, base, outbox, results):
        self.copies = [w.make(outbox.at[i], results.at[i], base + i, h.mate(o)[0]) for i, o in enumerate(CHIPS)]

    def __call__(self, i):
        self.copies[i].start()

    def last(self):
        for copy in self.copies:
            copy.wait()


def head_rows(ref, z):
    return rows_at(ref, z, HEAD_DIM)


def lanes_at(ref, z):
    return ref.at[:, pl.ds(pl.multiple_of(z * SPAN, SPAN), SPAN)]


class Planes:
    def __init__(self, h, w, base, full, low, piece, near, far):
        self.copies = []
        for up in range(1, 4):
            device, z = h.plane(up)
            wide = functools.partial(w.make, piece(full, z), near.at[up // 2], base + up, device)
            slim = functools.partial(w.make, piece(low, z), far.at[up - 1], base + up, device)
            to_near = {1: h.z < 3, 2: None, 3: h.z > 0}[up]
            from_near = {1: h.z > 0, 2: None, 3: h.z < 3}[up]
            self.copies.append((wide, slim, to_near, from_near))

    def each(self, near, act_wide, act_slim):
        if near is None:
            act_slim()
            return

        @pl.when(near)
        def _():
            act_wide()

        @pl.when(jnp.logical_not(near))
        def _():
            act_slim()

    def start(self):
        for wide, slim, to_near, _ in self.copies:
            self.each(to_near, lambda: wide().start(), lambda: slim().start())

    def wait(self):
        for wide, slim, to_near, from_near in self.copies:
            self.each(to_near, lambda: wide().wait_send(), lambda: slim().wait_send())
            self.each(from_near, lambda: wide().wait_recv(), lambda: slim().wait_recv())


def put_in(ref, *at):
    def put(rows, value):
        ref[(*at, rows, slice(None))] = value.astype(ref.dtype)

    return put


def third_direct(work, *refs):
    second, third = work.second, work
    ins, normed, refs = refs[:11], refs[11], refs[12:]
    (gy, gg, behind, suff, gog, gskip, gout, ggw), (gout_low, ggw_low, ends, chip, held, far) = refs[:8], refs[8:14]
    (blocks, inbox, state, decay, no_all, every, low, lows), sems = refs[14:22], refs[22:]
    act, cum, flags, _, _, _, _, gate, cot, wo, gain = ins
    h = Here()
    w = Wires(*sems)
    spans = PLANE
    across, _ = h.mate(CHIPS[0])
    start = ends.at[h.z]
    gates = Rows(gg)

    def gno(span):
        late = jnp.where(span >= 4, 1, 0)
        return blocks.at[span - 4 * late, :, pl.ds(pl.multiple_of(late * WIDE, WIDE), WIDE)]

    greet(near(h) + line(h))
    mine = every.at[h.t]
    third_begin(gog, gskip, gout, ggw, state, decay)

    @pl.loop(0, spans, unroll=2)
    def _(step):
        taken = views(second.in_specs, ins, step)
        second_kernel(*taken, view(second.out_specs[0], gy, step), gno(step), mine.at[pl.ds(step, 1)])

    for o in range(1, 8):
        w.send(mine, every.at[h.t], 10 + o, h.mate(o)[0])
    for o in range(1, 8):
        device, place = h.mate(o)
        w.arrived(every.at[place], 10 + o, device)

    taking = (gy, gate, None, every, act, cum, flags, gain, cot, wo, normed)

    @pl.loop(0, spans, unroll=2)
    def _(step):
        taken = [gno(spans - 1 - step) if i == 2 else view(third.in_specs[i], taking[i], step) for i in range(8)]
        one, two, three, four = views(third.out_specs[:4], (gy, gg, behind, suff), step)
        third_first(step, *taken, one, two, three, four, start, gog, gskip, state, decay, no_all, gates)

    chain = Chain(h, w, ends, low, lows, True)
    chain.start()
    cross = w.make(held.at[0, 0 : SPAN // 2], far, 8, across)
    fold = Fold(h, w, 4, blocks, inbox, held, chip, lambda i: None if i else cross.start())

    @pl.loop(0, spans)
    def _(span):
        taken = views(third.in_specs[8:], taking[8:], span + spans)
        third_second(span, turn(span), *taken, blocks.at[fold.slot(span)], gout, ggw, no_all, gates)
        fold.step(span)

    gout_low[...] = gout[...].astype(bf16)
    ggw_low[...] = ggw[...].astype(bf16)
    fold.last()
    cross.wait()
    chain.wait()
    w.finish()


def fourth_direct(work, *refs):
    ins, (held, ggw, ggw_low), refs = refs[:16], refs[16:19], refs[19:]
    (gpre, hsum), (rmix, far, near_gate, far_gate) = refs[:2], refs[2:6]
    (parts, total, tails, steps, after), refs = refs[6:11], refs[11:]
    (out, blocks, inbox, outbox, gstep, edge, first), sems = refs[:7], refs[7:]
    h = Here()
    w = Wires(*sems)
    local = sems[2]
    spans = PLANE
    below, above = h.plane(3)[0], h.plane(1)[0]
    gate_planes = Planes(h, w, 32, ggw, ggw_low, lanes_at, near_gate, far_gate)

    def to_place(src, dst, base, keep, place):
        @pl.when(place != h.t)
        def _():
            x, c, y = bits(place)
            device = (h.z, 2 * x + c, y)
            w.make(src, dst, base + place, device, base + h.t).start()

        @pl.when(place == h.t)
        def _():
            pltpu.make_async_copy(src, dst, local.at[keep]).start()

    greet(near(h) + line(h))
    gate_planes.start()
    branch = [w.make(held.at[1 + i], rmix.at[i], 12 + i, h.mate(o)[0]) for i, o in enumerate(CHIPS[1:])]
    branch.append(w.make(held.at[0, SPAN // 2 : SPAN], far, 11, h.mate(CHIPS[0])[0]))
    for copy in branch:
        copy.start()
    chips = ToChips(h, w, 8, outbox, parts)
    fold = Fold(h, w, 4, blocks, inbox, outbox, total, chips)

    @pl.loop(0, spans)
    def _(step):
        place = turn(step)
        taken = views(work.in_specs, ins, place)
        mine = view(work.out_specs[0], gpre, place)
        fourth_kernel(step, *taken, mine, blocks.at[fold.slot(step)], gstep.at[step], hsum, out)
        fold.step(step)
        to_place(gstep.at[step], steps.at[h.t], 16, 1, place)

        @pl.when(place == 0)
        def _():
            edge[...] = mine[0:8, :]
            w.make(edge, after, 14, below).start()
            w.make(blocks.at[step, 0:8], first, 15, below).start()

        @pl.when(place > 0)
        def _():
            to_place(blocks.at[step, 0:8], tails.at[h.t], 24, 2, place - 1)

    w.arrived(first, 15, above)
    to_place(first, tails.at[h.t], 24, 2, 7)
    fold.last()
    gate_planes.wait()
    for copy in branch:
        copy.wait()
    w.make(edge, after, 14, below).wait()
    w.make(blocks.at[0, 0:8], first, 15, below).wait_send()
    for place in range(PLANE):

        @pl.when(place != h.t)
        def _():
            device = (h.z, place // 2, place % 2)
            w.make(gstep.at[0], steps.at[place], 16 + place, device).wait()
            w.make(first, tails.at[place], 24 + place, device).wait()

    pltpu.make_async_copy(gstep.at[0], steps.at[h.t], local.at[1]).wait()
    pltpu.make_async_copy(first, tails.at[h.t], local.at[2]).wait()
    chips.last()


def fifth_direct(work, *refs):
    ins, (ggw, near_gate, far_gate, gstate, gout, gout_low), refs = refs[:13], refs[13:19], refs[19:]
    (rgp, chip, pgate, pinner, ps, psmall, near_out, far_out), refs = refs[:8], refs[8:]
    (blocks, inbox, outbox), scratch, (ginner, giw, giw_low, small) = refs[:3], refs[3:6], refs[6:10]
    (near_inner, far_inner, zsum, gatesum, state_in, state_low, state_got), refs = refs[10:17], refs[17:]
    (ssum, rsmall, smallsum), sems = refs[:3], refs[3:]
    h = Here()
    w = Wires(*sems)
    local = sems[2]
    spans = PLANE
    mate, _ = h.mate(CORE)

    friends = near(h) + line(h)
    barrier = call(friends)
    lanes = pl.ds(pl.multiple_of(h.z * SPAN, SPAN), SPAN)
    gatesum[...] = from_planes(h.z, ggw[:, lanes], near_gate, far_gate).T
    pl.semaphore_wait(barrier, len(friends))
    out_planes = Planes(h, w, 0, gout, gout_low, head_rows, near_out, far_out)
    out_planes.start()
    state = []
    for i, o in enumerate((*CHIPS, 0)):
        near_core = w.make(gstate.at[:, h.mate(o ^ CORE)[1]], state_in.at[i], 24 + i, mate)
        on = w.make(state_low.at[i], state_got.at[i], 28 + i, h.mate(o)[0]) if o else None
        state.append((near_core, on))
        near_core.start()
    for o in range(1, 8):
        device, place = h.mate(o)
        w.send(rows_at(gatesum, place, 32), pgate.at[h.t], 44 + o, device)
    keep = [w.keep(rows_at(gatesum, h.t, 32), pgate.at[h.t])]
    for i, (o, (near_core, on)) in enumerate(zip((*CHIPS, 0), state)):
        near_core.wait()
        both = gstate[:, h.mate(o)[1]] + state_in[i]
        if on is None:
            ssum[...] = both
        else:
            state_low[i] = both.astype(bf16)
            on.start()

    chips = ToChips(h, w, 8, outbox, rgp)
    fold = Fold(h, w, 4, blocks, inbox, outbox, chip, chips)

    def conv_step(step):
        place = turn(step)
        taken = views(work.in_specs[:7], ins, place)
        fifth_kernel(place, spans, *taken, ginner.at[step], giw, small, *scratch)

    def block_step(step):
        taken = views(work.in_specs[11:], ins[11:], turn(step))
        blocks[fold.slot(step)] = fifth_product(taken[0], ginner[step], taken[1])
        fold.step(step, early=1)

    fifth_begin(*ins[7:11], giw, small)

    @pl.loop(0, 2)
    def _(step):
        conv_step(step)
        block_step(step)

    @pl.loop(2, spans)
    def _(step):
        conv_step(step)

        @pl.when(step == 3)
        def _():
            fold.settle(0)

    giw_low[...] = giw[...].astype(bf16)
    inner_planes = Planes(h, w, 16, giw, giw_low, lanes_at, near_inner, far_inner)
    inner_planes.start()
    for up in range(1, 4):
        w.send(small, rsmall.at[h.z], 20 + up, h.plane(up)[0])
    keep_small = w.keep(small, rsmall.at[h.z])
    pl.loop(2, spans)(block_step)
    fold.last()

    for _, on in state[:3]:
        on.wait()
    ssum[...] = ssum[...] + jnp.sum(state_got[...].astype(f32), axis=0)
    for up in range(1, 4):
        device, z = h.plane(up)
        w.send(ssum.at[z], ps.at[h.z], 32 + up, device)
    keep.append(w.keep(ssum.at[h.z], ps.at[h.z]))

    keep_small.wait()
    for up in range(1, 4):
        device, z = h.plane(4 - up)
        w.arrived(rsmall.at[z], 20 + up, device)
    smallsum[...] = jnp.sum(rsmall[...], axis=0)
    for i, o in enumerate((*CHIPS, CORE)):
        w.send(smallsum, psmall.at[h.t], 36 + i, h.mate(o)[0])
    keep.append(w.keep(smallsum, psmall.at[h.t]))

    inner_planes.wait()
    zsum[...] = from_planes(h.z, giw[:, lanes], near_inner, far_inner).T
    for o in range(1, 8):
        device, place = h.mate(o)
        w.send(rows_at(zsum, place, 32), pinner.at[h.t], 52 + o, device)
    keep.append(w.keep(rows_at(zsum, h.t, 32), pinner.at[h.t]))

    for i, o in enumerate(CHIPS):
        device, place = h.mate(o)
        w.arrived(psmall.at[place], 36 + i, device)
        w.send(psmall.at[place], psmall.at[place], 40 + i, mate)
    w.arrived(psmall.at[h.mate(CORE)[1]], 39, mate)
    for i, o in enumerate(CHIPS):
        w.arrived(psmall.at[h.mate(o ^ CORE)[1]], 40 + i, mate)
    for o in range(1, 8):
        device, place = h.mate(o)
        w.arrived(pgate.at[place], 44 + o, device)
        w.arrived(pinner.at[place], 52 + o, device)
    for up in range(1, 4):
        device, z = h.plane(4 - up)
        w.arrived(ps.at[z], 32 + up, device)
    chips.last()
    out_planes.wait()
    for copy in keep:
        copy.wait()
    w.finish()


def view(block, ref, step):
    if block.block_shape is None:
        return ref
    cuts, full = [], True
    for at, size, total in zip(block.index_map(step), block.block_shape, ref.shape):
        if size is pl.squeezed:
            cuts.append(at)
        elif size == total:
            cuts.append(slice(None))
            continue
        else:
            cuts.append(pl.ds(at * size if isinstance(at, int) else pl.multiple_of(at * size, size), size))
        full = False
    return ref if full else ref.at[tuple(cuts)]


def views(blocks, refs, step):
    return [view(block, ref, step) for block, ref in zip(blocks, refs)]


class Rows:
    def __init__(self, ref):
        self.ref = ref

    def __getitem__(self, span):
        return self.ref[pl.ds(pl.multiple_of(span * SPAN, SPAN), SPAN), :]

    def __setitem__(self, span, value):
        pass


def kept(dims, dtype=f32):
    return pltpu.VMEM(dims, dtype)


def flat(kernel, number, name, work, ins, outs, scratch, far=()):
    shapes = [*[kept(a.shape, a.dtype) for a in work.outs], *outs]
    return pl.pallas_call(
        functools.partial(kernel, work),
        in_specs=[IN_VMEM] * (len(work.ins) + len(ins)) + [IN_HBM] * len(far),
        out_specs=[IN_VMEM] * len(shapes),
        out_shape=shapes,
        scratch_shapes=scratch,
        compiler_params=pltpu.CompilerParams(
            collective_id=number, has_side_effects=True, vmem_limit_bytes=SMALL_LIMIT
        ),
        name=name,
    )(*work.ins, *ins, *[pltpu.with_memory_space_constraint(a, pltpu.HBM) for a in far])


def total_kernel(mine, every, planes, lines, send, recv, local):
    h = Here()
    w = Wires(send, recv, local)
    greet(near(h) + line(h))
    keep = w.keep(mine, planes.at[h.z])
    for up in range(1, 4):
        w.send(mine, planes.at[h.z], up, h.plane(up)[0])
    keep.wait()
    for up in range(1, 4):
        device, z = h.plane(4 - up)
        w.arrived(planes.at[z], up, device)
    lines[...] = jnp.sum(planes[...], axis=0)
    for o in range(1, 8):
        w.send(lines, every.at[h.t], 3 + o, h.mate(o)[0])
    keep = w.keep(lines, every.at[h.t])
    for o in range(1, 8):
        device, place = h.mate(o)
        w.arrived(every.at[place], 3 + o, device)
    keep.wait()
    w.finish()


def vmem(*dims, dtype=f32):
    return pltpu.VMEM(dims, dtype)


class Direct:
    @staticmethod
    def start(in_weight, out_weight, tokens, docs, conv, head, gain, norm):
        rows = PLANE * SPAN
        outs = [kept((D, MAIN), bf16), kept((4, PLANE, 32, SHARED), bf16), kept((rows, D), bf16), kept((16, D), bf16),
                kept((8, LOCAL)), kept((1, 128)), kept((1, 128)), kept((1, WIDE)), kept((1, WIDE)),
                kept((128, 128), bf16), kept((4, 1, WIDE)), kept((4, 1, WIDE)), kept((rows + 8, 8)),
                kept((PLANE, 1, SPAN)), kept(out_weight.shape, bf16), kept((1, D))]
        ins = [in_weight, out_weight, tokens, docs.reshape(-1, 128), conv, head, gain, norm]
        ins = [pltpu.with_memory_space_constraint(a, pltpu.HBM) for a in ins]
        loaded = [ins[i] for i in (0, 1, 3, 4, 5, 6)]
        wm, ws, x, halo, *prepared, flags, doc_rows, out_low, norm = pl.pallas_call(
            start_kernel,
            in_specs=[IN_HBM] * len(ins),
            out_specs=[IN_VMEM] * len(outs),
            out_shape=outs,
            scratch_shapes=[*[pltpu.VMEM(a.shape, a.dtype) for a in loaded], vmem(PLANE, 32, MAIN, dtype=bf16),
                            vmem(32, SHARED, dtype=bf16)] + wires(51, 10),
            compiler_params=pltpu.CompilerParams(collective_id=0, has_side_effects=True, vmem_limit_bytes=SMALL_LIMIT),
            name="gather_start",
        )(*ins)
        return wm, ws.reshape(D, SHARED), x, halo, prepared, flags, doc_rows, out_low, norm

    @staticmethod
    def first(spans, work, cotangent, out):
        rows = spans * SPAN
        return flat(
            first_direct, 1, "project_scan", work, [out],
            [kept((NSTATE, WIDE)), kept((rows, D), bf16), kept((WIDE, D), bf16)],
            [*work.scratch[:3], vmem(4, PACK, WIDE), vmem(PACK, WIDE, dtype=bf16), vmem(4, PACK, WIDE, dtype=bf16)]
            + wires(16, 2), [cotangent],
        )

    @staticmethod
    def second(spans, work):
        return work, None, None

    @staticmethod
    def third(spans, work):
        work.second, normed = work.ins[0], work.ins[10]
        work.ins = [*work.second.ins, normed]
        *outs, gout, ggw, gout_low, ggw_low, ends, chip, held, far = flat(
            third_direct, 4, "carry_gate_back", work, [],
            [kept((WIDE, D), bf16), kept((WIDE, D), bf16), kept((4, PACK, WIDE)), kept((SPAN, D)),
             kept((3, SPAN, D), bf16), kept((SPAN // 2, D), bf16)],
            [vmem(4, SPAN, D), vmem(4, SPAN, D), *work.scratch[:3], vmem(PLANE, spans, 2, SPAN),
             vmem(PACK, WIDE, dtype=bf16), vmem(4, PACK, WIDE, dtype=bf16)] + wires(18, 1),
        )
        return *outs, (gout, gout_low), (ggw, ggw_low), ends, (chip, held, far)

    @staticmethod
    def fourth(spans, work, gout, ggw, mix):
        chip, held, far = mix
        gpre, hsum, rmix, far2, near_gate, far_gate, parts, own, tails, steps, after = flat(
            fourth_direct, 5, "scan_back", work, [held, *ggw],
            [kept((2, SPAN, D), bf16), kept((SPAN // 2, D), bf16), kept((2, WIDE, SPAN)),
             kept((3, WIDE, SPAN), bf16), kept((3, SPAN, STATES), bf16), kept((SPAN, STATES)), kept((PLANE, 8, STATES)),
             kept((PLANE, 8, SPAN)), kept((8, WIDE))],
            [*work.scratch, vmem(PLANE, SPAN, STATES), vmem(4, SPAN, STATES), vmem(3, SPAN, STATES, dtype=bf16), vmem(spans, 8, SPAN),
             vmem(8, WIDE), vmem(8, STATES)] + wires(36, 3),
        )
        ggw = [ggw[0], near_gate, far_gate]
        return gpre, hsum, [parts, own], tails, steps, after, gout, [chip, far, far2, rmix], ggw

    @staticmethod
    def fifth(spans, work, ggw, grad_state, gout):
        piece = vmem(4, 4, 32, SHARED)
        rgp, chip, pgate, pinner, ps, psmall, near_out, far_out, *spare = flat(
            fifth_direct, 6, "conv_back_reduce", work, [*ggw, grad_state.reshape(4, PLANE, 32, SHARED), *gout],
            [kept((3, SPAN, D), bf16), kept((SPAN, D)), kept((PLANE, 32, WIDE)), kept((PLANE, 32, WIDE)),
             kept((4, 32, SHARED)), kept((PLANE, SMALL, WIDE)), kept((2, HEAD_DIM, D)), kept((3, HEAD_DIM, D), bf16),
             kept((4, SPAN, D)), kept((4, SPAN, D)), kept((3, SPAN, D), bf16)],
            [*work.scratch, vmem(spans, SPAN, WIDE, dtype=bf16), vmem(WIDE, D), vmem(WIDE, D, dtype=bf16),
             vmem(SMALL, WIDE), vmem(2, SPAN, WIDE), vmem(3, SPAN, WIDE, dtype=bf16),
             vmem(SPAN, WIDE), vmem(SPAN, WIDE), piece, vmem(3, 4, 32, SHARED, dtype=bf16),
             vmem(3, 4, 32, SHARED, dtype=bf16), vmem(4, 32, SHARED),
             vmem(4, SMALL, WIDE), vmem(SMALL, WIDE)] + wires(60, 5),
        )
        return pgate, pinner, ps, [chip, rgp], psmall, spare, [gout[0], near_out, far_out]

    @staticmethod
    def total(part):
        return talk(
            total_kernel, 9, "sum_all", [kept((PLANE, *part.shape))], [part],
            [vmem(4, *part.shape), vmem(*part.shape)] + wires(11, 2),
        )[0]


class Plain:
    @staticmethod
    def start(in_weight, out_weight, tokens, docs, conv, head, gain, norm):
        main, shared, out_low = run_pack(in_weight, out_weight)
        rows = main.shape[1]
        main = lax.all_to_all(main, TP, split_axis=0, concat_axis=0, tiled=True)
        main = lax.all_gather(main.reshape(PLANE * rows, MAIN), "grp", axis=0, tiled=True)
        shared = lax.all_gather(shared, ALL, axis=0, tiled=True)
        x = lax.all_gather(tokens, TP, axis=0, tiled=True)
        groups, group = lax.axis_size("grp"), lax.axis_index("grp")
        halo = lax.ppermute(x[x.shape[0] - 16 :], "grp", [(g, (g + 1) % groups) for g in range(groups)])
        at = jnp.stack([group, lax.axis_index(TP)])
        flags = plain_flags(docs, group, x.shape[0])
        return main, shared, x, halo, run_prep(groups, at, conv, head, gain), *flags, out_low, norm

    @staticmethod
    def first(spans, work, cotangent, out):
        *outs, end = launch(
            functools.partial(first_plain, spans), "project_scan", 2 * spans, work.in_specs, work.ins,
            [*work.out_specs, whole(PACK, WIDE)], [*work.outs, shape(PACK, WIDE)], work.scratch,
        )
        groups, group = lax.axis_size("grp"), lax.axis_index("grp")
        ends = lax.all_gather(end, "grp")

        def one(g, carried):
            return jnp.where(g < group, ends[g, NSTATE : NSTATE + 1] * carried + ends[g, :NSTATE], carried)

        inc = lax.fori_loop(0, groups, one, jnp.zeros((NSTATE, WIDE), f32))
        every = lax.all_gather(out, ALL, axis=0, tiled=True).reshape(HERE, PLANE, HEAD_DIM, D)
        wo = lax.dynamic_index_in_dim(every, lax.axis_index(TP), 1, False).reshape(WIDE, D)
        return *outs, inc, lax.all_gather(cotangent, TP, axis=0, tiled=True), wo

    @staticmethod
    def second(spans, work):
        y, gno, sums = launch(
            second_kernel, "scan_carry", spans, work.in_specs, work.ins,
            [*work.out_specs, spec((1, 2, SPAN), lambda s: (s, 0, 0))], [*work.outs, shape(spans, 2, SPAN)],
        )
        return y, gno, lax.all_gather(sums, TP)

    @staticmethod
    def third(spans, work):
        start = (whole(PACK, WIDE), shape(PACK, WIDE))
        mix = (work.later(D), shape(spans * SPAN, D))
        *outs, start, mix = launch(
            functools.partial(third_plain, spans), "gate_norm_back", 2 * spans, work.in_specs, work.ins,
            [*work.out_specs, start[0], mix[0]], [*work.outs, start[1], mix[1]], work.scratch,
        )
        return *outs, lax.all_gather(start, "grp"), lax.psum_scatter(mix, TP, scatter_dimension=0, tiled=True)

    @staticmethod
    def fourth(spans, work, gout, ggw, mix):
        rows = spans * SPAN
        gpre, hsum, gst, gstep = launch(
            fourth_plain, "scan_back", spans, work.in_specs, work.ins,
            [*work.out_specs, spec((SPAN, STATES), lambda s: (s, 0)), spec((8, SPAN), lambda s: (0, s))],
            [*work.outs, shape(rows, STATES), shape(8, rows)], work.scratch,
        )
        groups = lax.axis_size("grp")
        back = [(g, (g - 1) % groups) for g in range(groups)]
        swap = lambda a: lax.all_to_all(a, TP, split_axis=0, concat_axis=0, tiled=True)
        blocks = gst.reshape(PLANE, SPAN, STATES)
        tails = jnp.concatenate([blocks[1:, 0:8], lax.ppermute(gst[0:8], "grp", back)[None]], axis=0)
        steps = gstep.reshape(8, PLANE, SPAN).transpose(1, 0, 2)
        empty = jnp.zeros((HERE, PLANE, HEAD_DIM, D), f32)
        mine = gout.reshape(HERE, HEAD_DIM, D)
        every = lax.dynamic_update_index_in_dim(empty, mine, lax.axis_index(TP), 1).reshape(INNER, D)
        out = lax.psum_scatter(every, ALL, scatter_dimension=0, tiled=True)
        after = lax.ppermute(gpre[0:8], "grp", back)
        return gpre, hsum, [swap(blocks)], swap(tails), swap(steps), after, [out], [mix], ggw

    @staticmethod
    def fifth(spans, work, ggw, grad_state, gout):
        gp, giw, small = launch(
            functools.partial(fifth_plain, spans), "conv_back", spans, work.in_specs, work.ins,
            [spec((SPAN, D), lambda s: (s, 0)), whole(WIDE, D), whole(SMALL, WIDE)],
            [shape(spans * SPAN, D), shape(WIDE, D), shape(SMALL, WIDE)],
            [*work.scratch, pltpu.VMEM((SPAN, WIDE), bf16)],
        )
        inner_z = lax.psum_scatter(giw.T, "grp", scatter_dimension=0, tiled=True)
        gate_z = lax.psum_scatter(ggw.T, "grp", scatter_dimension=0, tiled=True)
        rows = inner_z.shape[0] // PLANE
        home = lambda a: lax.all_to_all(a.reshape(PLANE, rows, WIDE), TP, split_axis=0, concat_axis=0, tiled=True)
        state = lax.psum_scatter(grad_state, ALL, scatter_dimension=0, tiled=True)
        small = lax.all_gather(lax.psum(small, "grp"), TP)
        gp = lax.psum_scatter(gp, TP, scatter_dimension=0, tiled=True)
        return home(gate_z), home(inner_z), state[None], [gp], small, [], gout

    @staticmethod
    def total(part):
        return lax.psum(part, ALL)[None]


def run_pack(in_weight, out_weight):
    rows = in_weight.shape[0]
    return pl.pallas_call(
        pack_kernel,
        out_shape=[shape(PLANE, rows, MAIN, dtype=bf16), shape(rows, SHARED, dtype=bf16),
                   shape(*out_weight.shape, dtype=bf16)],
        compiler_params=pltpu.CompilerParams(vmem_limit_bytes=SMALL_LIMIT),
        name="pack_weights",
    )(in_weight, out_weight)


def plain_flags(doc_ids, group, rows):
    spans = rows // SPAN
    padded = jnp.concatenate([jnp.full((8,), -1, jnp.int32), doc_ids, jnp.full((8,), -2, jnp.int32)])
    window = lax.dynamic_slice(padded, (group * rows,), (rows + 16,))
    now = window[8:]
    lags = [now == window[8 - k : rows + 16 - k] for k in range(1, CONV)]
    by_span = window[8 : rows + 8].reshape(spans, SPAN)
    rise = by_span == window[7 : rows + 7 : SPAN][:, None]
    tail = by_span == by_span[:, SPAN - 1 :]
    fill = lambda a: jnp.pad(a.reshape(rows), (0, 8))
    zero = jnp.zeros_like(now)
    flags = jnp.stack([a.astype(f32) for a in (*lags, fill(rise), fill(tail), now, zero, zero)], axis=1)
    return flags, by_span.astype(f32).reshape(spans, 1, SPAN)


def shards(
    plan,
    tokens, cotangent, doc_ids, norm_gain, in_weight, conv_params, head_params, out_gain, out_weight,
    norm_first, norm_second, in_first, in_second, conv_first, conv_second, head_first, head_second,
    gain_first, gain_second, out_first, out_second,
):
    groups = lax.axis_size("grp")
    group = lax.axis_index("grp")
    place = lax.axis_index(TP)
    tok_rows = tokens.shape[0]
    rows = PLANE * tok_rows
    spans = rows // SPAN

    wm, ws, x, halo, prepared, flags, doc_rows, out_low, norm_row = plan.start(
        in_weight, out_weight, tokens, doc_ids, conv_params, head_params, out_gain.reshape(INNER // 128, 128),
        norm_gain.reshape(1, D),
    )
    conv, bias, rate, skip, gain, pick, before_us, behind_us = prepared

    normed, gate, chan, pre, act, dt, cum, held, pref, edge, part, incoming, cot, wo = plan.first(
        spans, First(spans, x, halo, norm_row, wm, ws, pick, conv, bias, rate, flags, doc_rows, skip, before_us),
        cotangent, out_low,
    )
    y, gno, sums = plan.second(spans, Second(spans, act, cum, flags, held, pref, incoming, part, gate, cot, wo, gain))
    gy, ggate, behind, suff, gog, gskip, gout, ggw, starts, mix = plan.third(
        spans, Third(spans, y, gate, gno, sums, act, cum, flags, gain, cot, wo, normed)
    )
    gpre, hsum, parts, tails, steps, after, gout, mix, ggw = plan.fourth(
        spans,
        Fourth(spans, act, dt, cum, flags, doc_rows, held, pref, incoming, behind, suff, starts, behind_us, gy, pre,
               skip, rate),
        gout, ggw, mix,
    )
    gs, gconv_state, grad_state = run_sixth(parts, tails, steps, flags, chan, edge, conv, tokens, norm_row)
    g_gate, g_inner, g_shared, gp, small, spare, grads_out = plan.fifth(
        spans,
        Fifth(spans, gpre, after, flags, chan, edge, conv, normed, gconv_state, gog, gskip, hsum, ggate, wm),
        ggw, grad_state, gout,
    )
    mixed, grad_tokens, grad_norm_gain = run_seventh(gp, mix, gs, ws, tokens, cotangent, norm_row, spare)
    in_f, in_s, in_u, out_f, out_s, out_u, sums = run_adam(
        g_gate, g_inner, g_shared, grad_norm_gain, in_weight, in_first, in_second,
        out_weight, out_first, out_second, grads_out,
    )
    norm3 = [a.reshape(D // 128, 128) for a in (norm_gain, norm_first, norm_second)]
    gain3 = [a.reshape(INNER // 128, 128) for a in (out_gain, gain_first, gain_second)]
    params = [*norm3, conv_params, conv_first, conv_second, head_params, head_first, head_second, *gain3]
    in_w, out_w, *rest = run_last(plan.total(sums), small, [in_weight, in_u, out_weight, out_u], params)
    rest[0:3] = [a.reshape(D) for a in rest[0:3]]
    rest[9:12] = [a.reshape(INNER) for a in rest[9:12]]
    return (mixed, grad_tokens, *rest[0:3], in_f, in_s, in_w, *rest[3:12], out_f, out_s, out_w)


def solution(mesh):
    seq = mesh.shape["seq"]
    sub = PLANE // seq
    groups = mesh.shape["fsdp"] // sub
    cut = Mesh(mesh.devices.reshape(groups, sub, seq), ALL)
    plan = Direct if (groups, sub, seq) == (4, 4, 2) else Plain
    split = P(ALL, None)
    none = P()
    return jax.shard_map(
        functools.partial(shards, plan),
        mesh=cut,
        in_specs=(split, split, none, none, split, none, none, none, split, none, none, split, split)
        + (none,) * 6
        + (split, split),
        out_specs=(split, split) + (none,) * 3 + (split,) * 3 + (none,) * 9 + (split,) * 3,
        check_vma=False,
    )
```

```python
import functools

import jax
import jax.numpy as jnp
from jax import lax
from jax.experimental import pallas as pl
from jax.experimental.pallas import tpu as pltpu
from jax.sharding import Mesh, PartitionSpec as P

HEADS = 32
HEAD_DIM = 64
NSTATE = 128
CONV = 4
SPAN = 256
STEP = 10
INNER = 2048
D = 1024

EPS_NORM = 1e-05
BETA_ONE = 0.9
BETA_TWO = 0.999
ADAM_EPS = 1e-06
DECAY = 0.01
RATE = 0.5

PLANE = 8
HERE = HEADS // PLANE
WIDE = HERE * HEAD_DIM
STATES = 2 * NSTATE
LOCAL = WIDE + STATES
PACK = NSTATE + 8
MAIN = 2 * WIDE
SHARED = STATES + 128
SMALL = 24
TP = ("sub", "seq")
ALL = ("grp", "sub", "seq")

f32 = jnp.float32
bf16 = jnp.bfloat16


def dot(a, b, ca=1, cb=0):
    return lax.dot_general(a, b, (((ca,), (cb,)), ((), ())), preferred_element_type=f32)


def split2(x):
    high = x.astype(bf16)
    return high, (x - high.astype(f32)).astype(bf16)


def split3(x):
    high = x.astype(bf16)
    rest = x - high.astype(f32)
    mid = rest.astype(bf16)
    return high, mid, (rest - mid.astype(f32)).astype(bf16)


def exact_left(a, b, ca=1, cb=0):
    high, low = split2(b)
    return dot(a, high, ca, cb) + dot(a, low, ca, cb)


def exact_right(a, b, ca=1, cb=0):
    high, low = split2(a)
    return dot(high, b, ca, cb) + dot(low, b, ca, cb)


def both_split(a, b, ca=1, cb=0):
    ah, al = split2(a)
    bh, bl = split2(b)
    return dot(ah, bh, ca, cb) + dot(al, bh, ca, cb) + dot(ah, bl, ca, cb)


def running(mask, x):
    a, b, c = split3(x)
    return dot(mask, a) + dot(mask, b) + dot(mask, c)


def spread(cols):
    lane = lax.broadcasted_iota(jnp.int32, (cols.shape[0], 128), 1)
    halves = [
        jnp.where(lane < HEAD_DIM, cols[:, 2 * i : 2 * i + 1], cols[:, 2 * i + 1 : 2 * i + 2])
        for i in range(HERE // 2)
    ]
    return jnp.concatenate(halves, axis=1)


def head_sum(x):
    row = lax.broadcasted_iota(jnp.int32, (WIDE, 128), 0)
    lane = lax.broadcasted_iota(jnp.int32, (WIDE, 128), 1)
    pick = (row // HEAD_DIM == lane).astype(bf16)
    return exact_right(x, pick)


def sigmoid(x):
    return 1.0 / (1.0 + jnp.exp(-x))


def half_tanh(x):
    return 0.5 * jnp.tanh(0.5 * x) + 0.5


def silu(x):
    return x * half_tanh(x)


def silu_slope(x):
    s = half_tanh(x)
    return s * (1.0 + x * (1.0 - s))


def lower(rows):
    i = lax.broadcasted_iota(jnp.int32, (rows, rows), 0)
    j = lax.broadcasted_iota(jnp.int32, (rows, rows), 1)
    return j <= i


def head_mask(x, h):
    lane = lax.broadcasted_iota(jnp.int32, x.shape, 1)
    return jnp.where(lane // HEAD_DIM == h, x, jnp.zeros_like(x))


def pack_kernel(wi_ref, wo_ref, main_ref, shared_ref, out_ref):
    weight = wi_ref[...].astype(bf16)
    for base in (0, 1):
        for t in range(PLANE):
            lanes = slice(HEAD_DIM * (t % 2), HEAD_DIM * (t % 2 + 1))
            for half in range(HERE // 2):
                tiles = []
                for i in (2 * half, 2 * half + 1):
                    at = base * INNER + i * PLANE * HEAD_DIM + t // 2 * 128
                    tiles.append(weight[:, at : at + 128][:, lanes])
                at = base * WIDE + 128 * half
                main_ref[t, :, at : at + 128] = jnp.concatenate(tiles, axis=1)
    shared_ref[...] = jnp.zeros_like(shared_ref)
    shared_ref[:, : STATES + HEADS] = weight[:, 2 * INNER :]
    out_ref[...] = wo_ref[...].astype(bf16)


def prepare(
    group, place, conv_ref, head_ref, gain_ref,
    conv_out, bias_out, rate_out, skip_out, gain_out, pick_out, before_out, behind_out,
):
    pair = jnp.where(place >= 2, 1, 0) + jnp.where(place >= 4, 1, 0) + jnp.where(place >= 6, 1, 0)
    odd = place - 2 * pair == 1

    def half(x):
        return jnp.where(odd, x[:, HEAD_DIM:], x[:, :HEAD_DIM])

    def four(get):
        halves = [half(get(i)) for i in range(HERE)]
        return [jnp.concatenate(halves[2 * i : 2 * i + 2], axis=1) for i in range(HERE // 2)]

    conv_out[...] = jnp.zeros_like(conv_out)
    columns = lambda i: conv_ref[:, pl.ds(pl.multiple_of(i * PLANE * HEAD_DIM + pair * 128, 128), 128)]
    for i, tile in enumerate(four(columns)):
        conv_out[0 : CONV + 1, 128 * i : 128 * (i + 1)] = tile
    conv_out[0 : CONV + 1, WIDE:] = conv_ref[:, INNER:]
    for i, tile in enumerate(four(lambda i: gain_ref[pl.ds(i * PLANE // 2 + pair, 1), :])):
        gain_out[:, 128 * i : 128 * (i + 1)] = tile
    head = lax.broadcasted_iota(jnp.int32, (3, HEADS), 1)
    lane = lax.broadcasted_iota(jnp.int32, (3, 128), 1)
    mine = jnp.zeros((3, 128), f32)
    for i in range(HERE):
        one = jnp.sum(jnp.where(head == PLANE * i + place, head_ref[...], 0.0), axis=1, keepdims=True)
        mine = mine + jnp.where(lane == i, one, 0.0)
    bias_out[...] = mine[0:1]
    rate_out[...] = jnp.where(lane[0:1] < HERE, -jnp.exp(mine[1:2]), 0.0)
    skip_out[...] = spread(jnp.broadcast_to(mine[2:3], (8, 128)))[0:1]
    row = lax.broadcasted_iota(jnp.int32, (128, 128), 0)
    column = lax.broadcasted_iota(jnp.int32, (128, 128), 1)
    pick_out[...] = jnp.where((row == PLANE * column + place) & (row < HEADS), 1.0, 0.0).astype(bf16)
    rank = lax.broadcasted_iota(jnp.int32, before_out.shape, 0)
    before_out[...] = (rank < group).astype(f32)
    behind_out[...] = (rank > group).astype(f32)


def flags_of(z, docs, flags, doc_rows):
    lines = PLANE * SPAN // 128
    lane = lax.broadcasted_iota(jnp.int32, (1, 128), 1)
    total = docs.shape[0]
    first = z * lines

    def line(i):
        at = first + i
        inside = jnp.clip(at, 0, total - 1)
        got = docs[pl.ds(inside, 1), :].astype(f32)
        return jnp.where(at < 0, -1.0, jnp.where(at >= total, -2.0, got))

    rows = [line(i) for i in range(-1, lines + 1)]
    for i in range(lines + 1):
        now, last = rows[i + 1], rows[i]
        same = []
        for k in range(1, CONV):
            moved = jnp.where(lane < k, pltpu.roll(last, k, 1), pltpu.roll(now, k, 1))
            same.append((moved == now).astype(f32))
        span = min(i, lines - 1) // 2
        rise = (now == rows[2 * span][:, 127:128]).astype(f32)
        tail = (now == rows[2 * span + 2][:, 127:128]).astype(f32)
        both = jnp.concatenate([*same, rise, tail, now, now * 0.0, now * 0.0], axis=0).T
        if i < lines:
            flags[128 * i : 128 * (i + 1), :] = both
            doc_rows[i // 2, :, 128 * (i % 2) : 128 * (i % 2 + 1)] = now
        else:
            flags[128 * i : 128 * i + 8, :] = both[0:8, :]


def prep_kernel(at_ref, *refs):
    prepare(at_ref[0], at_ref[1], *refs)


def normalize(rows, gain):
    vals = rows.astype(f32)
    inv = lax.rsqrt(jnp.mean(vals * vals, axis=1, keepdims=True) + EPS_NORM)
    return (vals * inv * gain).astype(bf16)


def first_begin(halo_ref, ng_ref, wm_ref, ws_ref, edge_ref, ext, state, decay):
    before = normalize(halo_ref[...], ng_ref[...])
    inner = dot(before, wm_ref[:, WIDE : 2 * WIDE]).astype(bf16).astype(f32)
    shared = dot(before, ws_ref[:, :STATES]).astype(bf16).astype(f32)
    rows = jnp.concatenate([inner, shared], axis=1)[8:16]
    ext[SPAN : SPAN + 8, :] = rows
    edge_ref[...] = rows
    state[...] = jnp.zeros_like(state)
    decay[...] = jnp.ones_like(decay)


def first_phase(
    span, x_ref, halo_ref, ng_ref, wm_ref, ws_ref, pick_ref, conv_ref, bias_ref, rate_ref, fl_ref,
    normed_ref, gate_ref, chan_ref, pre_ref, act_ref, dt_ref, cum_ref, held_ref, pref_ref, edge_ref,
    ext, state, decay, end_ref, act_all, dt_all, cum_all,
):
    ext[0:8, :] = ext[SPAN : SPAN + 8, :]
    normed = normalize(x_ref[...], ng_ref[...])
    normed_ref[...] = normed
    main = dot(normed, wm_ref[...]).astype(bf16)
    shared = dot(normed, ws_ref[...]).astype(bf16)
    gate_ref[...] = main[:, :WIDE]
    chan = jnp.concatenate([main[:, WIDE:], shared[:, :STATES]], axis=1)
    chan_ref[...] = chan
    ext[8 : SPAN + 8, :] = chan.astype(f32)
    flags = fl_ref[...]
    pre = conv_ref[4:5, :] + ext[8 : SPAN + 8, :] * conv_ref[0:1, :]
    for k in range(1, CONV):
        moved = ext[8 - k : SPAN + 8 - k, :] * conv_ref[k : k + 1, :]
        pre = pre + jnp.where(flags[:, k - 1 : k] > 0.5, moved, 0.0)
    pre_ref[...] = pre
    act = silu(pre).astype(bf16)
    act_ref[...] = act
    act_all[span] = act
    step = dot(shared[:, STATES:], pick_ref[...]) + bias_ref[...]
    dt = jnp.maximum(step, 0.0) + jnp.log1p(jnp.exp(-jnp.abs(step)))
    lane = lax.broadcasted_iota(jnp.int32, dt.shape, 1)
    both = jnp.where(lane < HEAD_DIM, dt, pltpu.roll(sigmoid(step), HEAD_DIM, 1))
    dt_ref[...] = both
    dt_all[span] = both
    cum = running(lower(SPAN).astype(bf16), dt * rate_ref[...])
    cum_ref[...] = cum
    cum_all[span] = cum
    last = cum[SPAN - 1 : SPAN, :]
    ending = jnp.where(flags[:, 4:5] > 0.5, jnp.exp(last - cum), 0.0)
    inner = act[:, :WIDE]
    write = act[:, WIDE : WIDE + NSTATE]
    added = exact_left(write, spread(ending * dt) * inner.astype(f32), 0, 0)
    held = state[...]
    held_ref[0] = held
    pref_ref[0] = decay[...]
    closing = jnp.where(flags[SPAN - 1 : SPAN, 3:4] > 0.5, jnp.exp(last), 0.0)
    fade = spread(jnp.broadcast_to(closing, (8, 128)))
    held = fade[0:1, :] * held + added
    state[...] = held
    decay[...] = decay[...] * fade
    end_ref[0:NSTATE, :] = held
    end_ref[NSTATE:, :] = decay[...]


def carry_chain(ends_ref, ahead_ref, out_ref, reverse):
    out_ref[...] = jnp.zeros_like(out_ref)
    groups = ends_ref.shape[0]

    @pl.loop(0, groups)
    def _(step):
        g = groups - 1 - step if reverse else step
        one = ends_ref[g]
        on = ahead_ref[g] > 0.5
        held = out_ref[...]
        out_ref[...] = jnp.where(on, one[NSTATE : NSTATE + 1, :] * held + one[0:NSTATE, :], held)


def within_phase(span, fl_ref, row_ref, skip_ref, y_ref, act_all, dt_all, cum_all):
    act = act_all[span]
    inner = act[:, :WIDE]
    cum = cum_all[span]
    cum_t = cum.T
    dt_t = dt_all[span].T
    scores = dot(act[:, WIDE + NSTATE :], act[:, WIDE : WIDE + NSTATE], 1, 1)
    matched = (fl_ref[:, 5:6] == row_ref[0]) & lower(SPAN)
    y = skip_ref[...] * inner.astype(f32)
    for h in range(HERE):
        fade = jnp.exp(jnp.minimum(cum[:, h : h + 1] - cum_t[h : h + 1, :], 0.0))
        mixing = jnp.where(matched, fade, 0.0) * scores * dt_t[h : h + 1, :]
        y = y + exact_right(mixing, head_mask(inner, h))
    y_ref[...] = y


def second_kernel(
    read_ref, cum_ref, fl_ref, held_ref, pref_ref, inc_ref, part_ref, gate_ref, cot_ref, wo_ref, og_ref,
    y_ref, gno_ref, sums_ref,
):
    entering = held_ref[0] + pref_ref[0][0:1, :] * inc_ref[...]
    rising = jnp.where(fl_ref[:, 3:4] > 0.5, jnp.exp(cum_ref[...]), 0.0)
    y_low = (part_ref[...] + spread(rising) * exact_left(read_ref[...], entering)).astype(bf16)
    y_ref[...] = y_low
    gated = y_low.astype(f32) * silu(gate_ref[...].astype(f32))
    gno = dot(cot_ref[...], wo_ref[...], 1, 1)
    gno_ref[...] = gno
    squares = jnp.sum(gated * gated, axis=1, keepdims=True)
    along = jnp.sum(gno * og_ref[...] * gated, axis=1, keepdims=True)
    lane = lax.broadcasted_iota(jnp.int32, (SPAN, 128), 1)
    both = jnp.where(lane == 0, squares, jnp.where(lane == 1, along, 0.0))
    sums_ref[0] = both.T[0:2, :]


def third_begin(gog_ref, gskip_ref, gout_ref, ggw_ref, state, decay):
    for ref in (gog_ref, gskip_ref, gout_ref, ggw_ref, state):
        ref[...] = jnp.zeros_like(ref)
    decay[...] = jnp.ones_like(decay)


def third_first(
    at, y_ref, gate_ref, gno_ref, sums_ref, act_ref, cum_ref, fl_ref, og_ref,
    gy_ref, gg_ref, behind_ref, suff_ref, start_ref, gog_ref, gskip_ref,
    state, decay, no_all, gg_all,
):
    span = no_all.shape[0] - 1 - at
    act = act_ref[...]
    inner = act[:, :WIDE].astype(f32)
    read = act[:, WIDE + NSTATE :]
    flags = fl_ref[...]
    totals = jnp.sum(sums_ref[...], axis=0)
    inv_row = lax.rsqrt(totals[0:1, :] / INNER + EPS_NORM)
    mean_row = inv_row * totals[1:2, :] / INNER
    cols = jnp.concatenate([inv_row, mean_row, jnp.zeros((6, SPAN), f32)], axis=0).T
    inv = cols[:, 0:1]
    mean = cols[:, 1:2]
    y = y_ref[...].astype(f32)
    gate = gate_ref[...].astype(f32)
    gate_act = silu(gate)
    unit = y * gate_act * inv
    gno = gno_ref[...]
    no_all[span] = (unit * og_ref[...]).astype(bf16)
    grad_gated = inv * (gno * og_ref[...] - unit * mean)
    gy = (grad_gated * gate_act).astype(bf16)
    gy_ref[...] = gy
    ggate = (grad_gated * y * silu_slope(gate)).astype(bf16)
    gg_ref[...] = ggate
    gg_all[span] = ggate
    gyf = gy.astype(f32)
    gog_ref[...] += jnp.sum(gno * unit, axis=0, keepdims=True)
    gskip_ref[...] += jnp.sum(inner * gyf, axis=0, keepdims=True)
    rising = jnp.where(flags[:, 3:4] > 0.5, jnp.exp(cum_ref[...]), 0.0)
    wide = spread(rising)
    pulled = exact_left(read, wide * gyf, 0, 0)
    held = state[...]
    behind_ref[0] = held
    suff_ref[0] = decay[...]
    fade = wide[SPAN - 1 : SPAN, :]
    held = fade * held + pulled
    state[...] = held
    decay[...] = decay[...] * fade
    start_ref[0:NSTATE, :] = held
    start_ref[NSTATE:, :] = decay[...]


def third_second(span, place, cot_ref, wo_ref, normed_ref, mix_ref, gout_ref, ggw_ref, no_all, gg_all):
    mix_ref[...] = dot(no_all[place], wo_ref[...])
    gout_ref[...] += dot(no_all[span], cot_ref[...], 0, 0)
    ggw_ref[...] += dot(gg_all[span], normed_ref[...], 0, 0)


def fourth_kernel(
    at, act_ref, dt_ref, cum_ref, fl_ref, row_ref, held_ref, pref_ref, inc_ref, behind_ref, suff_ref,
    ends_ref, ahead_ref, gy_ref, pre_ref, skip_ref, rate_ref,
    gpre_ref, gst_ref, gstep_ref, hsum_ref,
    out_ref,
):
    @pl.when(at == 0)
    def _():
        hsum_ref[...] = jnp.zeros_like(hsum_ref)
        carry_chain(ends_ref, ahead_ref, out_ref, True)

    act = act_ref[...]
    inner = act[:, :WIDE]
    innerf = inner.astype(f32)
    write = act[:, WIDE : WIDE + NSTATE]
    read = act[:, WIDE + NSTATE :]
    flags = fl_ref[...]
    cum = cum_ref[...]
    dt = dt_ref[...]
    gy = gy_ref[...]
    gyf = gy.astype(f32)
    cum_t = cum.T
    entering = held_ref[0] + pref_ref[0][0:1, :] * inc_ref[...]
    leaving = behind_ref[0] + suff_ref[0][0:1, :] * out_ref[...]
    last = cum[SPAN - 1 : SPAN, :]
    rising = jnp.where(flags[:, 3:4] > 0.5, jnp.exp(cum), 0.0)
    ending = jnp.where(flags[:, 4:5] > 0.5, jnp.exp(last - cum), 0.0)
    scores = dot(write, read, 1, 1)
    i = lax.broadcasted_iota(jnp.int32, (SPAN, SPAN), 0)
    j = lax.broadcasted_iota(jnp.int32, (SPAN, SPAN), 1)
    matched = (flags[:, 5:6] == row_ref[0]) & (i <= j)
    lane = lax.broadcasted_iota(jnp.int32, (SPAN, 128), 1)
    from_state = exact_left(write, leaving)
    grad_scaled = spread(ending) * from_state
    grad_scores = jnp.zeros((SPAN, SPAN), f32)
    rows_of = []
    cols_of = jnp.zeros((SPAN, 128), f32)
    for h in range(HERE):
        fade = jnp.exp(jnp.minimum(cum_t[h : h + 1, :] - cum[:, h : h + 1], 0.0))
        weights = jnp.where(matched, fade, 0.0)
        grad_scaled = grad_scaled + exact_right(weights * scores, head_mask(gy, h))
        part = dot(head_mask(inner, h), gy, 1, 1) * weights * dt[:, h : h + 1]
        grad_scores = grad_scores + part
        logs = part * scores
        rows_of.append(jnp.sum(logs, axis=0, keepdims=True))
        cols_of = cols_of + jnp.where(lane == h, jnp.sum(logs, axis=1, keepdims=True), 0.0)
    rows_of.append(jnp.zeros((128 - HERE, SPAN), f32))
    grad_cum = jnp.concatenate(rows_of, axis=0).T - cols_of
    high, low = split2(grad_scores)
    grad_write = dot(high, read) + dot(low, read)
    grad_read = dot(high, write, 0, 0) + dot(low, write, 0, 0)
    read_state = exact_left(read, entering)
    grad_read = grad_read + both_split(spread(rising) * gyf, entering, 1, 1)
    grad_write = grad_write + both_split(spread(ending * dt) * innerf, leaving, 1, 1)
    tail = head_sum(innerf * from_state) * dt * ending
    grad_cum = grad_cum + head_sum(gyf * read_state) * rising - tail
    crossing = jnp.sum(entering * leaving, axis=0, keepdims=True)
    crossing = head_sum(jnp.broadcast_to(crossing, (8, WIDE)))[0:1, :] * rising[SPAN - 1 : SPAN, :]
    end_term = jnp.sum(tail, axis=0, keepdims=True) + crossing
    row = lax.broadcasted_iota(jnp.int32, (SPAN, 128), 0)
    grad_cum = grad_cum + jnp.where(row == SPAN - 1, end_term, 0.0)
    grad_log = running((i <= j).astype(bf16), grad_cum)
    grad_steps = grad_log * rate_ref[...] + head_sum(innerf * grad_scaled)
    grad_step_raw = jnp.where(lane < HERE, grad_steps * pltpu.roll(dt, HEAD_DIM, 1), 0.0)
    gstep_ref[...] = grad_step_raw.T[0:8, :]
    grad_rate = jnp.where(lane < HERE, grad_log * dt, 0.0)
    hsum_ref[0:1, :] += jnp.sum(grad_step_raw, axis=0, keepdims=True)
    hsum_ref[1:2, :] += jnp.sum(grad_rate, axis=0, keepdims=True)
    grad_inner = spread(dt) * grad_scaled + skip_ref[...] * gyf
    slope = silu_slope(pre_ref[...])
    gpre_ref[...] = grad_inner * slope[:, :WIDE]
    gst_ref[...] = jnp.concatenate([grad_write, grad_read], axis=1) * slope[:, WIDE:]


def conv_back(gpre, flags, chan_ext, conv_ref, masked):
    rows = gpre.shape[0] - 8
    total = gpre[0:rows, :] * conv_ref[0:1, :]
    sums = [jnp.sum(gpre[0:rows, :] * chan_ext[8 : rows + 8, :], axis=0, keepdims=True)]
    for k in range(1, CONV):
        masked[...] = jnp.where(flags[:, k - 1 : k] > 0.5, gpre, 0.0)
        total = total + masked[k : rows + k, :] * conv_ref[k : k + 1, :]
        sums.append(jnp.sum(masked[0:rows, :] * chan_ext[8 - k : rows + 8 - k, :], axis=0, keepdims=True))
    sums.append(jnp.sum(gpre[0:rows, :], axis=0, keepdims=True))
    sums.append(jnp.zeros((3, gpre.shape[1]), f32))
    return total, jnp.concatenate(sums, axis=0)


def fifth_begin(gstate_ref, gog_ref, gskip_ref, hsum_ref, giw_ref, small_ref):
    giw_ref[...] = jnp.zeros_like(giw_ref)
    small_ref[...] = jnp.zeros_like(small_ref)
    small_ref[8:16, :] = gstate_ref[...]
    small_ref[16:17, :] = gog_ref[...]
    small_ref[17:18, :] = gskip_ref[...]
    small_ref[18:19, 0:128] = hsum_ref[0:1, :]
    small_ref[18:19, 128:256] = hsum_ref[1:2, :]


def fifth_product(gg_ref, ginner, wm_ref):
    return dot(gg_ref[...], wm_ref[:, :WIDE], 1, 1) + dot(ginner, wm_ref[:, WIDE:], 1, 1)


def fifth_kernel(
    span, gpre_ref, fl_ref, chan_ref, edge_ref, conv_ref, normed_ref,
    ginner_ref, giw_ref, small_ref,
    chan_ext, masked,
):
    start = pl.multiple_of(span * SPAN, SPAN)

    @pl.when(span == 0)
    def _():
        chan_ext[0:8, :] = edge_ref[:, :WIDE]

    @pl.when(span > 0)
    def _():
        chan_ext[0:8, :] = chan_ref[pl.ds(pl.multiple_of(start - 16, 16), 16), :WIDE].astype(f32)[8:16, :]

    chan_ext[8 : SPAN + 8, :] = chan_ref[pl.ds(start, SPAN), :WIDE].astype(f32)
    gpre = gpre_ref[pl.ds(start, SPAN + 8), :]
    total, sums = conv_back(gpre, fl_ref[pl.ds(start, SPAN + 8), :], chan_ext, conv_ref, masked)
    ginner = total.astype(bf16)
    small_ref[0:8, :] += sums
    ginner_ref[...] = ginner
    giw_ref[...] += dot(ginner, normed_ref[...], 0, 0)


def sixth_kernel(count, *refs):
    sixth_body(refs[:count], *refs[count:])


def sixth_body(
    parts, tails_ref, steps_ref, fl_ref, chan_ref, edge_ref, conv_ref, x_ref, ng_ref,
    gs_ref, gconv_ref, gw_ref,
    gext, chan_ext, masked,
):
    place = lax.axis_index("sub") * lax.axis_size("seq") + lax.axis_index("seq")
    start = pl.multiple_of(place * SPAN, SPAN)
    total = jnp.sum(parts[0][...].astype(f32), axis=0)
    for part in parts[1:]:
        total = total + part[...]
    gext[0:SPAN, :] = total
    gext[SPAN : SPAN + 8, :] = jnp.sum(tails_ref[...], axis=0)
    chan_ext[8 : SPAN + 8, :] = chan_ref[pl.ds(start, SPAN), WIDE:].astype(f32)

    @pl.when(place == 0)
    def _():
        chan_ext[0:8, :] = edge_ref[:, WIDE:]

    @pl.when(place > 0)
    def _():
        chan_ext[0:8, :] = chan_ref[pl.ds(pl.multiple_of(start - 16, 16), 16), WIDE:].astype(f32)[8:16, :]

    conv = conv_ref.at[:, WIDE:]
    total, sums = conv_back(gext[...], fl_ref[pl.ds(start, SPAN + 8), :], chan_ext, conv, masked)
    gconv_ref[...] = sums
    steps = jnp.concatenate([steps_ref[:, i, :] for i in range(HERE)] + [jnp.zeros((128 - HEADS, SPAN), f32)], axis=0)
    grads = jnp.concatenate([total, steps.T], axis=1).astype(bf16)
    gs_ref[...] = grads
    vals = x_ref[...].astype(f32)
    inv = lax.rsqrt(jnp.mean(vals * vals, axis=1, keepdims=True) + EPS_NORM)
    gw_ref[...] = dot((vals * inv * ng_ref[...]).astype(bf16), grads, 0, 0)


def seventh_kernel(skip, count, many, *refs):
    refs = refs[skip:]
    parts, mixes, rest = refs[:count], refs[count : count + many], refs[count + many :]
    gs_ref, ws_ref, x_ref, cot_ref, ng_ref, mixed_ref, gt_ref, gain_ref = rest

    def add_all(total, refs):
        for ref in refs:
            if len(ref.shape) == 2:
                total = total + ref[...].astype(f32)
            else:
                for i in range(ref.shape[0]):
                    total = total + ref[i].astype(f32)
        return total

    vals = x_ref[...].astype(f32)
    mixed_ref[...] = add_all(vals, mixes).astype(bf16)
    grad = add_all(dot(gs_ref[...], ws_ref[...], 1, 1), parts)
    inv = lax.rsqrt(jnp.mean(vals * vals, axis=1, keepdims=True) + EPS_NORM)
    unit = vals * inv
    s = grad * ng_ref[...]
    gt_ref[...] = cot_ref[...].astype(f32) + inv * (s - unit * jnp.mean(s * unit, axis=1, keepdims=True))
    row = jnp.sum(grad * unit, axis=0, keepdims=True)
    for i in range(D // 128):
        gain_ref[i : i + 1, :] = row[:, 128 * i : 128 * (i + 1)]


def adam_terms(weight, grad, first, second):
    first_new = BETA_ONE * first + (1.0 - BETA_ONE) * grad
    second_new = BETA_TWO * second + (1.0 - BETA_TWO) * grad * grad
    update = (
        first_new / (1.0 - BETA_ONE**STEP) / (jnp.sqrt(second_new / (1.0 - BETA_TWO**STEP)) + ADAM_EPS)
        + DECAY * weight
    )
    return (first_new, second_new, update)


def square_sum(x):
    return jnp.sum(jnp.sum(x * x, axis=1, keepdims=True), axis=0, keepdims=True)


def lamb_apply(weight, update, weight_sq, update_sq):
    return weight - RATE * (jnp.sqrt(weight_sq) / (jnp.sqrt(update_sq) + ADAM_EPS)) * update


def two_heads(ref, rows, i, pair):
    cols = slice(HEAD_DIM * i, HEAD_DIM * (i + 1))
    return jnp.concatenate([ref[2 * pair, rows, cols], ref[2 * pair + 1, rows, cols]], axis=1)


def from_planes(z, own, near, far):
    first = jnp.where(z > 0, near[0], far[0].astype(f32))
    third = jnp.where(z < 3, near[1], far[2].astype(f32))
    return own + first + far[1].astype(f32) + third


def adam_kernel(skip, count, *refs):
    adam_body(count, *refs[skip:])


def adam_body(count, gate_ref, inner_ref, shared_ref, gain_ref, wi_ref, mi_ref, vi_ref, wo_ref, mo_ref, vo_ref, *refs):
    outs, (mi_out, vi_out, ui_out, mo_out, vo_out, uo_out, sums_ref, grad) = refs[:count], refs[count:]
    for base, ref in ((0, gate_ref), (INNER, inner_ref)):
        for i in range(HERE):
            for pair in range(PLANE // 2):
                at = base + i * PLANE * HEAD_DIM + pair * 128
                grad[:, at : at + 128] = two_heads(ref, slice(None), i, pair)
    grad[:, 2 * INNER :] = jnp.sum(shared_ref[...], axis=0)[:, : STATES + HEADS]
    weight = wi_ref[...]
    mi_out[...], vi_out[...], update = adam_terms(weight, grad[...], mi_ref[...], vi_ref[...])
    ui_out[...] = update
    sums_ref[0:8, :] = gain_ref[...]
    sums_ref[8:16, :] = jnp.zeros((8, 128), f32)
    sums_ref[8:9, :] = jnp.broadcast_to(square_sum(weight), (1, 128))
    sums_ref[9:10, :] = jnp.broadcast_to(square_sum(update), (1, 128))
    if count > 1:
        z = lax.axis_index("grp")
        total = from_planes(z, outs[0][pl.ds(pl.multiple_of(z * HEAD_DIM, HEAD_DIM), HEAD_DIM), :], *outs[1:])
    else:
        total = outs[0][...]
    weight = wo_ref[...]
    mo_out[...], vo_out[...], update = adam_terms(weight, total, mo_ref[...], vo_ref[...])
    uo_out[...] = update
    sums_ref[10:11, :] = jnp.broadcast_to(square_sum(weight), (1, 128))
    sums_ref[11:12, :] = jnp.broadcast_to(square_sum(update), (1, 128))


def last_kernel(
    every_ref, small_ref, wi_ref, ui_ref, wo_ref, uo_ref,
    nw_ref, nm_ref, nv_ref, cw_ref, cm_ref, cv_ref, hw_ref, hm_ref, hv_ref, gw_ref, gm_ref, gv_ref,
    wi_out, wo_out, nm_out, nv_out, nw_out, cm_out, cv_out, cw_out, hm_out, hv_out, hw_out, gm_out, gv_out, gw_out,
    conv, gain,
):
    total = jnp.sum(every_ref[...], axis=0)
    wi_out[...] = lamb_apply(wi_ref[...], ui_ref[...], total[8:9, 0:1], total[9:10, 0:1])
    wo_out[...] = lamb_apply(wo_ref[...], uo_ref[...], total[10:11, 0:1], total[11:12, 0:1])

    def update(grad, weight_ref, first_ref, second_ref, first_out, second_out, weight_out):
        weight = weight_ref[...]
        first, second, step = adam_terms(weight, grad, first_ref[...], second_ref[...])
        first_out[...] = first
        second_out[...] = second
        weight_out[...] = lamb_apply(weight, step, square_sum(weight), square_sum(step))

    update(total[0:8], nw_ref, nm_ref, nv_ref, nm_out, nv_out, nw_out)
    for i in range(HERE):
        for pair in range(PLANE // 2):
            at = i * PLANE * HEAD_DIM + pair * 128
            conv[:, at : at + 128] = two_heads(small_ref, slice(0, 8), i, pair)
            gain[at // 128 : at // 128 + 1, :] = two_heads(small_ref, slice(16, 17), i, pair)
    conv[:, INNER:] = jnp.sum(small_ref[:, 8:16, :], axis=0)
    update(conv[0:5, :], cw_ref, cm_ref, cv_ref, cm_out, cv_out, cw_out)
    update(gain[...], gw_ref, gm_ref, gv_ref, gm_out, gv_out, gw_out)

    t = lax.broadcasted_iota(jnp.int32, (PLANE, 128), 0)
    lane = lax.broadcasted_iota(jnp.int32, (PLANE, 128), 1)

    def by_head(cols):
        row = jnp.zeros((PLANE, 128), f32)
        for i in range(HERE):
            row = row + jnp.where(lane == PLANE * i + t, cols[:, i : i + 1], 0.0)
        return jnp.sum(row, axis=0, keepdims=True)[:, :HEADS]

    steps = by_head(small_ref[:, 18, 0:128])
    rates = by_head(small_ref[:, 18, 128:256]) * -jnp.exp(hw_ref[1:2, :])
    skips = by_head(head_sum(small_ref[:, 17, :]))
    update(jnp.concatenate([steps, rates, skips], axis=0), hw_ref, hm_ref, hv_ref, hm_out, hv_out, hw_out)


def spec(block, index):
    return pl.BlockSpec(block, index)


def whole(*dims):
    return pl.BlockSpec(dims, lambda *_: (0,) * len(dims))


def shape(*dims, dtype=f32):
    return jax.ShapeDtypeStruct(dims, dtype)


ANY = pl.BlockSpec(memory_space=pl.ANY)
IN_VMEM = pl.BlockSpec(memory_space=pltpu.VMEM)
IN_HBM = pl.BlockSpec(memory_space=pltpu.HBM)
MIB = 1024 * 1024
VMEM_LIMIT = 60 * MIB
SMALL_LIMIT = 12 * MIB


def launch(kernel, name, steps, in_specs, ins, out_specs, outs, scratch=()):
    grid = {"grid": (steps,), "in_specs": list(in_specs), "out_specs": list(out_specs)} if steps else {}
    return pl.pallas_call(
        kernel,
        out_shape=list(outs),
        scratch_shapes=list(scratch),
        compiler_params=pltpu.CompilerParams(vmem_limit_bytes=VMEM_LIMIT),
        name=name,
        **grid,
    )(*ins)


class First:
    def __init__(self, spans, x, halo, gain, wm, ws, pick, conv, bias, rate, flags, doc_rows, skip, ahead):
        rows = spans * SPAN
        early = lambda s: jnp.minimum(s, spans - 1)
        late = lambda s: jnp.maximum(s - spans, 0)
        both = lambda s: jnp.where(s >= spans, s - spans, s)
        block = lambda cols, at=early: spec((SPAN, cols), lambda s: (at(s), 0))
        span3 = lambda a, b, at=early: spec((1, a, b), lambda s: (at(s), 0, 0))
        self.ins = [x, halo, gain, wm, ws, pick, conv, bias, rate, flags, doc_rows, skip, ahead]
        self.in_specs = [
            block(D), whole(16, D), whole(1, D), whole(D, MAIN), whole(D, SHARED), whole(128, 128), whole(8, LOCAL),
            whole(1, 128), whole(1, 128), block(8, both), span3(1, SPAN, late), whole(1, WIDE), whole(*ahead.shape),
        ]
        self.out_specs = [
            block(D), block(WIDE), block(LOCAL), block(LOCAL), block(LOCAL), block(128), block(128),
            span3(NSTATE, WIDE), span3(8, WIDE), whole(8, LOCAL), block(WIDE, late),
        ]
        self.outs = [
            shape(rows, D, dtype=bf16), shape(rows, WIDE, dtype=bf16), shape(rows, LOCAL, dtype=bf16), shape(rows, LOCAL),
            shape(rows, LOCAL, dtype=bf16), shape(rows, 128), shape(rows, 128),
            shape(spans, NSTATE, WIDE), shape(spans, 8, WIDE), shape(8, LOCAL), shape(rows, WIDE),
        ]
        self.scratch = [
            pltpu.VMEM((SPAN + 8, LOCAL), f32), pltpu.VMEM((NSTATE, WIDE), f32), pltpu.VMEM((8, WIDE), f32),
            pltpu.VMEM((PACK, WIDE), f32), pltpu.VMEM((spans, SPAN, LOCAL), bf16), pltpu.VMEM((spans, SPAN, 128), f32),
            pltpu.VMEM((spans, SPAN, 128), f32),
        ]


def first_steps(step, spans, ins, outs, scratch):
    @pl.when(step == 0)
    def _():
        first_begin(*ins[1:5], outs[9], *scratch[:3])

    @pl.when(step < spans)
    def _():
        first_phase(step, *ins[:10], *outs[:10], *scratch)

    @pl.when(step >= spans)
    def _():
        within_phase(step - spans, *ins[9:12], outs[10], *scratch[4:])


def first_plain(spans, *refs):
    ins, outs, end, scratch = refs[:13], refs[13:24], refs[24], refs[25:]
    step = pl.program_id(0)
    first_steps(step, spans, ins, outs, scratch)

    @pl.when(step == spans - 1)
    def _():
        end[...] = scratch[3][...]


class Second:
    def __init__(self, spans, act, cum, flags, held, pref, incoming, part, gate, cot, wo, gain):
        rows = spans * SPAN
        block = lambda cols: spec((SPAN, cols), lambda s: (s, 0))
        span3 = lambda a, b: spec((1, a, b), lambda s: (s, 0, 0))
        self.ins = [act, cum, flags, held, pref, incoming, part, gate, cot, wo, gain]
        self.in_specs = [
            spec((SPAN, NSTATE), lambda s: (s, (WIDE + NSTATE) // NSTATE)), block(128), block(8), span3(NSTATE, WIDE),
            span3(8, WIDE), whole(NSTATE, WIDE), block(WIDE), block(WIDE), block(D), whole(WIDE, D), whole(1, WIDE),
        ]
        self.out_specs = [block(WIDE), block(WIDE)]
        self.outs = [shape(rows, WIDE, dtype=bf16), shape(rows, WIDE)]
        self.scratch = []


class Third:
    def __init__(self, spans, y, gate, gno, sums, act, cum, flags, gain, cot, wo, normed):
        rows = spans * SPAN
        back = lambda s: jnp.maximum(spans - 1 - s, 0)
        after = lambda s: jnp.maximum(s - spans, 0)
        block = lambda cols: spec((SPAN, cols), lambda s: (back(s), 0))
        later = lambda cols: spec((SPAN, cols), lambda s: (after(s), 0))
        span3 = lambda a, b: spec((1, a, b), lambda s: (back(s), 0, 0))
        self.later = later
        self.ins = [y, gate, gno, sums, act, cum, flags, gain, cot, wo, normed]
        self.in_specs = [
            block(WIDE), block(WIDE), block(WIDE), spec((PLANE, pl.squeezed, 2, SPAN), lambda s: (0, back(s), 0, 0)),
            block(LOCAL), block(128), block(8), whole(1, WIDE), later(D), whole(WIDE, D), later(D),
        ]
        self.out_specs = [block(WIDE), block(WIDE), span3(NSTATE, WIDE), span3(8, WIDE), whole(1, WIDE), whole(1, WIDE),
                          whole(WIDE, D), whole(WIDE, D)]
        self.outs = [
            shape(rows, WIDE, dtype=bf16), shape(rows, WIDE, dtype=bf16), shape(spans, NSTATE, WIDE),
            shape(spans, 8, WIDE), shape(1, WIDE), shape(1, WIDE), shape(WIDE, D), shape(WIDE, D),
        ]
        keep = pltpu.VMEM((spans, SPAN, WIDE), bf16)
        self.scratch = [pltpu.VMEM((NSTATE, WIDE), f32), pltpu.VMEM((8, WIDE), f32), keep, keep]


def third_plain(spans, *refs):
    ins, (gy, gg, behind, suff, gog, gskip, gout, ggw, start, mix), scratch = refs[:11], refs[11:21], refs[21:]
    step = pl.program_id(0)

    @pl.when(step == 0)
    def _():
        third_begin(gog, gskip, gout, ggw, *scratch[:2])

    @pl.when(step < spans)
    def _():
        third_first(step, *ins[:8], gy, gg, behind, suff, start, gog, gskip, *scratch)

    @pl.when(step >= spans)
    def _():
        third_second(step - spans, step - spans, *ins[8:], mix, gout, ggw, *scratch[2:])


class Fourth:
    def __init__(
        self, spans, act, dt, cum, flags, doc_rows, held, pref, incoming, behind, suff, ends, after_us, gy, pre,
        skip, rate,
    ):
        rows = spans * SPAN
        groups = ends.shape[0]
        block = lambda cols: spec((SPAN, cols), lambda s: (s, 0))
        span3 = lambda a, b: spec((1, a, b), lambda s: (s, 0, 0))
        self.ins = [act, dt, cum, flags, doc_rows, held, pref, incoming, behind, suff, ends, after_us, gy, pre, skip, rate]
        self.in_specs = [
            block(LOCAL), block(128), block(128), block(8), span3(1, SPAN), span3(NSTATE, WIDE),
            span3(8, WIDE), whole(NSTATE, WIDE), span3(NSTATE, WIDE), span3(8, WIDE), whole(groups, PACK, WIDE),
            whole(groups, 1, WIDE), block(WIDE), block(LOCAL), whole(1, WIDE), whole(1, 128),
        ]
        self.out_specs = [block(WIDE), whole(8, 128)]
        self.outs = [shape(rows + 8, WIDE), shape(8, 128)]
        self.scratch = [pltpu.VMEM((NSTATE, WIDE), f32)]


def fourth_plain(*refs):
    ins, (gpre, hsum, gst, gstep), scratch = refs[:16], refs[16:20], refs[20:]
    fourth_kernel(pl.program_id(0), *ins, gpre, gst, gstep, hsum, *scratch)


class Fifth:
    def __init__(self, spans, gpre, flags, chan, edge, conv, normed, gstate, gog, gskip, hsum, ggate, wm):
        rows = spans * SPAN
        block = lambda cols: spec((SPAN, cols), lambda s: (s, 0))
        self.ins = [gpre, flags, chan, edge, conv, normed, gstate, gog, gskip, hsum, ggate, wm]
        self.in_specs = [
            whole(rows + 8, WIDE), whole(rows + 8, 8), whole(rows, LOCAL), whole(8, LOCAL), whole(8, WIDE),
            block(D), whole(8, STATES), whole(1, WIDE), whole(1, WIDE), whole(8, 128), block(WIDE), whole(D, MAIN),
        ]
        self.outs = []
        self.scratch = [pltpu.VMEM((SPAN + 8, WIDE), f32)] * 2


def fifth_plain(spans, *refs):
    step = pl.program_id(0)
    ins, (gp, giw, small), (*scratch, ginner) = refs[:12], refs[12:15], refs[15:]

    @pl.when(step == 0)
    def _():
        fifth_begin(*ins[6:10], giw, small)

    fifth_kernel(step, *ins[:6], ginner, giw, small, *scratch)
    gp[...] = fifth_product(ins[10], ginner[...], ins[11])


def run_sixth(parts, tails, steps, flags, chan, edge, conv, x, gain):
    ins = [*parts, tails, steps, flags, chan, edge, conv, x, gain]
    return pl.pallas_call(
        functools.partial(sixth_kernel, len(parts)),
        in_specs=[IN_VMEM] * len(ins),
        out_shape=[shape(SPAN, SHARED, dtype=bf16), shape(8, STATES), shape(D, SHARED)],
        scratch_shapes=[pltpu.VMEM((SPAN + 8, STATES), f32)] * 3,
        compiler_params=pltpu.CompilerParams(vmem_limit_bytes=SMALL_LIMIT),
        name="conv_back_state",
    )(*ins)


def run_seventh(parts, mixes, gs, ws, x, cot, gain):
    ins = [*parts, *mixes, gs, ws, x, cot, gain]
    return pl.pallas_call(
        functools.partial(seventh_kernel, 0, len(parts), len(mixes)),
        in_specs=[IN_VMEM] * len(ins),
        out_shape=[shape(SPAN, D, dtype=bf16), shape(SPAN, D), shape(D // 128, 128)],
        compiler_params=pltpu.CompilerParams(vmem_limit_bytes=SMALL_LIMIT),
        name="token_gradient",
    )(*ins)


def run_adam(gate, inner, shared, gain, wi, mi, vi, wo, mo, vo, grads_out, spare):
    like = lambda a: shape(*a.shape)
    ins = [*spare, gate, inner, shared, gain, wi, mi, vi, wo, mo, vo, *grads_out]
    return pl.pallas_call(
        functools.partial(adam_kernel, len(spare), len(grads_out)),
        in_specs=[IN_VMEM] * len(ins),
        out_shape=[like(wi), like(wi), like(wi), like(wo), like(wo), like(wo), shape(16, 128)],
        scratch_shapes=[pltpu.VMEM(wi.shape, f32)],
        compiler_params=pltpu.CompilerParams(vmem_limit_bytes=SMALL_LIMIT),
        name="adam_terms",
    )(*ins)


def run_prep(groups, at, conv, head, gain):
    return pl.pallas_call(
        prep_kernel,
        in_specs=[pl.BlockSpec(memory_space=pltpu.SMEM)] + [pl.BlockSpec(memory_space=pltpu.VMEM)] * 3,
        out_shape=[shape(8, LOCAL), shape(1, 128), shape(1, 128), shape(1, WIDE), shape(1, WIDE),
                   shape(128, 128, dtype=bf16), shape(groups, 1, WIDE), shape(groups, 1, WIDE)],
        compiler_params=pltpu.CompilerParams(vmem_limit_bytes=VMEM_LIMIT),
        name="prepare",
    )(at, conv, head, gain)


def run_last(every, small, big, params):
    like = lambda a: shape(*a.shape)
    outs = [like(big[0]), like(big[2])]
    for weight in params[::3]:
        outs += [like(weight)] * 3
    return pl.pallas_call(
        last_kernel,
        out_shape=outs,
        scratch_shapes=[pltpu.VMEM((8, INNER + STATES), f32), pltpu.VMEM((INNER // 128, 128), f32)],
        compiler_params=pltpu.CompilerParams(vmem_limit_bytes=SMALL_LIMIT),
        name="lamb_apply",
    )(every, small, *big, *params)


MESH = pl.DeviceIdType.MESH


def bits(place):
    x = jnp.where(place >= 4, 1, 0)
    rest = place - 4 * x
    c = jnp.where(rest >= 2, 1, 0)
    return x, c, rest - 2 * c


class Here:
    def __init__(self):
        self.z = lax.axis_index("grp")
        self.sub = lax.axis_index("sub")
        self.y = lax.axis_index("seq")
        self.x = jnp.where(self.sub >= 2, 1, 0)
        self.c = self.sub - 2 * self.x
        self.t = self.sub * 2 + self.y

    def mate(self, o, up=0):
        x = 1 - self.x if o & 4 else self.x
        c = 1 - self.c if o & 2 else self.c
        y = 1 - self.y if o & 1 else self.y
        sub = x * 2 + c
        return (self.onward(up), sub, y), sub * 2 + y

    def onward(self, up):
        z = self.z + up
        return jnp.where(z >= 4, z - 4, z) if up else self.z

    def plane(self, up):
        return (self.onward(up), self.sub, self.y), self.onward(up)


CHIPS = (5, 4, 1)
CORE = 2


def near(h):
    return [h.mate(o)[0] for o in range(1, 8)]


def same_core(h):
    return [h.mate(o)[0] for o in CHIPS]


def line(h):
    return [h.plane(up)[0] for up in range(1, 4)]


def call(devices):
    barrier = pltpu.get_barrier_semaphore()
    for device in devices:
        pl.semaphore_signal(barrier, inc=1, device_id=device, device_id_type=MESH)
    return barrier


def greet(devices):
    pl.semaphore_wait(call(devices), len(devices))


def rows_at(ref, at, size):
    return ref.at[pl.ds(pl.multiple_of(at * size, size), size)]


class Wires:
    def __init__(self, send, recv, local, started=False):
        self.send_sem, self.recv_sem, self.local_sem = send, recv, local
        self.sent, self.kept, self.started = [], [], started

    def make(self, src, dst, i, device, j=None):
        return pltpu.make_async_remote_copy(
            src_ref=src, dst_ref=dst, send_sem=self.send_sem.at[i], recv_sem=self.recv_sem.at[i if j is None else j],
            device_id=device, device_id_type=MESH,
        )

    def send(self, src, dst, i, device):
        copy = self.make(src, dst, i, device)
        if not self.started:
            copy.start()
        self.sent.append(copy)

    def arrived(self, dst, i, device):
        self.make(dst, dst, i, device).wait_recv()

    def keep(self, src, dst):
        copy = pltpu.make_async_copy(src, dst, self.local_sem.at[len(self.kept)])
        if not self.started:
            copy.start()
        self.kept.append(copy)
        return copy

    def finish(self):
        for copy in self.sent:
            copy.wait_send()


def wires(copies, kept):
    return [pltpu.SemaphoreType.DMA((copies,)), pltpu.SemaphoreType.DMA((copies,)), pltpu.SemaphoreType.DMA((kept,))]


def talk(kernel, number, name, outs, ins, scratch):
    return pl.pallas_call(
        kernel,
        in_specs=[IN_VMEM] * len(ins),
        out_specs=[IN_VMEM] * len(outs),
        out_shape=outs,
        scratch_shapes=scratch,
        compiler_params=pltpu.CompilerParams(collective_id=number, has_side_effects=True, vmem_limit_bytes=SMALL_LIMIT),
        name=name,
    )(*ins)


class Relay:
    def __init__(self, h, w, base, block):
        self.h, self.w, self.base, self.block = h, w, base, block

    def copies(self, hop):
        h = self.h
        above, below = h.plane(1)[0], h.plane(3)[0]
        up = self.w.make, jnp.maximum(h.z - hop + 1, 0), self.base + hop, above
        down = self.w.make, jnp.minimum(h.z + hop - 1, 3), self.base + 4 + hop, below
        yield (h.z < 3) & (h.z >= hop - 1), up, h.z >= hop, jnp.maximum(h.z - hop, 0), below
        yield (h.z > 0) & (h.z <= 4 - hop), down, h.z <= 3 - hop, jnp.minimum(h.z + hop, 3), above

    def first(self):
        for sends, (make, z, i, device), *_ in self.copies(1):

            @pl.when(sends)
            def _():
                make(self.block(z), self.block(z), i, device).start()

    def onward(self, hop):
        for _, (_, _, i, _), comes, z, device in self.copies(hop):

            @pl.when(comes)
            def _():
                self.w.arrived(self.block(z), i, device)

        if hop < 3:
            for sends, (make, z, i, device), *_ in self.copies(hop + 1):

                @pl.when(sends)
                def _():
                    make(self.block(z), self.block(z), i, device).start()

    def finish(self):
        for hop in range(1, 4):
            for sends, (make, z, i, device), *_ in self.copies(hop):

                @pl.when(sends)
                def _():
                    make(self.block(z), self.block(z), i, device).wait_send()


def start_kernel(wi_in, wo_in, tok, docs_in, conv_in, head_in, gain_in, norm_in, *refs):
    (wm, ws, x, halo), outputs, (flags, doc_rows, out_low, norm), refs = refs[:4], refs[4:12], refs[12:16], refs[16:]
    (wi, wo, docs, conv, head, gain, main, shared), sems = refs[:8], refs[8:]
    h = Here()
    w = Wires(*sems)
    near_x, near_y, mate = [h.mate(o)[0] for o in (4, 1, CORE)]
    friends = near(h) + line(h)
    barrier = call(friends)
    loads = [w.keep(wi_in, wi), w.keep(wo_in, wo)]
    loads += [w.keep(*pair) for pair in ((docs_in, docs), (conv_in, conv), (head_in, head), (gain_in, gain), (norm_in, norm))]
    own = w.keep(tok, rows_at(x, h.t, SPAN))
    loads[0].wait()
    loads[1].wait()
    pack_kernel(wi, wo, main, shared, out_low)
    pl.semaphore_wait(barrier, len(friends))

    in_rows = lambda place: wm.at[pl.ds(pl.multiple_of(h.z * SPAN + place * 32, 32), 32)]
    keep = [w.keep(main.at[h.t], in_rows(h.t)), w.keep(shared, ws.at[h.z, h.t])]
    for o in range(1, 8):
        device, place = h.mate(o)
        w.send(main.at[place], in_rows(h.t), o, device)
    for up in range(1, 4):
        w.send(shared, ws.at[h.z, h.t], 10 + up, h.plane(up)[0])
    block = lambda o: rows_at(x, h.mate(o)[1], SPAN)
    w.send(tok, block(0), 21, near_x)
    w.send(tok, block(0), 22, near_y)
    w.send(tok, block(0), 23, mate)
    for copy in loads[2:]:
        copy.wait()
    prepare(h.z, h.t, conv, head, gain, *outputs)
    flags_of(h.z, docs, flags, doc_rows)
    keep[0].wait()
    for o in range(1, 8):
        device, place = h.mate(o)
        w.arrived(in_rows(place), o, device)
    relay = Relay(h, w, 30, lambda z: rows_at(wm, z, SPAN))
    relay.first()
    keep[1].wait()
    for up in range(1, 4):
        device, z = h.plane(4 - up)
        w.arrived(ws.at[z, h.t], 10 + up, device)
    for i, o in enumerate(CHIPS):
        w.send(ws.at[:, h.t], ws.at[:, h.t], 40 + i, h.mate(o)[0])
    w.send(ws.at[:, h.t], ws.at[:, h.t], 43, mate)
    half = SPAN // 2
    upper, lower = pl.ds(0, half), pl.ds(half, half)
    relay.onward(1)
    w.arrived(block(4), 21, near_x)
    w.send(block(4).at[upper], block(4).at[upper], 20, near_y)
    w.send(block(4), block(4), 25, mate)
    w.arrived(block(1), 22, near_y)
    w.send(block(1).at[lower], block(1).at[lower], 27, near_x)
    w.send(block(1), block(1), 26, mate)
    for i, o in enumerate(CHIPS):
        device, place = h.mate(o)
        w.arrived(ws.at[:, place], 40 + i, device)
        w.send(ws.at[:, place], ws.at[:, place], 44 + i, mate)
    relay.onward(2)
    w.arrived(block(5).at[upper], 20, near_y)
    w.arrived(block(5).at[lower], 27, near_x)
    w.send(block(5), block(5), 24, mate)
    own.wait()
    w.arrived(block(CORE), 23, mate)
    w.arrived(ws.at[:, h.mate(CORE)[1]], 43, mate)
    for i, o in enumerate(CHIPS):
        w.arrived(block(o ^ CORE), 24 + i, mate)
    w.send(x.at[pl.ds(PLANE * SPAN - 16, 16)], halo, 50, h.plane(1)[0])
    for i, o in enumerate(CHIPS):
        w.arrived(ws.at[:, h.mate(o ^ CORE)[1]], 44 + i, mate)
    relay.onward(3)
    relay.finish()
    w.arrived(halo, 50, h.plane(3)[0])
    w.finish()


class Chain:
    def __init__(self, h, w, ends, low, lows, reverse):
        self.h, self.w, self.ends, self.low, self.lows = h, w, ends, low, lows
        self.hops = []
        for up in range(1, 4):
            ahead = 4 - up if reverse else up
            goes = h.z >= up if reverse else h.z < 4 - up
            comes = h.z < 4 - up if reverse else h.z >= up
            self.hops.append((up, goes, h.plane(ahead)[0], comes, *h.plane(4 - ahead)))

    def copy(self, up, device):
        z = self.h.z
        if up == 1:
            return self.w.make(self.ends.at[z], self.ends.at[z], up, device)
        return self.w.make(self.low, self.lows.at[z], up, device)

    def start(self):
        self.low[...] = self.ends[self.h.z].astype(bf16)
        for up, goes, device, *_ in self.hops:

            @pl.when(goes)
            def _():
                self.copy(up, device).start()

    def wait(self):
        for up, goes, device, comes, back, z in self.hops:

            @pl.when(comes)
            def _():
                self.w.arrived((self.lows if up > 1 else self.ends).at[z], up, back)
                if up > 1:
                    self.ends[z] = self.lows[z].astype(f32)

            @pl.when(goes)
            def _():
                self.copy(up, device).wait_send()


def first_direct(work, *refs):
    ins, (out, cot), refs = refs[:13], refs[13:15], refs[15:]
    outs, (inc, g, wo), refs = refs[:11], refs[11:14], refs[14:]
    (ext, state, decay, ends, low, lows), sems = refs[:6], refs[6:]
    h = Here()
    w = Wires(*sems)
    local = sems[2]
    mate, _ = h.mate(CORE)
    end = ends.at[h.z]
    spans = PLANE
    rows_of = [Rows(outs[i]) for i in (4, 5, 6)]

    greet(line(h) + same_core(h) + [mate])
    rows = [w.make(out, rows_at(wo, h.z, HEAD_DIM), 8 + up, h.plane(up)[0]) for up in range(1, 4)]
    block = lambda o: rows_at(g, h.mate(o)[1], SPAN)
    across = [w.make(cot, block(0), 4 + i, h.mate(o)[0]) for i, o in enumerate(CHIPS)]
    for copy in (*rows, *across):
        copy.start()
    loads = [pltpu.make_async_copy(cot, block(0), local.at[0]),
             pltpu.make_async_copy(out, rows_at(wo, h.z, HEAD_DIM), local.at[1])]
    for copy in loads:
        copy.start()
    first_begin(*ins[1:5], outs[9], ext, state, decay)

    @pl.loop(0, spans, unroll=2)
    def _(step):
        taken = views(work.in_specs[:10], ins, step)
        given = views(work.out_specs[:10], outs, step)
        first_phase(step, *taken, *given, ext, state, decay, end, *rows_of)

    chain = Chain(h, w, ends, low, lows, False)
    chain.start()
    over = [w.make(block(o), block(o), 12 + i, mate) for i, o in enumerate((*CHIPS, 0))]

    def within(span):
        taken = views(work.in_specs[9:12], ins[9:12], span + spans)
        within_phase(span, *taken, view(work.out_specs[10], outs[10], span + spans), *rows_of)

    pl.loop(0, spans // 2, unroll=2)(within)
    loads[0].wait()
    over[3].start()
    for i, o in enumerate(CHIPS):
        across[i].wait_send()
        w.arrived(block(o), 4 + i, h.mate(o)[0])
        over[i].start()
    pl.loop(spans // 2, spans, unroll=2)(within)
    for i, o in enumerate((*CHIPS, 0)):
        over[i].wait_send()
        w.arrived(block(o ^ CORE), 12 + i, mate)
    for up in range(1, 4):
        rows[up - 1].wait_send()
        w.arrived(rows_at(wo, h.onward(4 - up), HEAD_DIM), 8 + up, h.plane(4 - up)[0])
    loads[1].wait()
    chain.wait()
    carry_chain(ends, ins[12], inc, False)


def turn(step):
    h = Here()
    a, b, e = bits(7 - step)
    x, c, y = h.x + a - 2 * h.x * a, h.c + e - 2 * h.c * e, h.y + b - 2 * h.y * b
    return x * 4 + c * 2 + y


class Across:
    def __init__(self, h, w, base, block, upper, lower):
        self.w, self.base, self.block, self.upper, self.lower = w, base, block, upper, lower
        self.near_x, self.near_y = h.mate(4)[0], h.mate(1)[0]

    def copies(self):
        half = SPAN // 2
        return (
            self.w.make(self.block.at[0:half], self.upper, self.base, self.near_x),
            self.w.make(self.block.at[half:SPAN], self.lower, self.base + 1, self.near_y),
        )

    def start(self):
        for copy in self.copies():
            copy.start()

    def extra(self, i):
        if i == 1:
            self.w.arrived(self.lower, self.base + 1, self.near_y)
            return 1, self.lower
        self.w.arrived(self.upper, self.base, self.near_x)
        return 0, self.upper

    def last(self):
        for copy in self.copies():
            copy.wait_send()


class Fold:
    def __init__(self, h, w, base, blocks, inbox, outbox, total, across, deliver=None):
        self.h, self.w, self.base, self.deliver = h, w, base, deliver
        self.blocks, self.inbox, self.outbox, self.total, self.across = blocks, inbox, outbox, total, across
        self.mate, _ = h.mate(CORE)
        self.slots = blocks.shape[0]

    def sent(self, i):
        self.w.make(self.inbox.at[i], self.inbox.at[i], self.base + i, self.mate).wait_send()

    def slot(self, step):
        for i in (2, 3):

            @pl.when(step == 2 * i)
            def _():
                self.sent(i - 2)

        return jnp.where(step >= 4, step - 4, step) if self.slots == 4 else step

    def each(self, get, put, extra=None):
        for half in range(2):

            @pl.loop(0, SPAN // 2, step=32)
            def _(row):
                rows = pl.ds(pl.multiple_of(row + half * (SPAN // 2), 32), 32)
                value = get(rows)
                if extra is not None and extra[0] == half:
                    value = value + extra[1][pl.ds(pl.multiple_of(row, 32), 32), :].astype(f32)
                put(rows, value)

    def add(self, pair, put, extra=None):
        slot = (2 * pair + 1) % self.slots
        self.each(lambda rows: self.blocks[slot, rows, :] + self.inbox[pair, rows, :], put, extra)

    def settle(self, i):
        self.w.arrived(self.inbox.at[i], self.base + i, self.mate)
        if i == 0:
            self.add(0, put_in(self.across.block))
            self.across.start()
        elif self.outbox is None:
            self.add(i, put_in(self.inbox, i))
        else:
            self.add(i, put_in(self.outbox, i - 1), self.across.extra(i))
            self.deliver(i - 1)

    def collect(self, held):
        for i in (1, 2):
            self.each(lambda rows: self.inbox[i, rows, :], put_in(held, i - 1), self.across.extra(i))

    def step(self, step, early=0):
        for i in range(4):

            @pl.when(step == 2 * i)
            def _():
                self.w.make(self.blocks.at[2 * i % self.slots], self.inbox.at[i], self.base + i, self.mate).start()
                if i > early:
                    self.settle(i - 1)

    def last(self):
        self.w.arrived(self.inbox.at[3], self.base + 3, self.mate)
        self.add(3, put_in(self.total))
        self.sent(2)
        self.sent(3)
        self.across.last()


class ToChips:
    def __init__(self, h, w, base, outbox, results):
        self.copies = [w.make(outbox.at[i], results.at[i], base + i, h.mate(o)[0]) for i, o in enumerate(CHIPS[1:])]

    def __call__(self, i):
        self.copies[i].start()

    def last(self):
        for copy in self.copies:
            copy.wait()


def head_rows(ref, z):
    return rows_at(ref, z, HEAD_DIM)


def lanes_at(ref, z):
    return ref.at[:, pl.ds(pl.multiple_of(z * SPAN, SPAN), SPAN)]


class Planes:
    def __init__(self, h, w, base, full, low, piece, near, far):
        self.copies = []
        for up in range(1, 4):
            device, z = h.plane(up)
            wide = near is not None and functools.partial(w.make, piece(full, z), near.at[up // 2], base + up, device)
            slim = functools.partial(w.make, piece(low, z), far.at[up - 1], base + up, device)
            to_near = {1: h.z < 3, 2: None, 3: h.z > 0}[up] if near is not None else None
            from_near = {1: h.z > 0, 2: None, 3: h.z < 3}[up] if near is not None else None
            self.copies.append((wide, slim, to_near, from_near))

    def each(self, near, act_wide, act_slim):
        if near is None:
            act_slim()
            return

        @pl.when(near)
        def _():
            act_wide()

        @pl.when(jnp.logical_not(near))
        def _():
            act_slim()

    def start(self):
        for wide, slim, to_near, _ in self.copies:
            self.each(to_near, lambda: wide().start(), lambda: slim().start())

    def wait(self):
        for wide, slim, to_near, from_near in self.copies:
            self.each(to_near, lambda: wide().wait_send(), lambda: slim().wait_send())
            self.each(from_near, lambda: wide().wait_recv(), lambda: slim().wait_recv())


def put_in(ref, *at):
    def put(rows, value):
        ref[(*at, rows, slice(None))] = value.astype(ref.dtype)

    return put


def third_direct(work, *refs):
    second, third = work.second, work
    ins, normed, refs = refs[:11], refs[11], refs[12:]
    (gy, gg, behind, suff, gog, gskip, gout, ggw), (ends, chip, held) = refs[:8], refs[8:11]
    (blocks, inbox, state, decay, no_all, every, low, lows), sems = refs[11:19], refs[19:]
    act, cum, flags, _, _, _, _, gate, cot, wo, gain = ins
    h = Here()
    w = Wires(*sems)
    spans = PLANE
    start = ends.at[h.z]
    gates = Rows(gg)

    def gno(span):
        late = jnp.where(span >= 4, 1, 0)
        return blocks.at[span - 4 * late, :, pl.ds(pl.multiple_of(late * WIDE, WIDE), WIDE)]

    greet(near(h) + line(h))
    mine = every.at[h.t]
    third_begin(gog, gskip, gout, ggw, state, decay)

    @pl.loop(0, spans, unroll=2)
    def _(step):
        taken = views(second.in_specs, ins, step)
        second_kernel(*taken, view(second.out_specs[0], gy, step), gno(step), mine.at[pl.ds(step, 1)])

    for o in range(1, 8):
        w.send(mine, every.at[h.t], 10 + o, h.mate(o)[0])
    for o in range(1, 8):
        device, place = h.mate(o)
        w.arrived(every.at[place], 10 + o, device)

    taking = (gy, gate, None, every, act, cum, flags, gain, cot, wo, normed)

    @pl.loop(0, spans, unroll=2)
    def _(step):
        taken = [gno(spans - 1 - step) if i == 2 else view(third.in_specs[i], taking[i], step) for i in range(8)]
        one, two, three, four = views(third.out_specs[:4], (gy, gg, behind, suff), step)
        third_first(step, *taken, one, two, three, four, start, gog, gskip, state, decay, no_all, gates)

    chain = Chain(h, w, ends, low, lows, True)
    chain.start()
    half = SPAN // 2
    across = Across(h, w, 8, held.at[0], held.at[1, 0:half], held.at[1, half:SPAN])
    fold = Fold(h, w, 4, blocks, inbox, None, chip, across)

    @pl.loop(0, spans)
    def _(span):
        taken = views(third.in_specs[8:], taking[8:], span + spans)
        third_second(span, turn(span), *taken, blocks.at[fold.slot(span)], gout, ggw, no_all, gates)
        fold.step(span)

    fold.last()
    chain.wait()
    fold.collect(held)
    w.finish()


def fourth_direct(work, *refs):
    ins, (held, ggw), refs = refs[:16], refs[16:18], refs[18:]
    (gpre, hsum), (rmix, near_gate, far_gate) = refs[:2], refs[2:5]
    (parts, total, tails, steps), refs = refs[5:9], refs[9:]
    (out, blocks, inbox, outbox, gstep, edge, cross, upper, lower, ggw_low), sems = refs[:10], refs[10:]
    h = Here()
    w = Wires(*sems)
    local = sems[2]
    spans = PLANE
    below = h.plane(3)[0]
    corner = (h.onward(3), 3, 1)
    after = gpre.at[pl.ds(PLANE * SPAN, 8)]
    gate_planes = Planes(h, w, 32, ggw, ggw_low, lanes_at, near_gate, far_gate)

    def to_place(src, dst, base, keep, place):
        @pl.when(place != h.t)
        def _():
            x, c, y = bits(place)
            device = (h.z, 2 * x + c, y)
            w.make(src, dst, base + place, device, base + h.t).start()

        @pl.when(place == h.t)
        def _():
            pltpu.make_async_copy(src, dst, local.at[keep]).start()

    friends = near(h) + line(h)
    barrier = call(friends)

    @pl.when(h.t == 7)
    def _():
        call([h.mate(o, 1)[0] for o in range(8)])

    ggw_low[...] = ggw[...].astype(bf16)
    pl.semaphore_wait(barrier, len(friends) + 1)
    gate_planes.start()
    branch = [w.make(held.at[i], rmix.at[i], 12 + i, h.mate(o)[0]) for i, o in enumerate(CHIPS[1:])]
    for copy in branch:
        copy.start()
    chips = ToChips(h, w, 8, outbox, parts)
    fold = Fold(h, w, 4, blocks, inbox, outbox, total, Across(h, w, 10, cross, upper, lower), chips)

    @pl.loop(0, spans)
    def _(step):
        place = turn(step)
        taken = views(work.in_specs, ins, place)
        mine = view(work.out_specs[0], gpre, place)
        fourth_kernel(step, *taken, mine, blocks.at[fold.slot(step)], gstep.at[step], hsum, out)
        fold.step(step)
        to_place(gstep.at[step], steps.at[h.t], 16, 1, place)

        @pl.when(place == 0)
        def _():
            edge[...] = mine[0:8, :]
            w.make(edge, after, 14, below).start()
            w.make(blocks.at[step, 0:8], tails.at[h.t], 31, corner, 24 + h.t).start()

        @pl.when(place > 0)
        def _():
            to_place(blocks.at[step, 0:8], tails.at[h.t], 24, 2, place - 1)

    fold.last()
    gate_planes.wait()
    for copy in branch:
        copy.wait()
    w.make(edge, after, 14, below).wait()
    rows = blocks.at[0, 0:8]
    for place in range(PLANE):
        device = (h.z, place // 2, place % 2)

        @pl.when(place != h.t)
        def _():
            w.make(gstep.at[0], steps.at[place], 16 + place, device).wait()

        @pl.when((place != h.t) | (h.t == 7))
        def _():
            w.arrived(tails.at[place], 24 + place, device)

        @pl.when((place != h.t) | (place == 7))
        def _():
            w.make(rows, tails.at[place], 24 + place, device).wait_send()

    pltpu.make_async_copy(gstep.at[0], steps.at[h.t], local.at[1]).wait()

    @pl.when(h.t < 7)
    def _():
        pltpu.make_async_copy(rows, tails.at[h.t], local.at[2]).wait()

    chips.last()


def fifth_direct(work, *refs):
    ins, (ggw, near_gate, far_gate, gstate, gout), rest, refs = refs[:12], refs[12:17], refs[17:24], refs[24:]
    (pgate, pinner, ps, psmall, near_out, far_out, mixed, gtok, gain), refs = refs[:9], refs[9:]
    (blocks, inbox, outbox, rgp, chip), scratch, (ginner, giw, giw_low, small) = refs[:5], refs[5:7], refs[7:11]
    (far_inner, zsum, gatesum, state_in, state_low, state_got), refs = refs[11:17], refs[17:]
    (ssum, rsmall, smallsum, cross, upper, lower, gout_low), sems = refs[:7], refs[7:]
    h = Here()
    w = Wires(*sems)
    local = sems[2]
    spans = PLANE
    mate, _ = h.mate(CORE)

    friends = near(h) + line(h)
    barrier = call(friends)
    lanes = pl.ds(pl.multiple_of(h.z * SPAN, SPAN), SPAN)
    gatesum[...] = from_planes(h.z, ggw[:, lanes], near_gate, far_gate).T
    gout_low[...] = gout[...].astype(bf16)
    pl.semaphore_wait(barrier, len(friends))
    out_planes = Planes(h, w, 0, gout, gout_low, head_rows, near_out, far_out)
    out_planes.start()
    state = []
    for i, o in enumerate((*CHIPS, 0)):
        near_core = w.make(gstate.at[:, h.mate(o ^ CORE)[1]], state_in.at[i], 24 + i, mate)
        on = w.make(state_low.at[i], state_got.at[i], 28 + i, h.mate(o)[0]) if o else None
        state.append((near_core, on))
        near_core.start()
    for o in range(1, 8):
        device, place = h.mate(o)
        w.send(rows_at(gatesum, place, 32), pgate.at[h.t], 44 + o, device)
    keep = [w.keep(rows_at(gatesum, h.t, 32), pgate.at[h.t])]
    chips = ToChips(h, w, 8, outbox, rgp)
    fold = Fold(h, w, 4, blocks, inbox, outbox, chip, Across(h, w, 10, cross, upper, lower), chips)

    def conv_step(step):
        place = turn(step)
        taken = views(work.in_specs[:6], ins, place)
        fifth_kernel(place, *taken, ginner.at[step], giw, small, *scratch)

    def block_step(step):
        taken = views(work.in_specs[10:], ins[10:], turn(step))
        blocks[fold.slot(step)] = fifth_product(taken[0], ginner[step], taken[1])
        fold.step(step, early=1)

    fifth_begin(*ins[6:10], giw, small)

    @pl.loop(0, 2)
    def _(step):
        conv_step(step)
        block_step(step)

    for i, (o, (near_core, on)) in enumerate(zip((*CHIPS, 0), state)):
        near_core.wait()
        both = gstate[:, h.mate(o)[1]] + state_in[i]
        if on is None:
            ssum[...] = both
        else:
            state_low[i] = both.astype(bf16)
            on.start()

    @pl.loop(2, spans)
    def _(step):
        conv_step(step)

        @pl.when(step == 3)
        def _():
            fold.settle(0)

    giw_low[...] = giw[...].astype(bf16)
    inner_planes = Planes(h, w, 16, giw, giw_low, lanes_at, None, far_inner)
    inner_planes.start()
    for up in range(1, 4):
        w.send(small, rsmall.at[h.z], 20 + up, h.plane(up)[0])
    keep_small = w.keep(small, rsmall.at[h.z])
    pl.loop(2, spans)(block_step)
    fold.last()

    for _, on in state[:3]:
        on.wait()
    ssum[...] = ssum[...] + jnp.sum(state_got[...].astype(f32), axis=0)
    for up in range(1, 4):
        device, z = h.plane(up)
        w.send(ssum.at[z], ps.at[h.z], 32 + up, device)
    keep.append(w.keep(ssum.at[h.z], ps.at[h.z]))

    keep_small.wait()
    for up in range(1, 4):
        device, z = h.plane(4 - up)
        w.arrived(rsmall.at[z], 20 + up, device)
    smallsum[...] = jnp.sum(rsmall[...], axis=0)
    for i, o in enumerate((*CHIPS, CORE)):
        w.send(smallsum, psmall.at[h.t], 36 + i, h.mate(o)[0])
    keep.append(w.keep(smallsum, psmall.at[h.t]))

    inner_planes.wait()
    zsum[...] = (giw[:, lanes] + jnp.sum(far_inner[...].astype(f32), axis=0)).T
    for o in range(1, 8):
        device, place = h.mate(o)
        w.send(rows_at(zsum, place, 32), pinner.at[h.t], 52 + o, device)
    keep.append(w.keep(rows_at(zsum, h.t, 32), pinner.at[h.t]))
    chips.last()
    seventh_kernel(0, 2, 2, chip, rgp, *rest, mixed, gtok, gain)

    for i, o in enumerate(CHIPS):
        device, place = h.mate(o)
        w.arrived(psmall.at[place], 36 + i, device)
        w.send(psmall.at[place], psmall.at[place], 40 + i, mate)
    w.arrived(psmall.at[h.mate(CORE)[1]], 39, mate)
    for i, o in enumerate(CHIPS):
        w.arrived(psmall.at[h.mate(o ^ CORE)[1]], 40 + i, mate)
    for o in range(1, 8):
        device, place = h.mate(o)
        w.arrived(pgate.at[place], 44 + o, device)
        w.arrived(pinner.at[place], 52 + o, device)
    for up in range(1, 4):
        device, z = h.plane(4 - up)
        w.arrived(ps.at[z], 32 + up, device)
    out_planes.wait()
    for copy in keep:
        copy.wait()
    w.finish()


def view(block, ref, step):
    if block.block_shape is None:
        return ref
    cuts, full = [], True
    for at, size, total in zip(block.index_map(step), block.block_shape, ref.shape):
        if size is pl.squeezed:
            cuts.append(at)
        elif size == total:
            cuts.append(slice(None))
            continue
        else:
            cuts.append(pl.ds(at * size if isinstance(at, int) else pl.multiple_of(at * size, size), size))
        full = False
    return ref if full else ref.at[tuple(cuts)]


def views(blocks, refs, step):
    return [view(block, ref, step) for block, ref in zip(blocks, refs)]


class Rows:
    def __init__(self, ref):
        self.ref = ref

    def __getitem__(self, span):
        return self.ref[pl.ds(pl.multiple_of(span * SPAN, SPAN), SPAN), :]

    def __setitem__(self, span, value):
        pass


def kept(dims, dtype=f32):
    return pltpu.VMEM(dims, dtype)


def flat(kernel, number, name, work, ins, outs, scratch, far=()):
    shapes = [*[kept(a.shape, a.dtype) for a in work.outs], *outs]
    return pl.pallas_call(
        functools.partial(kernel, work),
        in_specs=[IN_VMEM] * (len(work.ins) + len(ins)) + [IN_HBM] * len(far),
        out_specs=[IN_VMEM] * len(shapes),
        out_shape=shapes,
        scratch_shapes=scratch,
        compiler_params=pltpu.CompilerParams(
            collective_id=number, has_side_effects=True, vmem_limit_bytes=SMALL_LIMIT
        ),
        name=name,
    )(*work.ins, *ins, *[pltpu.with_memory_space_constraint(a, pltpu.HBM) for a in far])


def total_kernel(mine, every, planes, lines, send, recv, local):
    h = Here()
    w = Wires(send, recv, local)
    greet(near(h) + line(h))
    keep = w.keep(mine, planes.at[h.z])
    for up in range(1, 4):
        w.send(mine, planes.at[h.z], up, h.plane(up)[0])
    keep.wait()
    for up in range(1, 4):
        device, z = h.plane(4 - up)
        w.arrived(planes.at[z], up, device)
    lines[...] = jnp.sum(planes[...], axis=0)
    for o in range(1, 8):
        w.send(lines, every.at[h.t], 3 + o, h.mate(o)[0])
    keep = w.keep(lines, every.at[h.t])
    for o in range(1, 8):
        device, place = h.mate(o)
        w.arrived(every.at[place], 3 + o, device)
    keep.wait()
    w.finish()


def vmem(*dims, dtype=f32):
    return pltpu.VMEM(dims, dtype)


class Direct:
    @staticmethod
    def start(in_weight, out_weight, tokens, docs, conv, head, gain, norm):
        rows = PLANE * SPAN
        outs = [kept((D, MAIN), bf16), kept((4, PLANE, 32, SHARED), bf16), kept((rows, D), bf16), kept((16, D), bf16),
                kept((8, LOCAL)), kept((1, 128)), kept((1, 128)), kept((1, WIDE)), kept((1, WIDE)),
                kept((128, 128), bf16), kept((4, 1, WIDE)), kept((4, 1, WIDE)), kept((rows + 8, 8)),
                kept((PLANE, 1, SPAN)), kept(out_weight.shape, bf16), kept((1, D))]
        ins = [in_weight, out_weight, tokens, docs.reshape(-1, 128), conv, head, gain, norm]
        ins = [pltpu.with_memory_space_constraint(a, pltpu.HBM) for a in ins]
        loaded = [ins[i] for i in (0, 1, 3, 4, 5, 6)]
        wm, ws, x, halo, *prepared, flags, doc_rows, out_low, norm = pl.pallas_call(
            start_kernel,
            in_specs=[IN_HBM] * len(ins),
            out_specs=[IN_VMEM] * len(outs),
            out_shape=outs,
            scratch_shapes=[*[pltpu.VMEM(a.shape, a.dtype) for a in loaded], vmem(PLANE, 32, MAIN, dtype=bf16),
                            vmem(32, SHARED, dtype=bf16)] + wires(51, 10),
            compiler_params=pltpu.CompilerParams(collective_id=0, has_side_effects=True, vmem_limit_bytes=SMALL_LIMIT),
            name="gather_start",
        )(*ins)
        return wm, ws.reshape(D, SHARED), x, halo, prepared, flags, doc_rows, out_low, norm

    @staticmethod
    def first(spans, work, cotangent, out):
        rows = spans * SPAN
        return flat(
            first_direct, 1, "project_scan", work, [out],
            [kept((NSTATE, WIDE)), kept((rows, D), bf16), kept((WIDE, D), bf16)],
            [*work.scratch[:3], vmem(4, PACK, WIDE), vmem(PACK, WIDE, dtype=bf16), vmem(4, PACK, WIDE, dtype=bf16)]
            + wires(16, 2), [cotangent],
        )

    @staticmethod
    def second(spans, work):
        return work, None, None

    @staticmethod
    def third(spans, work):
        work.second, normed = work.ins[0], work.ins[10]
        work.ins = [*work.second.ins, normed]
        *outs, gout, ggw, ends, chip, held = flat(
            third_direct, 4, "carry_gate_back", work, [],
            [kept((4, PACK, WIDE)), kept((SPAN, D)), kept((2, SPAN, D), bf16)],
            [vmem(4, SPAN, D), vmem(4, SPAN, D), *work.scratch[:3], vmem(PLANE, spans, 2, SPAN),
             vmem(PACK, WIDE, dtype=bf16), vmem(4, PACK, WIDE, dtype=bf16)] + wires(18, 1),
        )
        return *outs, gout, ggw, ends, (chip, held)

    @staticmethod
    def fourth(spans, work, gout, ggw, mix):
        chip, held = mix
        gpre, hsum, rmix, near_gate, far_gate, parts, own, tails, steps = flat(
            fourth_direct, 5, "scan_back", work, [held, ggw],
            [kept((2, SPAN, D), bf16), kept((2, WIDE, SPAN)),
             kept((3, WIDE, SPAN), bf16), kept((2, SPAN, STATES), bf16), kept((SPAN, STATES)), kept((PLANE, 8, STATES)),
             kept((PLANE, 8, SPAN))],
            [*work.scratch, vmem(PLANE, SPAN, STATES), vmem(4, SPAN, STATES), vmem(2, SPAN, STATES, dtype=bf16), vmem(spans, 8, SPAN),
             vmem(8, WIDE), vmem(SPAN, STATES, dtype=bf16), vmem(SPAN // 2, STATES, dtype=bf16),
             vmem(SPAN // 2, STATES, dtype=bf16), vmem(WIDE, D, dtype=bf16)] + wires(36, 3),
        )
        ggw = [ggw, near_gate, far_gate]
        return gpre, hsum, [parts, own], tails, steps, gout, [chip, rmix], ggw

    @staticmethod
    def fifth(spans, work, ggw, grad_state, gout, rest):
        piece = vmem(4, 4, 32, SHARED)
        mix, *rest = rest
        pgate, pinner, ps, psmall, near_out, far_out, *tokens_back = flat(
            fifth_direct, 6, "conv_back_reduce", work, [*ggw, grad_state.reshape(4, PLANE, 32, SHARED), gout, *mix, *rest],
            [kept((PLANE, 32, WIDE)), kept((PLANE, 32, WIDE)), kept((4, 32, SHARED)), kept((PLANE, SMALL, WIDE)),
             kept((2, HEAD_DIM, D)), kept((3, HEAD_DIM, D), bf16), kept((SPAN, D), bf16), kept((SPAN, D)),
             kept((D // 128, 128)), kept((4, SPAN, D)), kept((4, SPAN, D)), kept((2, SPAN, D), bf16),
             kept((2, SPAN, D), bf16), kept((SPAN, D))],
            [*work.scratch, vmem(spans, SPAN, WIDE, dtype=bf16), vmem(WIDE, D), vmem(WIDE, D, dtype=bf16),
             vmem(SMALL, WIDE), vmem(3, SPAN, WIDE, dtype=bf16),
             vmem(SPAN, WIDE), vmem(SPAN, WIDE), piece, vmem(3, 4, 32, SHARED, dtype=bf16),
             vmem(3, 4, 32, SHARED, dtype=bf16), vmem(4, 32, SHARED),
             vmem(4, SMALL, WIDE), vmem(SMALL, WIDE), vmem(SPAN, D, dtype=bf16), vmem(SPAN // 2, D, dtype=bf16),
             vmem(SPAN // 2, D, dtype=bf16), vmem(WIDE, D, dtype=bf16)] + wires(60, 5),
        )
        return pgate, pinner, ps, tokens_back[:3], psmall, tokens_back[3:], [gout, near_out, far_out]

    @staticmethod
    def total(part):
        return talk(
            total_kernel, 9, "sum_all", [kept((PLANE, *part.shape))], [part],
            [vmem(4, *part.shape), vmem(*part.shape)] + wires(11, 2),
        )[0]


class Plain:
    @staticmethod
    def start(in_weight, out_weight, tokens, docs, conv, head, gain, norm):
        main, shared, out_low = run_pack(in_weight, out_weight)
        rows = main.shape[1]
        main = lax.all_to_all(main, TP, split_axis=0, concat_axis=0, tiled=True)
        main = lax.all_gather(main.reshape(PLANE * rows, MAIN), "grp", axis=0, tiled=True)
        shared = lax.all_gather(shared, ALL, axis=0, tiled=True)
        x = lax.all_gather(tokens, TP, axis=0, tiled=True)
        groups, group = lax.axis_size("grp"), lax.axis_index("grp")
        halo = lax.ppermute(x[x.shape[0] - 16 :], "grp", [(g, (g + 1) % groups) for g in range(groups)])
        at = jnp.stack([group, lax.axis_index(TP)])
        flags = plain_flags(docs, group, x.shape[0])
        return main, shared, x, halo, run_prep(groups, at, conv, head, gain), *flags, out_low, norm

    @staticmethod
    def first(spans, work, cotangent, out):
        *outs, end = launch(
            functools.partial(first_plain, spans), "project_scan", 2 * spans, work.in_specs, work.ins,
            [*work.out_specs, whole(PACK, WIDE)], [*work.outs, shape(PACK, WIDE)], work.scratch,
        )
        groups, group = lax.axis_size("grp"), lax.axis_index("grp")
        ends = lax.all_gather(end, "grp")

        def one(g, carried):
            return jnp.where(g < group, ends[g, NSTATE : NSTATE + 1] * carried + ends[g, :NSTATE], carried)

        inc = lax.fori_loop(0, groups, one, jnp.zeros((NSTATE, WIDE), f32))
        every = lax.all_gather(out, ALL, axis=0, tiled=True).reshape(HERE, PLANE, HEAD_DIM, D)
        wo = lax.dynamic_index_in_dim(every, lax.axis_index(TP), 1, False).reshape(WIDE, D)
        return *outs, inc, lax.all_gather(cotangent, TP, axis=0, tiled=True), wo

    @staticmethod
    def second(spans, work):
        y, gno, sums = launch(
            second_kernel, "scan_carry", spans, work.in_specs, work.ins,
            [*work.out_specs, spec((1, 2, SPAN), lambda s: (s, 0, 0))], [*work.outs, shape(spans, 2, SPAN)],
        )
        return y, gno, lax.all_gather(sums, TP)

    @staticmethod
    def third(spans, work):
        start = (whole(PACK, WIDE), shape(PACK, WIDE))
        mix = (work.later(D), shape(spans * SPAN, D))
        *outs, start, mix = launch(
            functools.partial(third_plain, spans), "gate_norm_back", 2 * spans, work.in_specs, work.ins,
            [*work.out_specs, start[0], mix[0]], [*work.outs, start[1], mix[1]], work.scratch,
        )
        return *outs, lax.all_gather(start, "grp"), lax.psum_scatter(mix, TP, scatter_dimension=0, tiled=True)

    @staticmethod
    def fourth(spans, work, gout, ggw, mix):
        rows = spans * SPAN
        gpre, hsum, gst, gstep = launch(
            fourth_plain, "scan_back", spans, work.in_specs, work.ins,
            [*work.out_specs, spec((SPAN, STATES), lambda s: (s, 0)), spec((8, SPAN), lambda s: (0, s))],
            [shape(rows, WIDE), work.outs[1], shape(rows, STATES), shape(8, rows)], work.scratch,
        )
        groups = lax.axis_size("grp")
        back = [(g, (g - 1) % groups) for g in range(groups)]
        swap = lambda a: lax.all_to_all(a, TP, split_axis=0, concat_axis=0, tiled=True)
        blocks = gst.reshape(PLANE, SPAN, STATES)
        tails = jnp.concatenate([blocks[1:, 0:8], lax.ppermute(gst[0:8], "grp", back)[None]], axis=0)
        steps = gstep.reshape(8, PLANE, SPAN).transpose(1, 0, 2)
        empty = jnp.zeros((HERE, PLANE, HEAD_DIM, D), f32)
        mine = gout.reshape(HERE, HEAD_DIM, D)
        every = lax.dynamic_update_index_in_dim(empty, mine, lax.axis_index(TP), 1).reshape(INNER, D)
        out = lax.psum_scatter(every, ALL, scatter_dimension=0, tiled=True)
        gpre = jnp.concatenate([gpre, lax.ppermute(gpre[0:8], "grp", back)], axis=0)
        return gpre, hsum, [swap(blocks)], swap(tails), swap(steps), [out], [mix], ggw

    @staticmethod
    def fifth(spans, work, ggw, grad_state, gout, rest):
        gp, giw, small = launch(
            functools.partial(fifth_plain, spans), "conv_back", spans, work.in_specs, work.ins,
            [spec((SPAN, D), lambda s: (s, 0)), whole(WIDE, D), whole(SMALL, WIDE)],
            [shape(spans * SPAN, D), shape(WIDE, D), shape(SMALL, WIDE)],
            [*work.scratch, pltpu.VMEM((SPAN, WIDE), bf16)],
        )
        inner_z = lax.psum_scatter(giw.T, "grp", scatter_dimension=0, tiled=True)
        gate_z = lax.psum_scatter(ggw.T, "grp", scatter_dimension=0, tiled=True)
        rows = inner_z.shape[0] // PLANE
        home = lambda a: lax.all_to_all(a.reshape(PLANE, rows, WIDE), TP, split_axis=0, concat_axis=0, tiled=True)
        state = lax.psum_scatter(grad_state, ALL, scatter_dimension=0, tiled=True)
        small = lax.all_gather(lax.psum(small, "grp"), TP)
        gp = lax.psum_scatter(gp, TP, scatter_dimension=0, tiled=True)
        return home(gate_z), home(inner_z), state[None], run_seventh([gp], *rest), small, [], gout

    @staticmethod
    def total(part):
        return lax.psum(part, ALL)[None]


def run_pack(in_weight, out_weight):
    rows = in_weight.shape[0]
    return pl.pallas_call(
        pack_kernel,
        out_shape=[shape(PLANE, rows, MAIN, dtype=bf16), shape(rows, SHARED, dtype=bf16),
                   shape(*out_weight.shape, dtype=bf16)],
        compiler_params=pltpu.CompilerParams(vmem_limit_bytes=SMALL_LIMIT),
        name="pack_weights",
    )(in_weight, out_weight)


def plain_flags(doc_ids, group, rows):
    spans = rows // SPAN
    padded = jnp.concatenate([jnp.full((8,), -1, jnp.int32), doc_ids, jnp.full((8,), -2, jnp.int32)])
    window = lax.dynamic_slice(padded, (group * rows,), (rows + 16,))
    now = window[8:]
    lags = [now == window[8 - k : rows + 16 - k] for k in range(1, CONV)]
    by_span = window[8 : rows + 8].reshape(spans, SPAN)
    rise = by_span == window[7 : rows + 7 : SPAN][:, None]
    tail = by_span == by_span[:, SPAN - 1 :]
    fill = lambda a: jnp.pad(a.reshape(rows), (0, 8))
    zero = jnp.zeros_like(now)
    flags = jnp.stack([a.astype(f32) for a in (*lags, fill(rise), fill(tail), now, zero, zero)], axis=1)
    return flags, by_span.astype(f32).reshape(spans, 1, SPAN)


def shards(
    plan,
    tokens, cotangent, doc_ids, norm_gain, in_weight, conv_params, head_params, out_gain, out_weight,
    norm_first, norm_second, in_first, in_second, conv_first, conv_second, head_first, head_second,
    gain_first, gain_second, out_first, out_second,
):
    groups = lax.axis_size("grp")
    group = lax.axis_index("grp")
    place = lax.axis_index(TP)
    tok_rows = tokens.shape[0]
    rows = PLANE * tok_rows
    spans = rows // SPAN

    wm, ws, x, halo, prepared, flags, doc_rows, out_low, norm_row = plan.start(
        in_weight, out_weight, tokens, doc_ids, conv_params, head_params, out_gain.reshape(INNER // 128, 128),
        norm_gain.reshape(1, D),
    )
    conv, bias, rate, skip, gain, pick, before_us, behind_us = prepared

    normed, gate, chan, pre, act, dt, cum, held, pref, edge, part, incoming, cot, wo = plan.first(
        spans, First(spans, x, halo, norm_row, wm, ws, pick, conv, bias, rate, flags, doc_rows, skip, before_us),
        cotangent, out_low,
    )
    y, gno, sums = plan.second(spans, Second(spans, act, cum, flags, held, pref, incoming, part, gate, cot, wo, gain))
    gy, ggate, behind, suff, gog, gskip, gout, ggw, starts, mix = plan.third(
        spans, Third(spans, y, gate, gno, sums, act, cum, flags, gain, cot, wo, normed)
    )
    gpre, hsum, parts, tails, steps, gout, mix, ggw = plan.fourth(
        spans,
        Fourth(spans, act, dt, cum, flags, doc_rows, held, pref, incoming, behind, suff, starts, behind_us, gy, pre,
               skip, rate),
        gout, ggw, mix,
    )
    gs, gconv_state, grad_state = run_sixth(parts, tails, steps, flags, chan, edge, conv, tokens, norm_row)
    g_gate, g_inner, g_shared, tokens_back, small, spare, grads_out = plan.fifth(
        spans,
        Fifth(spans, gpre, flags, chan, edge, conv, normed, gconv_state, gog, gskip, hsum, ggate, wm),
        ggw, grad_state, gout, (mix, gs, ws, tokens, cotangent, norm_row),
    )
    mixed, grad_tokens, grad_norm_gain = tokens_back
    in_f, in_s, in_u, out_f, out_s, out_u, sums = run_adam(
        g_gate, g_inner, g_shared, grad_norm_gain, in_weight, in_first, in_second,
        out_weight, out_first, out_second, grads_out, spare,
    )
    norm3 = [a.reshape(D // 128, 128) for a in (norm_gain, norm_first, norm_second)]
    gain3 = [a.reshape(INNER // 128, 128) for a in (out_gain, gain_first, gain_second)]
    params = [*norm3, conv_params, conv_first, conv_second, head_params, head_first, head_second, *gain3]
    in_w, out_w, *rest = run_last(plan.total(sums), small, [in_weight, in_u, out_weight, out_u], params)
    rest[0:3] = [a.reshape(D) for a in rest[0:3]]
    rest[9:12] = [a.reshape(INNER) for a in rest[9:12]]
    return (mixed, grad_tokens, *rest[0:3], in_f, in_s, in_w, *rest[3:12], out_f, out_s, out_w)


def solution(mesh):
    seq = mesh.shape["seq"]
    sub = PLANE // seq
    groups = mesh.shape["fsdp"] // sub
    cut = Mesh(mesh.devices.reshape(groups, sub, seq), ALL)
    plan = Direct if (groups, sub, seq) == (4, 4, 2) else Plain
    split = P(ALL, None)
    none = P()
    return jax.shard_map(
        functools.partial(shards, plan),
        mesh=cut,
        in_specs=(split, split, none, none, split, none, none, none, split, none, none, split, split)
        + (none,) * 6
        + (split, split),
        out_specs=(split, split) + (none,) * 3 + (split,) * 3 + (none,) * 9 + (split,) * 3,
        check_vma=False,
    )
```

```python
import functools

import jax
import jax.numpy as jnp
from jax import lax
from jax.experimental import pallas as pl
from jax.experimental.pallas import tpu as pltpu
from jax.sharding import Mesh, PartitionSpec as P

HEADS = 32
HEAD_DIM = 64
NSTATE = 128
CONV = 4
SPAN = 256
STEP = 10
INNER = 2048
D = 1024

EPS_NORM = 1e-05
BETA_ONE = 0.9
BETA_TWO = 0.999
ADAM_EPS = 1e-06
DECAY = 0.01
RATE = 0.5

PLANE = 8
HERE = HEADS // PLANE
WIDE = HERE * HEAD_DIM
STATES = 2 * NSTATE
LOCAL = WIDE + STATES
PACK = NSTATE + 8
MAIN = 2 * WIDE
SHARED = STATES + 128
SMALL = 24
TP = ("sub", "seq")
ALL = ("grp", "sub", "seq")

f32 = jnp.float32
bf16 = jnp.bfloat16


def dot(a, b, ca=1, cb=0):
    return lax.dot_general(a, b, (((ca,), (cb,)), ((), ())), preferred_element_type=f32)


def split2(x):
    high = x.astype(bf16)
    return high, (x - high.astype(f32)).astype(bf16)


def split3(x):
    high = x.astype(bf16)
    rest = x - high.astype(f32)
    mid = rest.astype(bf16)
    return high, mid, (rest - mid.astype(f32)).astype(bf16)


def exact_left(a, b, ca=1, cb=0):
    high, low = split2(b)
    return dot(a, high, ca, cb) + dot(a, low, ca, cb)


def exact_right(a, b, ca=1, cb=0):
    high, low = split2(a)
    return dot(high, b, ca, cb) + dot(low, b, ca, cb)


def both_split(a, b, ca=1, cb=0):
    ah, al = split2(a)
    bh, bl = split2(b)
    return dot(ah, bh, ca, cb) + dot(al, bh, ca, cb) + dot(ah, bl, ca, cb)


def running(mask, x):
    a, b, c = split3(x)
    return dot(mask, a) + dot(mask, b) + dot(mask, c)


def spread(cols):
    lane = lax.broadcasted_iota(jnp.int32, (cols.shape[0], 128), 1)
    halves = [
        jnp.where(lane < HEAD_DIM, cols[:, 2 * i : 2 * i + 1], cols[:, 2 * i + 1 : 2 * i + 2])
        for i in range(HERE // 2)
    ]
    return jnp.concatenate(halves, axis=1)


def head_sum(x):
    row = lax.broadcasted_iota(jnp.int32, (WIDE, 128), 0)
    lane = lax.broadcasted_iota(jnp.int32, (WIDE, 128), 1)
    pick = (row // HEAD_DIM == lane).astype(bf16)
    return exact_right(x, pick)


def sigmoid(x):
    return 1.0 / (1.0 + jnp.exp(-x))


def half_tanh(x):
    return 0.5 * jnp.tanh(0.5 * x) + 0.5


def silu(x):
    return x * half_tanh(x)


def silu_slope(x):
    s = half_tanh(x)
    return s * (1.0 + x * (1.0 - s))


def lower(rows):
    i = lax.broadcasted_iota(jnp.int32, (rows, rows), 0)
    j = lax.broadcasted_iota(jnp.int32, (rows, rows), 1)
    return j <= i


def head_mask(x, h):
    lane = lax.broadcasted_iota(jnp.int32, x.shape, 1)
    return jnp.where(lane // HEAD_DIM == h, x, jnp.zeros_like(x))


def pack_kernel(wi_ref, wo_ref, main_ref, shared_ref, out_ref):
    weight = wi_ref[...].astype(bf16)
    for base in (0, 1):
        for t in range(PLANE):
            lanes = slice(HEAD_DIM * (t % 2), HEAD_DIM * (t % 2 + 1))
            for half in range(HERE // 2):
                tiles = []
                for i in (2 * half, 2 * half + 1):
                    at = base * INNER + i * PLANE * HEAD_DIM + t // 2 * 128
                    tiles.append(weight[:, at : at + 128][:, lanes])
                at = base * WIDE + 128 * half
                main_ref[t, :, at : at + 128] = jnp.concatenate(tiles, axis=1)
    shared_ref[...] = jnp.zeros_like(shared_ref)
    shared_ref[:, : STATES + HEADS] = weight[:, 2 * INNER :]
    out_ref[...] = wo_ref[...].astype(bf16)


def prepare(
    group, place, conv_ref, head_ref, gain_ref,
    conv_out, bias_out, rate_out, skip_out, gain_out, pick_out, before_out, behind_out,
):
    pair = jnp.where(place >= 2, 1, 0) + jnp.where(place >= 4, 1, 0) + jnp.where(place >= 6, 1, 0)
    odd = place - 2 * pair == 1

    def half(x):
        return jnp.where(odd, x[:, HEAD_DIM:], x[:, :HEAD_DIM])

    def four(get):
        halves = [half(get(i)) for i in range(HERE)]
        return [jnp.concatenate(halves[2 * i : 2 * i + 2], axis=1) for i in range(HERE // 2)]

    conv_out[...] = jnp.zeros_like(conv_out)
    columns = lambda i: conv_ref[:, pl.ds(pl.multiple_of(i * PLANE * HEAD_DIM + pair * 128, 128), 128)]
    for i, tile in enumerate(four(columns)):
        conv_out[0 : CONV + 1, 128 * i : 128 * (i + 1)] = tile
    conv_out[0 : CONV + 1, WIDE:] = conv_ref[:, INNER:]
    for i, tile in enumerate(four(lambda i: gain_ref[pl.ds(i * PLANE // 2 + pair, 1), :])):
        gain_out[:, 128 * i : 128 * (i + 1)] = tile
    head = lax.broadcasted_iota(jnp.int32, (3, HEADS), 1)
    lane = lax.broadcasted_iota(jnp.int32, (3, 128), 1)
    mine = jnp.zeros((3, 128), f32)
    for i in range(HERE):
        one = jnp.sum(jnp.where(head == PLANE * i + place, head_ref[...], 0.0), axis=1, keepdims=True)
        mine = mine + jnp.where(lane == i, one, 0.0)
    bias_out[...] = mine[0:1]
    rate_out[...] = jnp.where(lane[0:1] < HERE, -jnp.exp(mine[1:2]), 0.0)
    skip_out[...] = spread(jnp.broadcast_to(mine[2:3], (8, 128)))[0:1]
    row = lax.broadcasted_iota(jnp.int32, (128, 128), 0)
    column = lax.broadcasted_iota(jnp.int32, (128, 128), 1)
    pick_out[...] = jnp.where((row == PLANE * column + place) & (row < HEADS), 1.0, 0.0).astype(bf16)
    rank = lax.broadcasted_iota(jnp.int32, before_out.shape, 0)
    before_out[...] = (rank < group).astype(f32)
    behind_out[...] = (rank > group).astype(f32)


def flags_of(z, docs, flags, doc_rows):
    lines = PLANE * SPAN // 128
    lane = lax.broadcasted_iota(jnp.int32, (1, 128), 1)
    total = docs.shape[0]
    first = z * lines

    def line(i):
        at = first + i
        inside = jnp.clip(at, 0, total - 1)
        got = docs[pl.ds(inside, 1), :].astype(f32)
        return jnp.where(at < 0, -1.0, jnp.where(at >= total, -2.0, got))

    rows = [line(i) for i in range(-1, lines + 1)]
    for i in range(lines + 1):
        now, last = rows[i + 1], rows[i]
        same = []
        for k in range(1, CONV):
            moved = jnp.where(lane < k, pltpu.roll(last, k, 1), pltpu.roll(now, k, 1))
            same.append((moved == now).astype(f32))
        span = min(i, lines - 1) // 2
        rise = (now == rows[2 * span][:, 127:128]).astype(f32)
        tail = (now == rows[2 * span + 2][:, 127:128]).astype(f32)
        both = jnp.concatenate([*same, rise, tail, now, now * 0.0, now * 0.0], axis=0).T
        if i < lines:
            flags[128 * i : 128 * (i + 1), :] = both
            doc_rows[i // 2, :, 128 * (i % 2) : 128 * (i % 2 + 1)] = now
        else:
            flags[128 * i : 128 * i + 8, :] = both[0:8, :]


def prep_kernel(at_ref, *refs):
    prepare(at_ref[0], at_ref[1], *refs)


def normalize(rows, gain):
    vals = rows.astype(f32)
    inv = lax.rsqrt(jnp.mean(vals * vals, axis=1, keepdims=True) + EPS_NORM)
    return (vals * inv * gain).astype(bf16)


def first_begin(halo_ref, ng_ref, wm_ref, ws_ref, edge_ref, ext, state, decay):
    before = normalize(halo_ref[...], ng_ref[...])
    inner = dot(before, wm_ref[:, WIDE : 2 * WIDE]).astype(bf16).astype(f32)
    shared = dot(before, ws_ref[:, :STATES]).astype(bf16).astype(f32)
    rows = jnp.concatenate([inner, shared], axis=1)[8:16]
    ext[SPAN : SPAN + 8, :] = rows
    edge_ref[...] = rows
    state[...] = jnp.zeros_like(state)
    decay[...] = jnp.ones_like(decay)


def first_phase(
    span, x_ref, halo_ref, ng_ref, wm_ref, ws_ref, pick_ref, conv_ref, bias_ref, rate_ref, fl_ref,
    normed_ref, gate_ref, chan_ref, pre_ref, act_ref, dt_ref, cum_ref, held_ref, pref_ref, edge_ref,
    ext, state, decay, end_ref, act_all, dt_all, cum_all,
):
    ext[0:8, :] = ext[SPAN : SPAN + 8, :]
    normed = normalize(x_ref[...], ng_ref[...])
    normed_ref[...] = normed
    main = dot(normed, wm_ref[...]).astype(bf16)
    shared = dot(normed, ws_ref[...]).astype(bf16)
    gate_ref[...] = main[:, :WIDE]
    chan = jnp.concatenate([main[:, WIDE:], shared[:, :STATES]], axis=1)
    chan_ref[...] = chan
    ext[8 : SPAN + 8, :] = chan.astype(f32)
    flags = fl_ref[...]
    pre = conv_ref[4:5, :] + ext[8 : SPAN + 8, :] * conv_ref[0:1, :]
    for k in range(1, CONV):
        moved = ext[8 - k : SPAN + 8 - k, :] * conv_ref[k : k + 1, :]
        pre = pre + jnp.where(flags[:, k - 1 : k] > 0.5, moved, 0.0)
    pre_ref[...] = pre
    act = silu(pre).astype(bf16)
    act_ref[...] = act
    act_all[span] = act
    step = dot(shared[:, STATES:], pick_ref[...]) + bias_ref[...]
    dt = jnp.maximum(step, 0.0) + jnp.log1p(jnp.exp(-jnp.abs(step)))
    lane = lax.broadcasted_iota(jnp.int32, dt.shape, 1)
    both = jnp.where(lane < HEAD_DIM, dt, pltpu.roll(sigmoid(step), HEAD_DIM, 1))
    dt_ref[...] = both
    dt_all[span] = both
    cum = running(lower(SPAN).astype(bf16), dt * rate_ref[...])
    cum_ref[...] = cum
    cum_all[span] = cum
    last = cum[SPAN - 1 : SPAN, :]
    ending = jnp.where(flags[:, 4:5] > 0.5, jnp.exp(last - cum), 0.0)
    inner = act[:, :WIDE]
    write = act[:, WIDE : WIDE + NSTATE]
    added = exact_left(write, spread(ending * dt) * inner.astype(f32), 0, 0)
    held = state[...]
    held_ref[0] = held
    pref_ref[0] = decay[...]
    closing = jnp.where(flags[SPAN - 1 : SPAN, 3:4] > 0.5, jnp.exp(last), 0.0)
    fade = spread(jnp.broadcast_to(closing, (8, 128)))
    held = fade[0:1, :] * held + added
    state[...] = held
    decay[...] = decay[...] * fade
    end_ref[0:NSTATE, :] = held
    end_ref[NSTATE:, :] = decay[...]


def carry_chain(ends_ref, ahead_ref, out_ref, reverse):
    out_ref[...] = jnp.zeros_like(out_ref)
    groups = ends_ref.shape[0]

    @pl.loop(0, groups)
    def _(step):
        g = groups - 1 - step if reverse else step
        one = ends_ref[g]
        on = ahead_ref[g] > 0.5
        held = out_ref[...]
        out_ref[...] = jnp.where(on, one[NSTATE : NSTATE + 1, :] * held + one[0:NSTATE, :], held)


def within_phase(span, fl_ref, row_ref, skip_ref, y_ref, act_all, dt_all, cum_all):
    act = act_all[span]
    inner = act[:, :WIDE]
    cum = cum_all[span]
    cum_t = cum.T
    dt_t = dt_all[span].T
    scores = dot(act[:, WIDE + NSTATE :], act[:, WIDE : WIDE + NSTATE], 1, 1)
    matched = (fl_ref[:, 5:6] == row_ref[0]) & lower(SPAN)
    y = skip_ref[...] * inner.astype(f32)
    for h in range(HERE):
        fade = jnp.exp(jnp.minimum(cum[:, h : h + 1] - cum_t[h : h + 1, :], 0.0))
        mixing = jnp.where(matched, fade, 0.0) * scores * dt_t[h : h + 1, :]
        y = y + exact_right(mixing, head_mask(inner, h))
    y_ref[...] = y


def second_kernel(
    read_ref, cum_ref, fl_ref, held_ref, pref_ref, inc_ref, part_ref, gate_ref, cot_ref, wo_ref, og_ref,
    y_ref, gno_ref, sums_ref,
):
    entering = held_ref[0] + pref_ref[0][0:1, :] * inc_ref[...]
    rising = jnp.where(fl_ref[:, 3:4] > 0.5, jnp.exp(cum_ref[...]), 0.0)
    y_low = (part_ref[...] + spread(rising) * exact_left(read_ref[...], entering)).astype(bf16)
    y_ref[...] = y_low
    gated = y_low.astype(f32) * silu(gate_ref[...].astype(f32))
    gno = dot(cot_ref[...], wo_ref[...], 1, 1)
    gno_ref[...] = gno
    squares = jnp.sum(gated * gated, axis=1, keepdims=True)
    along = jnp.sum(gno * og_ref[...] * gated, axis=1, keepdims=True)
    lane = lax.broadcasted_iota(jnp.int32, (SPAN, 128), 1)
    both = jnp.where(lane == 0, squares, jnp.where(lane == 1, along, 0.0))
    sums_ref[0] = both.T[0:2, :]


def third_begin(gog_ref, gskip_ref, gout_ref, ggw_ref, state, decay):
    for ref in (gog_ref, gskip_ref, gout_ref, ggw_ref, state):
        ref[...] = jnp.zeros_like(ref)
    decay[...] = jnp.ones_like(decay)


def third_first(
    at, y_ref, gate_ref, gno_ref, sums_ref, act_ref, cum_ref, fl_ref, og_ref,
    gy_ref, gg_ref, behind_ref, suff_ref, start_ref, gog_ref, gskip_ref,
    state, decay, no_all, gg_all,
):
    span = no_all.shape[0] - 1 - at
    act = act_ref[...]
    inner = act[:, :WIDE].astype(f32)
    read = act[:, WIDE + NSTATE :]
    flags = fl_ref[...]
    totals = jnp.sum(sums_ref[...], axis=0)
    inv_row = lax.rsqrt(totals[0:1, :] / INNER + EPS_NORM)
    mean_row = inv_row * totals[1:2, :] / INNER
    cols = jnp.concatenate([inv_row, mean_row, jnp.zeros((6, SPAN), f32)], axis=0).T
    inv = cols[:, 0:1]
    mean = cols[:, 1:2]
    y = y_ref[...].astype(f32)
    gate = gate_ref[...].astype(f32)
    gate_act = silu(gate)
    unit = y * gate_act * inv
    gno = gno_ref[...]
    no_all[span] = (unit * og_ref[...]).astype(bf16)
    grad_gated = inv * (gno * og_ref[...] - unit * mean)
    gy = (grad_gated * gate_act).astype(bf16)
    gy_ref[...] = gy
    ggate = (grad_gated * y * silu_slope(gate)).astype(bf16)
    gg_ref[...] = ggate
    gg_all[span] = ggate
    gyf = gy.astype(f32)
    gog_ref[...] += jnp.sum(gno * unit, axis=0, keepdims=True)
    gskip_ref[...] += jnp.sum(inner * gyf, axis=0, keepdims=True)
    rising = jnp.where(flags[:, 3:4] > 0.5, jnp.exp(cum_ref[...]), 0.0)
    wide = spread(rising)
    pulled = exact_left(read, wide * gyf, 0, 0)
    held = state[...]
    behind_ref[0] = held
    suff_ref[0] = decay[...]
    fade = wide[SPAN - 1 : SPAN, :]
    held = fade * held + pulled
    state[...] = held
    decay[...] = decay[...] * fade
    start_ref[0:NSTATE, :] = held
    start_ref[NSTATE:, :] = decay[...]


def third_second(span, place, cot_ref, wo_ref, normed_ref, mix_ref, gout_ref, ggw_ref, no_all, gg_all):
    mix_ref[...] = dot(no_all[place], wo_ref[...])
    gout_ref[...] += dot(no_all[span], cot_ref[...], 0, 0)
    ggw_ref[...] += dot(gg_all[span], normed_ref[...], 0, 0)


def fourth_kernel(
    at, act_ref, dt_ref, cum_ref, fl_ref, row_ref, held_ref, pref_ref, inc_ref, behind_ref, suff_ref,
    ends_ref, ahead_ref, gy_ref, pre_ref, skip_ref, rate_ref,
    gpre_ref, gst_ref, gstep_ref, hsum_ref,
    out_ref,
):
    @pl.when(at == 0)
    def _():
        hsum_ref[...] = jnp.zeros_like(hsum_ref)
        carry_chain(ends_ref, ahead_ref, out_ref, True)

    act = act_ref[...]
    inner = act[:, :WIDE]
    innerf = inner.astype(f32)
    write = act[:, WIDE : WIDE + NSTATE]
    read = act[:, WIDE + NSTATE :]
    flags = fl_ref[...]
    cum = cum_ref[...]
    dt = dt_ref[...]
    gy = gy_ref[...]
    gyf = gy.astype(f32)
    cum_t = cum.T
    entering = held_ref[0] + pref_ref[0][0:1, :] * inc_ref[...]
    leaving = behind_ref[0] + suff_ref[0][0:1, :] * out_ref[...]
    last = cum[SPAN - 1 : SPAN, :]
    rising = jnp.where(flags[:, 3:4] > 0.5, jnp.exp(cum), 0.0)
    ending = jnp.where(flags[:, 4:5] > 0.5, jnp.exp(last - cum), 0.0)
    scores = dot(write, read, 1, 1)
    i = lax.broadcasted_iota(jnp.int32, (SPAN, SPAN), 0)
    j = lax.broadcasted_iota(jnp.int32, (SPAN, SPAN), 1)
    matched = (flags[:, 5:6] == row_ref[0]) & (i <= j)
    lane = lax.broadcasted_iota(jnp.int32, (SPAN, 128), 1)
    from_state = exact_left(write, leaving)
    grad_scaled = spread(ending) * from_state
    grad_scores = jnp.zeros((SPAN, SPAN), f32)
    rows_of = []
    cols_of = jnp.zeros((SPAN, 128), f32)
    for h in range(HERE):
        fade = jnp.exp(jnp.minimum(cum_t[h : h + 1, :] - cum[:, h : h + 1], 0.0))
        weights = jnp.where(matched, fade, 0.0)
        grad_scaled = grad_scaled + exact_right(weights * scores, head_mask(gy, h))
        part = dot(head_mask(inner, h), gy, 1, 1) * weights * dt[:, h : h + 1]
        grad_scores = grad_scores + part
        logs = part * scores
        rows_of.append(jnp.sum(logs, axis=0, keepdims=True))
        cols_of = cols_of + jnp.where(lane == h, jnp.sum(logs, axis=1, keepdims=True), 0.0)
    rows_of.append(jnp.zeros((128 - HERE, SPAN), f32))
    grad_cum = jnp.concatenate(rows_of, axis=0).T - cols_of
    high, low = split2(grad_scores)
    grad_write = dot(high, read) + dot(low, read)
    grad_read = dot(high, write, 0, 0) + dot(low, write, 0, 0)
    read_state = exact_left(read, entering)
    grad_read = grad_read + both_split(spread(rising) * gyf, entering, 1, 1)
    grad_write = grad_write + both_split(spread(ending * dt) * innerf, leaving, 1, 1)
    tail = head_sum(innerf * from_state) * dt * ending
    grad_cum = grad_cum + head_sum(gyf * read_state) * rising - tail
    crossing = jnp.sum(entering * leaving, axis=0, keepdims=True)
    crossing = head_sum(jnp.broadcast_to(crossing, (8, WIDE)))[0:1, :] * rising[SPAN - 1 : SPAN, :]
    end_term = jnp.sum(tail, axis=0, keepdims=True) + crossing
    row = lax.broadcasted_iota(jnp.int32, (SPAN, 128), 0)
    grad_cum = grad_cum + jnp.where(row == SPAN - 1, end_term, 0.0)
    grad_log = running((i <= j).astype(bf16), grad_cum)
    grad_steps = grad_log * rate_ref[...] + head_sum(innerf * grad_scaled)
    grad_step_raw = jnp.where(lane < HERE, grad_steps * pltpu.roll(dt, HEAD_DIM, 1), 0.0)
    gstep_ref[...] = grad_step_raw.T[0:8, :]
    grad_rate = jnp.where(lane < HERE, grad_log * dt, 0.0)
    hsum_ref[0:1, :] += jnp.sum(grad_step_raw, axis=0, keepdims=True)
    hsum_ref[1:2, :] += jnp.sum(grad_rate, axis=0, keepdims=True)
    grad_inner = spread(dt) * grad_scaled + skip_ref[...] * gyf
    slope = silu_slope(pre_ref[...])
    gpre_ref[...] = grad_inner * slope[:, :WIDE]
    gst_ref[...] = jnp.concatenate([grad_write, grad_read], axis=1) * slope[:, WIDE:]


def conv_back(gpre, flags, chan_ext, conv_ref, masked):
    rows = gpre.shape[0] - 8
    total = gpre[0:rows, :] * conv_ref[0:1, :]
    sums = [jnp.sum(gpre[0:rows, :] * chan_ext[8 : rows + 8, :], axis=0, keepdims=True)]
    for k in range(1, CONV):
        masked[...] = jnp.where(flags[:, k - 1 : k] > 0.5, gpre, 0.0)
        total = total + masked[k : rows + k, :] * conv_ref[k : k + 1, :]
        sums.append(jnp.sum(masked[0:rows, :] * chan_ext[8 - k : rows + 8 - k, :], axis=0, keepdims=True))
    sums.append(jnp.sum(gpre[0:rows, :], axis=0, keepdims=True))
    sums.append(jnp.zeros((3, gpre.shape[1]), f32))
    return total, jnp.concatenate(sums, axis=0)


def fifth_begin(gstate_ref, gog_ref, gskip_ref, hsum_ref, giw_ref, small_ref):
    giw_ref[...] = jnp.zeros_like(giw_ref)
    small_ref[...] = jnp.zeros_like(small_ref)
    small_ref[8:16, :] = gstate_ref[...]
    small_ref[16:17, :] = gog_ref[...]
    small_ref[17:18, :] = gskip_ref[...]
    small_ref[18:19, 0:128] = hsum_ref[0:1, :]
    small_ref[18:19, 128:256] = hsum_ref[1:2, :]


def fifth_product(gg_ref, ginner, wm_ref):
    return dot(gg_ref[...], wm_ref[:, :WIDE], 1, 1) + dot(ginner, wm_ref[:, WIDE:], 1, 1)


def fifth_kernel(
    span, gpre_ref, fl_ref, chan_ref, edge_ref, conv_ref, normed_ref,
    ginner_ref, giw_ref, small_ref,
    chan_ext, masked,
):
    start = pl.multiple_of(span * SPAN, SPAN)

    @pl.when(span == 0)
    def _():
        chan_ext[0:8, :] = edge_ref[:, :WIDE]

    @pl.when(span > 0)
    def _():
        chan_ext[0:8, :] = chan_ref[pl.ds(pl.multiple_of(start - 16, 16), 16), :WIDE].astype(f32)[8:16, :]

    chan_ext[8 : SPAN + 8, :] = chan_ref[pl.ds(start, SPAN), :WIDE].astype(f32)
    gpre = gpre_ref[pl.ds(start, SPAN + 8), :]
    total, sums = conv_back(gpre, fl_ref[pl.ds(start, SPAN + 8), :], chan_ext, conv_ref, masked)
    ginner = total.astype(bf16)
    small_ref[0:8, :] += sums
    ginner_ref[...] = ginner
    giw_ref[...] += dot(ginner, normed_ref[...], 0, 0)


def sixth_kernel(count, *refs):
    sixth_body(refs[:count], *refs[count:])


def sixth_body(
    parts, tails_ref, steps_ref, fl_ref, chan_ref, edge_ref, conv_ref, x_ref, ng_ref,
    gs_ref, gconv_ref, gw_ref,
    gext, chan_ext, masked,
):
    place = lax.axis_index("sub") * lax.axis_size("seq") + lax.axis_index("seq")
    start = pl.multiple_of(place * SPAN, SPAN)
    total = jnp.sum(parts[0][...].astype(f32), axis=0)
    for part in parts[1:]:
        total = total + part[...]
    gext[0:SPAN, :] = total
    gext[SPAN : SPAN + 8, :] = jnp.sum(tails_ref[...], axis=0)
    chan_ext[8 : SPAN + 8, :] = chan_ref[pl.ds(start, SPAN), WIDE:].astype(f32)

    @pl.when(place == 0)
    def _():
        chan_ext[0:8, :] = edge_ref[:, WIDE:]

    @pl.when(place > 0)
    def _():
        chan_ext[0:8, :] = chan_ref[pl.ds(pl.multiple_of(start - 16, 16), 16), WIDE:].astype(f32)[8:16, :]

    conv = conv_ref.at[:, WIDE:]
    total, sums = conv_back(gext[...], fl_ref[pl.ds(start, SPAN + 8), :], chan_ext, conv, masked)
    gconv_ref[...] = sums
    steps = jnp.concatenate([steps_ref[:, i, :] for i in range(HERE)] + [jnp.zeros((128 - HEADS, SPAN), f32)], axis=0)
    grads = jnp.concatenate([total, steps.T], axis=1).astype(bf16)
    gs_ref[...] = grads
    vals = x_ref[...].astype(f32)
    inv = lax.rsqrt(jnp.mean(vals * vals, axis=1, keepdims=True) + EPS_NORM)
    gw_ref[...] = dot((vals * inv * ng_ref[...]).astype(bf16), grads, 0, 0)


def seventh_kernel(skip, count, many, *refs):
    refs = refs[skip:]
    parts, mixes, rest = refs[:count], refs[count : count + many], refs[count + many :]
    gs_ref, ws_ref, x_ref, cot_ref, ng_ref, mixed_ref, gt_ref, gain_ref = rest

    def add_all(total, refs):
        for ref in refs:
            if len(ref.shape) == 2:
                total = total + ref[...].astype(f32)
            else:
                for i in range(ref.shape[0]):
                    total = total + ref[i].astype(f32)
        return total

    vals = x_ref[...].astype(f32)
    mixed_ref[...] = add_all(vals, mixes).astype(bf16)
    grad = add_all(dot(gs_ref[...], ws_ref[...], 1, 1), parts)
    inv = lax.rsqrt(jnp.mean(vals * vals, axis=1, keepdims=True) + EPS_NORM)
    unit = vals * inv
    s = grad * ng_ref[...]
    gt_ref[...] = cot_ref[...].astype(f32) + inv * (s - unit * jnp.mean(s * unit, axis=1, keepdims=True))
    row = jnp.sum(grad * unit, axis=0, keepdims=True)
    for i in range(D // 128):
        gain_ref[i : i + 1, :] = row[:, 128 * i : 128 * (i + 1)]


def adam_terms(weight, grad, first, second):
    first_new = BETA_ONE * first + (1.0 - BETA_ONE) * grad
    second_new = BETA_TWO * second + (1.0 - BETA_TWO) * grad * grad
    update = (
        first_new / (1.0 - BETA_ONE**STEP) / (jnp.sqrt(second_new / (1.0 - BETA_TWO**STEP)) + ADAM_EPS)
        + DECAY * weight
    )
    return (first_new, second_new, update)


def square_sum(x):
    return jnp.sum(jnp.sum(x * x, axis=1, keepdims=True), axis=0, keepdims=True)


def lamb_apply(weight, update, weight_sq, update_sq):
    return weight - RATE * (jnp.sqrt(weight_sq) / (jnp.sqrt(update_sq) + ADAM_EPS)) * update


def two_heads(ref, rows, i, pair):
    cols = slice(HEAD_DIM * i, HEAD_DIM * (i + 1))
    return jnp.concatenate([ref[2 * pair, rows, cols], ref[2 * pair + 1, rows, cols]], axis=1)


def from_planes(z, own, near, far):
    first = jnp.where(z > 0, near[0], far[0].astype(f32))
    third = jnp.where(z < 3, near[1], far[2].astype(f32))
    return own + first + far[1].astype(f32) + third


def adam_kernel(skip, count, *refs):
    refs = refs[skip:]
    results, refs = refs[:2], refs[2:]
    gate_ref, inner_ref, shared_ref, gain_ref, wi_ref, mi_ref, vi_ref, wo_ref, mo_ref, vo_ref = refs[:10]
    outs, refs = refs[10 : 10 + count], refs[10 + count :]
    mi_out, vi_out, ui_out, mo_out, vo_out, uo_out, sums_ref, *passed, grad = refs
    for ref, out in zip(results, passed):
        out[...] = ref[...]
    for base, ref in ((0, gate_ref), (INNER, inner_ref)):
        for i in range(HERE):
            for pair in range(PLANE // 2):
                at = base + i * PLANE * HEAD_DIM + pair * 128
                grad[:, at : at + 128] = two_heads(ref, slice(None), i, pair)
    grad[:, 2 * INNER :] = jnp.sum(shared_ref[...], axis=0)[:, : STATES + HEADS]
    weight = wi_ref[...]
    mi_out[...], vi_out[...], update = adam_terms(weight, grad[...], mi_ref[...], vi_ref[...])
    ui_out[...] = update
    sums_ref[0:8, :] = gain_ref[...]
    sums_ref[8:16, :] = jnp.zeros((8, 128), f32)
    sums_ref[8:9, :] = jnp.broadcast_to(square_sum(weight), (1, 128))
    sums_ref[9:10, :] = jnp.broadcast_to(square_sum(update), (1, 128))
    if count > 1:
        z = lax.axis_index("grp")
        total = from_planes(z, outs[0][pl.ds(pl.multiple_of(z * HEAD_DIM, HEAD_DIM), HEAD_DIM), :], *outs[1:])
    else:
        total = outs[0][...]
    weight = wo_ref[...]
    mo_out[...], vo_out[...], update = adam_terms(weight, total, mo_ref[...], vo_ref[...])
    uo_out[...] = update
    sums_ref[10:11, :] = jnp.broadcast_to(square_sum(weight), (1, 128))
    sums_ref[11:12, :] = jnp.broadcast_to(square_sum(update), (1, 128))


def last_kernel(
    every_ref, small_ref, wi_ref, ui_ref, wo_ref, uo_ref,
    nw_ref, nm_ref, nv_ref, cw_ref, cm_ref, cv_ref, hw_ref, hm_ref, hv_ref, gw_ref, gm_ref, gv_ref,
    wi_out, wo_out, nm_out, nv_out, nw_out, cm_out, cv_out, cw_out, hm_out, hv_out, hw_out, gm_out, gv_out, gw_out,
    conv, gain,
):
    total = jnp.sum(every_ref[...], axis=0)
    wi_out[...] = lamb_apply(wi_ref[...], ui_ref[...], total[8:9, 0:1], total[9:10, 0:1])
    wo_out[...] = lamb_apply(wo_ref[...], uo_ref[...], total[10:11, 0:1], total[11:12, 0:1])

    def update(grad, weight_ref, first_ref, second_ref, first_out, second_out, weight_out):
        weight = weight_ref[...]
        first, second, step = adam_terms(weight, grad, first_ref[...], second_ref[...])
        first_out[...] = first
        second_out[...] = second
        weight_out[...] = lamb_apply(weight, step, square_sum(weight), square_sum(step))

    update(total[0:8], nw_ref, nm_ref, nv_ref, nm_out, nv_out, nw_out)
    for i in range(HERE):
        for pair in range(PLANE // 2):
            at = i * PLANE * HEAD_DIM + pair * 128
            conv[:, at : at + 128] = two_heads(small_ref, slice(0, 8), i, pair)
            gain[at // 128 : at // 128 + 1, :] = two_heads(small_ref, slice(16, 17), i, pair)
    conv[:, INNER:] = jnp.sum(small_ref[:, 8:16, :], axis=0)
    update(conv[0:5, :], cw_ref, cm_ref, cv_ref, cm_out, cv_out, cw_out)
    update(gain[...], gw_ref, gm_ref, gv_ref, gm_out, gv_out, gw_out)

    t = lax.broadcasted_iota(jnp.int32, (PLANE, 128), 0)
    lane = lax.broadcasted_iota(jnp.int32, (PLANE, 128), 1)

    def by_head(cols):
        row = jnp.zeros((PLANE, 128), f32)
        for i in range(HERE):
            row = row + jnp.where(lane == PLANE * i + t, cols[:, i : i + 1], 0.0)
        return jnp.sum(row, axis=0, keepdims=True)[:, :HEADS]

    steps = by_head(small_ref[:, 18, 0:128])
    rates = by_head(small_ref[:, 18, 128:256]) * -jnp.exp(hw_ref[1:2, :])
    skips = by_head(head_sum(small_ref[:, 17, :]))
    update(jnp.concatenate([steps, rates, skips], axis=0), hw_ref, hm_ref, hv_ref, hm_out, hv_out, hw_out)


def spec(block, index):
    return pl.BlockSpec(block, index)


def whole(*dims):
    return pl.BlockSpec(dims, lambda *_: (0,) * len(dims))


def shape(*dims, dtype=f32):
    return jax.ShapeDtypeStruct(dims, dtype)


ANY = pl.BlockSpec(memory_space=pl.ANY)
IN_VMEM = pl.BlockSpec(memory_space=pltpu.VMEM)
IN_HBM = pl.BlockSpec(memory_space=pltpu.HBM)
MIB = 1024 * 1024
VMEM_LIMIT = 60 * MIB
SMALL_LIMIT = 12 * MIB


def launch(kernel, name, steps, in_specs, ins, out_specs, outs, scratch=()):
    grid = {"grid": (steps,), "in_specs": list(in_specs), "out_specs": list(out_specs)} if steps else {}
    return pl.pallas_call(
        kernel,
        out_shape=list(outs),
        scratch_shapes=list(scratch),
        compiler_params=pltpu.CompilerParams(vmem_limit_bytes=VMEM_LIMIT),
        name=name,
        **grid,
    )(*ins)


class First:
    def __init__(self, spans, x, halo, gain, wm, ws, pick, conv, bias, rate, flags, doc_rows, skip, ahead):
        rows = spans * SPAN
        early = lambda s: jnp.minimum(s, spans - 1)
        late = lambda s: jnp.maximum(s - spans, 0)
        both = lambda s: jnp.where(s >= spans, s - spans, s)
        block = lambda cols, at=early: spec((SPAN, cols), lambda s: (at(s), 0))
        span3 = lambda a, b, at=early: spec((1, a, b), lambda s: (at(s), 0, 0))
        self.ins = [x, halo, gain, wm, ws, pick, conv, bias, rate, flags, doc_rows, skip, ahead]
        self.in_specs = [
            block(D), whole(16, D), whole(1, D), whole(D, MAIN), whole(D, SHARED), whole(128, 128), whole(8, LOCAL),
            whole(1, 128), whole(1, 128), block(8, both), span3(1, SPAN, late), whole(1, WIDE), whole(*ahead.shape),
        ]
        self.out_specs = [
            block(D), block(WIDE), block(LOCAL), block(LOCAL), block(LOCAL), block(128), block(128),
            span3(NSTATE, WIDE), span3(8, WIDE), whole(8, LOCAL), block(WIDE, late),
        ]
        self.outs = [
            shape(rows, D, dtype=bf16), shape(rows, WIDE, dtype=bf16), shape(rows, LOCAL, dtype=bf16), shape(rows, LOCAL),
            shape(rows, LOCAL, dtype=bf16), shape(rows, 128), shape(rows, 128),
            shape(spans, NSTATE, WIDE), shape(spans, 8, WIDE), shape(8, LOCAL), shape(rows, WIDE),
        ]
        self.scratch = [
            pltpu.VMEM((SPAN + 8, LOCAL), f32), pltpu.VMEM((NSTATE, WIDE), f32), pltpu.VMEM((8, WIDE), f32),
            pltpu.VMEM((PACK, WIDE), f32), pltpu.VMEM((spans, SPAN, LOCAL), bf16), pltpu.VMEM((spans, SPAN, 128), f32),
            pltpu.VMEM((spans, SPAN, 128), f32),
        ]


def first_steps(step, spans, ins, outs, scratch):
    @pl.when(step == 0)
    def _():
        first_begin(*ins[1:5], outs[9], *scratch[:3])

    @pl.when(step < spans)
    def _():
        first_phase(step, *ins[:10], *outs[:10], *scratch)

    @pl.when(step >= spans)
    def _():
        within_phase(step - spans, *ins[9:12], outs[10], *scratch[4:])


def first_plain(spans, *refs):
    ins, outs, end, scratch = refs[:13], refs[13:24], refs[24], refs[25:]
    step = pl.program_id(0)
    first_steps(step, spans, ins, outs, scratch)

    @pl.when(step == spans - 1)
    def _():
        end[...] = scratch[3][...]


class Second:
    def __init__(self, spans, act, cum, flags, held, pref, incoming, part, gate, cot, wo, gain):
        rows = spans * SPAN
        block = lambda cols: spec((SPAN, cols), lambda s: (s, 0))
        span3 = lambda a, b: spec((1, a, b), lambda s: (s, 0, 0))
        self.ins = [act, cum, flags, held, pref, incoming, part, gate, cot, wo, gain]
        self.in_specs = [
            spec((SPAN, NSTATE), lambda s: (s, (WIDE + NSTATE) // NSTATE)), block(128), block(8), span3(NSTATE, WIDE),
            span3(8, WIDE), whole(NSTATE, WIDE), block(WIDE), block(WIDE), block(D), whole(WIDE, D), whole(1, WIDE),
        ]
        self.out_specs = [block(WIDE), block(WIDE)]
        self.outs = [shape(rows, WIDE, dtype=bf16), shape(rows, WIDE)]
        self.scratch = []


class Third:
    def __init__(self, spans, y, gate, gno, sums, act, cum, flags, gain, cot, wo, normed):
        rows = spans * SPAN
        back = lambda s: jnp.maximum(spans - 1 - s, 0)
        after = lambda s: jnp.maximum(s - spans, 0)
        block = lambda cols: spec((SPAN, cols), lambda s: (back(s), 0))
        later = lambda cols: spec((SPAN, cols), lambda s: (after(s), 0))
        span3 = lambda a, b: spec((1, a, b), lambda s: (back(s), 0, 0))
        self.later = later
        self.ins = [y, gate, gno, sums, act, cum, flags, gain, cot, wo, normed]
        self.in_specs = [
            block(WIDE), block(WIDE), block(WIDE), spec((PLANE, pl.squeezed, 2, SPAN), lambda s: (0, back(s), 0, 0)),
            block(LOCAL), block(128), block(8), whole(1, WIDE), later(D), whole(WIDE, D), later(D),
        ]
        self.out_specs = [block(WIDE), block(WIDE), span3(NSTATE, WIDE), span3(8, WIDE), whole(1, WIDE), whole(1, WIDE),
                          whole(WIDE, D), whole(WIDE, D)]
        self.outs = [
            shape(rows, WIDE, dtype=bf16), shape(rows, WIDE, dtype=bf16), shape(spans, NSTATE, WIDE),
            shape(spans, 8, WIDE), shape(1, WIDE), shape(1, WIDE), shape(WIDE, D), shape(WIDE, D),
        ]
        keep = pltpu.VMEM((spans, SPAN, WIDE), bf16)
        self.scratch = [pltpu.VMEM((NSTATE, WIDE), f32), pltpu.VMEM((8, WIDE), f32), keep, keep]


def third_plain(spans, *refs):
    ins, (gy, gg, behind, suff, gog, gskip, gout, ggw, start, mix), scratch = refs[:11], refs[11:21], refs[21:]
    step = pl.program_id(0)

    @pl.when(step == 0)
    def _():
        third_begin(gog, gskip, gout, ggw, *scratch[:2])

    @pl.when(step < spans)
    def _():
        third_first(step, *ins[:8], gy, gg, behind, suff, start, gog, gskip, *scratch)

    @pl.when(step >= spans)
    def _():
        third_second(step - spans, step - spans, *ins[8:], mix, gout, ggw, *scratch[2:])


class Fourth:
    def __init__(
        self, spans, act, dt, cum, flags, doc_rows, held, pref, incoming, behind, suff, ends, after_us, gy, pre,
        skip, rate,
    ):
        rows = spans * SPAN
        groups = ends.shape[0]
        block = lambda cols: spec((SPAN, cols), lambda s: (s, 0))
        span3 = lambda a, b: spec((1, a, b), lambda s: (s, 0, 0))
        self.ins = [act, dt, cum, flags, doc_rows, held, pref, incoming, behind, suff, ends, after_us, gy, pre, skip, rate]
        self.in_specs = [
            block(LOCAL), block(128), block(128), block(8), span3(1, SPAN), span3(NSTATE, WIDE),
            span3(8, WIDE), whole(NSTATE, WIDE), span3(NSTATE, WIDE), span3(8, WIDE), whole(groups, PACK, WIDE),
            whole(groups, 1, WIDE), block(WIDE), block(LOCAL), whole(1, WIDE), whole(1, 128),
        ]
        self.out_specs = [block(WIDE), whole(8, 128)]
        self.outs = [shape(rows + 8, WIDE), shape(8, 128)]
        self.scratch = [pltpu.VMEM((NSTATE, WIDE), f32)]


def fourth_plain(*refs):
    ins, (gpre, hsum, gst, gstep), scratch = refs[:16], refs[16:20], refs[20:]
    fourth_kernel(pl.program_id(0), *ins, gpre, gst, gstep, hsum, *scratch)


class Fifth:
    def __init__(self, spans, gpre, flags, chan, edge, conv, normed, gstate, gog, gskip, hsum, ggate, wm):
        rows = spans * SPAN
        block = lambda cols: spec((SPAN, cols), lambda s: (s, 0))
        self.ins = [gpre, flags, chan, edge, conv, normed, gstate, gog, gskip, hsum, ggate, wm]
        self.in_specs = [
            whole(rows + 8, WIDE), whole(rows + 8, 8), whole(rows, LOCAL), whole(8, LOCAL), whole(8, WIDE),
            block(D), whole(8, STATES), whole(1, WIDE), whole(1, WIDE), whole(8, 128), block(WIDE), whole(D, MAIN),
        ]
        self.outs = []
        self.scratch = [pltpu.VMEM((SPAN + 8, WIDE), f32)] * 2


def fifth_plain(spans, *refs):
    step = pl.program_id(0)
    ins, (gp, giw, small), (*scratch, ginner) = refs[:12], refs[12:15], refs[15:]

    @pl.when(step == 0)
    def _():
        fifth_begin(*ins[6:10], giw, small)

    fifth_kernel(step, *ins[:6], ginner, giw, small, *scratch)
    gp[...] = fifth_product(ins[10], ginner[...], ins[11])


def run_sixth(parts, tails, steps, flags, chan, edge, conv, x, gain):
    ins = [*parts, tails, steps, flags, chan, edge, conv, x, gain]
    return pl.pallas_call(
        functools.partial(sixth_kernel, len(parts)),
        in_specs=[IN_VMEM] * len(ins),
        out_shape=[shape(SPAN, SHARED, dtype=bf16), shape(8, STATES), shape(D, SHARED)],
        scratch_shapes=[pltpu.VMEM((SPAN + 8, STATES), f32)] * 3,
        compiler_params=pltpu.CompilerParams(vmem_limit_bytes=SMALL_LIMIT),
        name="conv_back_state",
    )(*ins)


def run_seventh(parts, mixes, gs, ws, x, cot, gain):
    ins = [*parts, *mixes, gs, ws, x, cot, gain]
    return pl.pallas_call(
        functools.partial(seventh_kernel, 0, len(parts), len(mixes)),
        in_specs=[IN_VMEM] * len(ins),
        out_shape=[shape(SPAN, D, dtype=bf16), shape(SPAN, D), shape(D // 128, 128)],
        compiler_params=pltpu.CompilerParams(vmem_limit_bytes=SMALL_LIMIT),
        name="token_gradient",
    )(*ins)


def run_adam(results, gate, inner, shared, gain, wi, mi, vi, wo, mo, vo, grads_out, spare):
    like = lambda a: shape(*a.shape)
    ins = [*spare, *results, gate, inner, shared, gain, wi, mi, vi, wo, mo, vo, *grads_out]
    return pl.pallas_call(
        functools.partial(adam_kernel, len(spare), len(grads_out)),
        in_specs=[IN_VMEM] * len(ins),
        out_shape=[like(wi), like(wi), like(wi), like(wo), like(wo), like(wo), shape(16, 128), shape(SPAN, D, dtype=bf16),
                   shape(SPAN, D)],
        scratch_shapes=[pltpu.VMEM(wi.shape, f32)],
        compiler_params=pltpu.CompilerParams(vmem_limit_bytes=SMALL_LIMIT),
        name="adam_terms",
    )(*ins)


def run_prep(groups, at, conv, head, gain):
    return pl.pallas_call(
        prep_kernel,
        in_specs=[pl.BlockSpec(memory_space=pltpu.SMEM)] + [pl.BlockSpec(memory_space=pltpu.VMEM)] * 3,
        out_shape=[shape(8, LOCAL), shape(1, 128), shape(1, 128), shape(1, WIDE), shape(1, WIDE),
                   shape(128, 128, dtype=bf16), shape(groups, 1, WIDE), shape(groups, 1, WIDE)],
        compiler_params=pltpu.CompilerParams(vmem_limit_bytes=VMEM_LIMIT),
        name="prepare",
    )(at, conv, head, gain)


def run_last(every, small, big, params):
    like = lambda a: shape(*a.shape)
    outs = [like(big[0]), like(big[2])]
    for weight in params[::3]:
        outs += [like(weight)] * 3
    return pl.pallas_call(
        last_kernel,
        out_shape=outs,
        scratch_shapes=[pltpu.VMEM((8, INNER + STATES), f32), pltpu.VMEM((INNER // 128, 128), f32)],
        compiler_params=pltpu.CompilerParams(vmem_limit_bytes=SMALL_LIMIT),
        name="lamb_apply",
    )(every, small, *big, *params)


MESH = pl.DeviceIdType.MESH


def bits(place):
    x = jnp.where(place >= 4, 1, 0)
    rest = place - 4 * x
    c = jnp.where(rest >= 2, 1, 0)
    return x, c, rest - 2 * c


class Here:
    def __init__(self):
        self.z = lax.axis_index("grp")
        self.sub = lax.axis_index("sub")
        self.y = lax.axis_index("seq")
        self.x = jnp.where(self.sub >= 2, 1, 0)
        self.c = self.sub - 2 * self.x
        self.t = self.sub * 2 + self.y

    def mate(self, o, up=0):
        x = 1 - self.x if o & 4 else self.x
        c = 1 - self.c if o & 2 else self.c
        y = 1 - self.y if o & 1 else self.y
        sub = x * 2 + c
        return (self.onward(up), sub, y), sub * 2 + y

    def onward(self, up):
        z = self.z + up
        return jnp.where(z >= 4, z - 4, z) if up else self.z

    def plane(self, up):
        return (self.onward(up), self.sub, self.y), self.onward(up)


CHIPS = (5, 4, 1)
CORE = 2


def near(h):
    return [h.mate(o)[0] for o in range(1, 8)]


def same_core(h):
    return [h.mate(o)[0] for o in CHIPS]


def line(h):
    return [h.plane(up)[0] for up in range(1, 4)]


def call(devices):
    barrier = pltpu.get_barrier_semaphore()
    for device in devices:
        pl.semaphore_signal(barrier, inc=1, device_id=device, device_id_type=MESH)
    return barrier


def greet(devices):
    pl.semaphore_wait(call(devices), len(devices))


def rows_at(ref, at, size):
    return ref.at[pl.ds(pl.multiple_of(at * size, size), size)]


class Wires:
    def __init__(self, send, recv, local, started=False):
        self.send_sem, self.recv_sem, self.local_sem = send, recv, local
        self.sent, self.kept, self.started = [], [], started

    def make(self, src, dst, i, device, j=None):
        return pltpu.make_async_remote_copy(
            src_ref=src, dst_ref=dst, send_sem=self.send_sem.at[i], recv_sem=self.recv_sem.at[i if j is None else j],
            device_id=device, device_id_type=MESH,
        )

    def send(self, src, dst, i, device):
        copy = self.make(src, dst, i, device)
        if not self.started:
            copy.start()
        self.sent.append(copy)

    def arrived(self, dst, i, device):
        self.make(dst, dst, i, device).wait_recv()

    def keep(self, src, dst):
        copy = pltpu.make_async_copy(src, dst, self.local_sem.at[len(self.kept)])
        if not self.started:
            copy.start()
        self.kept.append(copy)
        return copy

    def finish(self):
        for copy in self.sent:
            copy.wait_send()


def wires(copies, kept):
    return [pltpu.SemaphoreType.DMA((copies,)), pltpu.SemaphoreType.DMA((copies,)), pltpu.SemaphoreType.DMA((kept,))]


def talk(kernel, number, name, outs, ins, scratch):
    return pl.pallas_call(
        kernel,
        in_specs=[IN_VMEM] * len(ins),
        out_specs=[IN_VMEM] * len(outs),
        out_shape=outs,
        scratch_shapes=scratch,
        compiler_params=pltpu.CompilerParams(collective_id=number, has_side_effects=True, vmem_limit_bytes=SMALL_LIMIT),
        name=name,
    )(*ins)


class Relay:
    def __init__(self, h, w, base, block):
        self.h, self.w, self.base, self.block = h, w, base, block

    def copies(self, hop):
        h = self.h
        above, below = h.plane(1)[0], h.plane(3)[0]
        up = self.w.make, jnp.maximum(h.z - hop + 1, 0), self.base + hop, above
        down = self.w.make, jnp.minimum(h.z + hop - 1, 3), self.base + 4 + hop, below
        yield (h.z < 3) & (h.z >= hop - 1), up, h.z >= hop, jnp.maximum(h.z - hop, 0), below
        yield (h.z > 0) & (h.z <= 4 - hop), down, h.z <= 3 - hop, jnp.minimum(h.z + hop, 3), above

    def first(self):
        for sends, (make, z, i, device), *_ in self.copies(1):

            @pl.when(sends)
            def _():
                make(self.block(z), self.block(z), i, device).start()

    def onward(self, hop):
        for _, (_, _, i, _), comes, z, device in self.copies(hop):

            @pl.when(comes)
            def _():
                self.w.arrived(self.block(z), i, device)

        if hop < 3:
            for sends, (make, z, i, device), *_ in self.copies(hop + 1):

                @pl.when(sends)
                def _():
                    make(self.block(z), self.block(z), i, device).start()

    def finish(self):
        for hop in range(1, 4):
            for sends, (make, z, i, device), *_ in self.copies(hop):

                @pl.when(sends)
                def _():
                    make(self.block(z), self.block(z), i, device).wait_send()


def start_kernel(wi_in, wo_in, tok, docs_in, conv_in, head_in, gain_in, norm_in, *refs):
    (wm, ws, x, halo), outputs, (flags, doc_rows, out_low, norm), refs = refs[:4], refs[4:12], refs[12:16], refs[16:]
    (wi, wo, docs, conv, head, gain, main, shared), sems = refs[:8], refs[8:]
    h = Here()
    w = Wires(*sems)
    near_x, near_y, mate = [h.mate(o)[0] for o in (4, 1, CORE)]
    friends = near(h) + line(h)
    barrier = call(friends)
    loads = [w.keep(wi_in, wi), w.keep(wo_in, wo)]
    loads += [w.keep(*pair) for pair in ((docs_in, docs), (conv_in, conv), (head_in, head), (gain_in, gain), (norm_in, norm))]
    own = w.keep(tok, rows_at(x, h.t, SPAN))
    loads[0].wait()
    loads[1].wait()
    pack_kernel(wi, wo, main, shared, out_low)
    pl.semaphore_wait(barrier, len(friends))

    in_rows = lambda place: wm.at[pl.ds(pl.multiple_of(h.z * SPAN + place * 32, 32), 32)]
    keep = [w.keep(main.at[h.t], in_rows(h.t)), w.keep(shared, ws.at[h.z, h.t])]
    for o in range(1, 8):
        device, place = h.mate(o)
        w.send(main.at[place], in_rows(h.t), o, device)
    for up in range(1, 4):
        w.send(shared, ws.at[h.z, h.t], 10 + up, h.plane(up)[0])
    block = lambda o: rows_at(x, h.mate(o)[1], SPAN)
    w.send(tok, block(0), 21, near_x)
    w.send(tok, block(0), 22, near_y)
    w.send(tok, block(0), 23, mate)
    for copy in loads[2:]:
        copy.wait()
    prepare(h.z, h.t, conv, head, gain, *outputs)
    flags_of(h.z, docs, flags, doc_rows)
    keep[0].wait()
    for o in range(1, 8):
        device, place = h.mate(o)
        w.arrived(in_rows(place), o, device)
    relay = Relay(h, w, 30, lambda z: rows_at(wm, z, SPAN))
    relay.first()
    keep[1].wait()
    for up in range(1, 4):
        device, z = h.plane(4 - up)
        w.arrived(ws.at[z, h.t], 10 + up, device)
    for i, o in enumerate(CHIPS):
        w.send(ws.at[:, h.t], ws.at[:, h.t], 40 + i, h.mate(o)[0])
    w.send(ws.at[:, h.t], ws.at[:, h.t], 43, mate)
    half = SPAN // 2
    upper, lower = pl.ds(0, half), pl.ds(half, half)
    relay.onward(1)
    w.arrived(block(4), 21, near_x)
    w.send(block(4).at[upper], block(4).at[upper], 20, near_y)
    w.send(block(4), block(4), 25, mate)
    w.arrived(block(1), 22, near_y)
    w.send(block(1).at[lower], block(1).at[lower], 27, near_x)
    w.send(block(1), block(1), 26, mate)
    for i, o in enumerate(CHIPS):
        device, place = h.mate(o)
        w.arrived(ws.at[:, place], 40 + i, device)
        w.send(ws.at[:, place], ws.at[:, place], 44 + i, mate)
    relay.onward(2)
    w.arrived(block(5).at[upper], 20, near_y)
    w.arrived(block(5).at[lower], 27, near_x)
    w.send(block(5), block(5), 24, mate)
    own.wait()
    w.arrived(block(CORE), 23, mate)
    w.arrived(ws.at[:, h.mate(CORE)[1]], 43, mate)
    for i, o in enumerate(CHIPS):
        w.arrived(block(o ^ CORE), 24 + i, mate)
    w.send(x.at[pl.ds(PLANE * SPAN - 16, 16)], halo, 50, h.plane(1)[0])
    for i, o in enumerate(CHIPS):
        w.arrived(ws.at[:, h.mate(o ^ CORE)[1]], 44 + i, mate)
    relay.onward(3)
    relay.finish()
    w.arrived(halo, 50, h.plane(3)[0])
    w.finish()


class Chain:
    def __init__(self, h, w, ends, low, lows, reverse):
        self.h, self.w, self.ends, self.low, self.lows = h, w, ends, low, lows
        self.hops = []
        for up in range(1, 4):
            ahead = 4 - up if reverse else up
            goes = h.z >= up if reverse else h.z < 4 - up
            comes = h.z < 4 - up if reverse else h.z >= up
            self.hops.append((up, goes, h.plane(ahead)[0], comes, *h.plane(4 - ahead)))

    def copy(self, up, device):
        z = self.h.z
        if up == 1:
            return self.w.make(self.ends.at[z], self.ends.at[z], up, device)
        return self.w.make(self.low, self.lows.at[z], up, device)

    def start(self):
        self.low[...] = self.ends[self.h.z].astype(bf16)
        for up, goes, device, *_ in self.hops:

            @pl.when(goes)
            def _():
                self.copy(up, device).start()

    def wait(self):
        for up, goes, device, comes, back, z in self.hops:

            @pl.when(comes)
            def _():
                self.w.arrived((self.lows if up > 1 else self.ends).at[z], up, back)
                if up > 1:
                    self.ends[z] = self.lows[z].astype(f32)

            @pl.when(goes)
            def _():
                self.copy(up, device).wait_send()


def first_direct(work, *refs):
    ins, (out, cot), refs = refs[:13], refs[13:15], refs[15:]
    outs, (inc, g, wo), refs = refs[:11], refs[11:14], refs[14:]
    (ext, state, decay, ends, low, lows), sems = refs[:6], refs[6:]
    h = Here()
    w = Wires(*sems)
    local = sems[2]
    mate, _ = h.mate(CORE)
    end = ends.at[h.z]
    spans = PLANE
    rows_of = [Rows(outs[i]) for i in (4, 5, 6)]

    greet(line(h) + same_core(h) + [mate])
    rows = [w.make(out, rows_at(wo, h.z, HEAD_DIM), 8 + up, h.plane(up)[0]) for up in range(1, 4)]
    block = lambda o: rows_at(g, h.mate(o)[1], SPAN)
    across = [w.make(cot, block(0), 4 + i, h.mate(o)[0]) for i, o in enumerate(CHIPS)]
    for copy in (*rows, *across):
        copy.start()
    loads = [pltpu.make_async_copy(cot, block(0), local.at[0]),
             pltpu.make_async_copy(out, rows_at(wo, h.z, HEAD_DIM), local.at[1])]
    for copy in loads:
        copy.start()
    first_begin(*ins[1:5], outs[9], ext, state, decay)

    @pl.loop(0, spans, unroll=2)
    def _(step):
        taken = views(work.in_specs[:10], ins, step)
        given = views(work.out_specs[:10], outs, step)
        first_phase(step, *taken, *given, ext, state, decay, end, *rows_of)

    chain = Chain(h, w, ends, low, lows, False)
    chain.start()
    over = [w.make(block(o), block(o), 12 + i, mate) for i, o in enumerate((*CHIPS, 0))]

    def within(span):
        taken = views(work.in_specs[9:12], ins[9:12], span + spans)
        within_phase(span, *taken, view(work.out_specs[10], outs[10], span + spans), *rows_of)

    pl.loop(0, spans // 2, unroll=2)(within)
    loads[0].wait()
    over[3].start()
    for i, o in enumerate(CHIPS):
        across[i].wait_send()
        w.arrived(block(o), 4 + i, h.mate(o)[0])
        over[i].start()
    pl.loop(spans // 2, spans, unroll=2)(within)
    for i, o in enumerate((*CHIPS, 0)):
        over[i].wait_send()
        w.arrived(block(o ^ CORE), 12 + i, mate)
    for up in range(1, 4):
        rows[up - 1].wait_send()
        w.arrived(rows_at(wo, h.onward(4 - up), HEAD_DIM), 8 + up, h.plane(4 - up)[0])
    loads[1].wait()
    chain.wait()
    carry_chain(ends, ins[12], inc, False)


def turn(step):
    h = Here()
    a, b, e = bits(7 - step)
    x, c, y = h.x + a - 2 * h.x * a, h.c + e - 2 * h.c * e, h.y + b - 2 * h.y * b
    return x * 4 + c * 2 + y


class Across:
    def __init__(self, h, w, base, block, upper, lower):
        self.w, self.base, self.block, self.upper, self.lower = w, base, block, upper, lower
        self.near_x, self.near_y = h.mate(4)[0], h.mate(1)[0]

    def copies(self):
        half = SPAN // 2
        return (
            self.w.make(self.block.at[0:half], self.upper, self.base, self.near_x),
            self.w.make(self.block.at[half:SPAN], self.lower, self.base + 1, self.near_y),
        )

    def start(self):
        for copy in self.copies():
            copy.start()

    def extra(self, i):
        if i == 1:
            self.w.arrived(self.lower, self.base + 1, self.near_y)
            return 1, self.lower
        self.w.arrived(self.upper, self.base, self.near_x)
        return 0, self.upper

    def last(self):
        for copy in self.copies():
            copy.wait_send()


class Fold:
    def __init__(self, h, w, base, blocks, inbox, outbox, total, across, deliver=None):
        self.h, self.w, self.base, self.deliver = h, w, base, deliver
        self.blocks, self.inbox, self.outbox, self.total, self.across = blocks, inbox, outbox, total, across
        self.mate, _ = h.mate(CORE)
        self.slots = blocks.shape[0]

    def sent(self, i):
        self.w.make(self.inbox.at[i], self.inbox.at[i], self.base + i, self.mate).wait_send()

    def slot(self, step):
        for i in (2, 3):

            @pl.when(step == 2 * i)
            def _():
                self.sent(i - 2)

        return jnp.where(step >= 4, step - 4, step) if self.slots == 4 else step

    def each(self, get, put, extra=None):
        for half in range(2):

            @pl.loop(0, SPAN // 2, step=32)
            def _(row):
                rows = pl.ds(pl.multiple_of(row + half * (SPAN // 2), 32), 32)
                value = get(rows)
                if extra is not None and extra[0] == half:
                    value = value + extra[1][pl.ds(pl.multiple_of(row, 32), 32), :].astype(f32)
                put(rows, value)

    def add(self, pair, put, extra=None):
        slot = (2 * pair + 1) % self.slots
        self.each(lambda rows: self.blocks[slot, rows, :] + self.inbox[pair, rows, :], put, extra)

    def settle(self, i):
        self.w.arrived(self.inbox.at[i], self.base + i, self.mate)
        if i == 0:
            self.add(0, put_in(self.across.block))
            self.across.start()
        elif self.outbox is None:
            self.add(i, put_in(self.inbox, i))
        else:
            self.add(i, put_in(self.outbox, i - 1), self.across.extra(i))
            self.deliver(i - 1)

    def collect(self, held):
        for i in (1, 2):
            self.each(lambda rows: self.inbox[i, rows, :], put_in(held, i - 1), self.across.extra(i))

    def step(self, step, early=0):
        for i in range(4):

            @pl.when(step == 2 * i)
            def _():
                self.w.make(self.blocks.at[2 * i % self.slots], self.inbox.at[i], self.base + i, self.mate).start()
                if i > early:
                    self.settle(i - 1)

    def last(self):
        self.w.arrived(self.inbox.at[3], self.base + 3, self.mate)
        self.add(3, put_in(self.total))
        self.sent(2)
        self.sent(3)
        self.across.last()


class ToChips:
    def __init__(self, h, w, base, outbox, results):
        self.copies = [w.make(outbox.at[i], results.at[i], base + i, h.mate(o)[0]) for i, o in enumerate(CHIPS[1:])]

    def __call__(self, i):
        self.copies[i].start()

    def last(self):
        for copy in self.copies:
            copy.wait()


def head_rows(ref, z):
    return rows_at(ref, z, HEAD_DIM)


def lanes_at(ref, z):
    return ref.at[:, pl.ds(pl.multiple_of(z * SPAN, SPAN), SPAN)]


class Planes:
    def __init__(self, h, w, base, full, low, piece, near, far):
        self.copies = []
        for up in range(1, 4):
            device, z = h.plane(up)
            wide = near is not None and functools.partial(w.make, piece(full, z), near.at[up // 2], base + up, device)
            slim = functools.partial(w.make, piece(low, z), far.at[up - 1], base + up, device)
            to_near = {1: h.z < 3, 2: None, 3: h.z > 0}[up] if near is not None else None
            from_near = {1: h.z > 0, 2: None, 3: h.z < 3}[up] if near is not None else None
            self.copies.append((wide, slim, to_near, from_near))

    def each(self, near, act_wide, act_slim):
        if near is None:
            act_slim()
            return

        @pl.when(near)
        def _():
            act_wide()

        @pl.when(jnp.logical_not(near))
        def _():
            act_slim()

    def start(self):
        for wide, slim, to_near, _ in self.copies:
            self.each(to_near, lambda: wide().start(), lambda: slim().start())

    def wait(self):
        for wide, slim, to_near, from_near in self.copies:
            self.each(to_near, lambda: wide().wait_send(), lambda: slim().wait_send())
            self.each(from_near, lambda: wide().wait_recv(), lambda: slim().wait_recv())


def put_in(ref, *at):
    def put(rows, value):
        ref[(*at, rows, slice(None))] = value.astype(ref.dtype)

    return put


def third_direct(work, *refs):
    second, third = work.second, work
    ins, normed, refs = refs[:11], refs[11], refs[12:]
    (gy, gg, behind, suff, gog, gskip, gout, ggw), (ends, chip, held) = refs[:8], refs[8:11]
    (blocks, inbox, state, decay, no_all, every, low, lows), sems = refs[11:19], refs[19:]
    act, cum, flags, _, _, _, _, gate, cot, wo, gain = ins
    h = Here()
    w = Wires(*sems)
    spans = PLANE
    start = ends.at[h.z]
    gates = Rows(gg)

    def gno(span):
        late = jnp.where(span >= 4, 1, 0)
        return blocks.at[span - 4 * late, :, pl.ds(pl.multiple_of(late * WIDE, WIDE), WIDE)]

    greet(near(h) + line(h))
    mine = every.at[h.t]
    third_begin(gog, gskip, gout, ggw, state, decay)

    @pl.loop(0, spans, unroll=2)
    def _(step):
        taken = views(second.in_specs, ins, step)
        second_kernel(*taken, view(second.out_specs[0], gy, step), gno(step), mine.at[pl.ds(step, 1)])

    for o in range(1, 8):
        w.send(mine, every.at[h.t], 10 + o, h.mate(o)[0])
    for o in range(1, 8):
        device, place = h.mate(o)
        w.arrived(every.at[place], 10 + o, device)

    taking = (gy, gate, None, every, act, cum, flags, gain, cot, wo, normed)

    @pl.loop(0, spans, unroll=2)
    def _(step):
        taken = [gno(spans - 1 - step) if i == 2 else view(third.in_specs[i], taking[i], step) for i in range(8)]
        one, two, three, four = views(third.out_specs[:4], (gy, gg, behind, suff), step)
        third_first(step, *taken, one, two, three, four, start, gog, gskip, state, decay, no_all, gates)

    chain = Chain(h, w, ends, low, lows, True)
    chain.start()
    half = SPAN // 2
    across = Across(h, w, 8, held.at[0], held.at[1, 0:half], held.at[1, half:SPAN])
    fold = Fold(h, w, 4, blocks, inbox, None, chip, across)

    @pl.loop(0, spans)
    def _(span):
        taken = views(third.in_specs[8:], taking[8:], span + spans)
        third_second(span, turn(span), *taken, blocks.at[fold.slot(span)], gout, ggw, no_all, gates)
        fold.step(span)

    fold.last()
    chain.wait()
    fold.collect(held)
    w.finish()


def fourth_direct(work, *refs):
    ins, (held, ggw), refs = refs[:16], refs[16:18], refs[18:]
    (gpre, hsum), (rmix, near_gate, far_gate) = refs[:2], refs[2:5]
    (parts, total, tails, steps), refs = refs[5:9], refs[9:]
    (out, blocks, inbox, outbox, gstep, edge, cross, upper, lower, ggw_low), sems = refs[:10], refs[10:]
    h = Here()
    w = Wires(*sems)
    local = sems[2]
    spans = PLANE
    below = h.plane(3)[0]
    corner = (h.onward(3), 3, 1)
    after = gpre.at[pl.ds(PLANE * SPAN, 8)]
    gate_planes = Planes(h, w, 32, ggw, ggw_low, lanes_at, near_gate, far_gate)

    def to_place(src, dst, base, keep, place):
        @pl.when(place != h.t)
        def _():
            x, c, y = bits(place)
            device = (h.z, 2 * x + c, y)
            w.make(src, dst, base + place, device, base + h.t).start()

        @pl.when(place == h.t)
        def _():
            pltpu.make_async_copy(src, dst, local.at[keep]).start()

    friends = near(h) + line(h)
    barrier = call(friends)

    @pl.when(h.t == 7)
    def _():
        call([h.mate(o, 1)[0] for o in range(8)])

    ggw_low[...] = ggw[...].astype(bf16)
    pl.semaphore_wait(barrier, len(friends) + 1)
    gate_planes.start()
    branch = [w.make(held.at[i], rmix.at[i], 12 + i, h.mate(o)[0]) for i, o in enumerate(CHIPS[1:])]
    for copy in branch:
        copy.start()
    chips = ToChips(h, w, 8, outbox, parts)
    fold = Fold(h, w, 4, blocks, inbox, outbox, total, Across(h, w, 10, cross, upper, lower), chips)

    @pl.loop(0, spans)
    def _(step):
        place = turn(step)
        taken = views(work.in_specs, ins, place)
        mine = view(work.out_specs[0], gpre, place)
        fourth_kernel(step, *taken, mine, blocks.at[fold.slot(step)], gstep.at[step], hsum, out)
        fold.step(step)
        to_place(gstep.at[step], steps.at[h.t], 16, 1, place)

        @pl.when(place == 0)
        def _():
            edge[...] = mine[0:8, :]
            w.make(edge, after, 14, below).start()
            w.make(blocks.at[step, 0:8], tails.at[h.t], 31, corner, 24 + h.t).start()

        @pl.when(place > 0)
        def _():
            to_place(blocks.at[step, 0:8], tails.at[h.t], 24, 2, place - 1)

    fold.last()
    gate_planes.wait()
    for copy in branch:
        copy.wait()
    w.make(edge, after, 14, below).wait()
    rows = blocks.at[0, 0:8]
    for place in range(PLANE):
        device = (h.z, place // 2, place % 2)

        @pl.when(place != h.t)
        def _():
            w.make(gstep.at[0], steps.at[place], 16 + place, device).wait()

        @pl.when((place != h.t) | (h.t == 7))
        def _():
            w.arrived(tails.at[place], 24 + place, device)

        @pl.when((place != h.t) | (place == 7))
        def _():
            w.make(rows, tails.at[place], 24 + place, device).wait_send()

    pltpu.make_async_copy(gstep.at[0], steps.at[h.t], local.at[1]).wait()

    @pl.when(h.t < 7)
    def _():
        pltpu.make_async_copy(rows, tails.at[h.t], local.at[2]).wait()

    chips.last()


def fifth_direct(work, *refs):
    ins, (ggw, near_gate, far_gate, gstate, gout), rest, refs = refs[:12], refs[12:17], refs[17:24], refs[24:]
    (pgate, pinner, ps, psmall, near_out, far_out, mixed, gtok, gain), refs = refs[:9], refs[9:]
    (blocks, inbox, outbox, rgp, chip), scratch, (ginner, giw, giw_low, small) = refs[:5], refs[5:7], refs[7:11]
    (far_inner, zsum, gatesum, state_in, state_low, state_got), refs = refs[11:17], refs[17:]
    (ssum, rsmall, smallsum, cross, upper, lower, gout_low), sems = refs[:7], refs[7:]
    h = Here()
    w = Wires(*sems)
    local = sems[2]
    spans = PLANE
    mate, _ = h.mate(CORE)

    friends = near(h) + line(h)
    barrier = call(friends)
    lanes = pl.ds(pl.multiple_of(h.z * SPAN, SPAN), SPAN)
    gatesum[...] = from_planes(h.z, ggw[:, lanes], near_gate, far_gate).T
    gout_low[...] = gout[...].astype(bf16)
    pl.semaphore_wait(barrier, len(friends))
    out_planes = Planes(h, w, 0, gout, gout_low, head_rows, near_out, far_out)
    out_planes.start()
    state = []
    for i, o in enumerate((*CHIPS, 0)):
        near_core = w.make(gstate.at[:, h.mate(o ^ CORE)[1]], state_in.at[i], 24 + i, mate)
        on = w.make(state_low.at[i], state_got.at[i], 28 + i, h.mate(o)[0]) if o else None
        state.append((near_core, on))
        near_core.start()
    for o in range(1, 8):
        device, place = h.mate(o)
        w.send(rows_at(gatesum, place, 32), pgate.at[h.t], 44 + o, device)
    keep = [w.keep(rows_at(gatesum, h.t, 32), pgate.at[h.t])]
    chips = ToChips(h, w, 8, outbox, rgp)
    fold = Fold(h, w, 4, blocks, inbox, outbox, chip, Across(h, w, 10, cross, upper, lower), chips)

    def conv_step(step):
        place = turn(step)
        taken = views(work.in_specs[:6], ins, place)
        fifth_kernel(place, *taken, ginner.at[step], giw, small, *scratch)

    def block_step(step):
        taken = views(work.in_specs[10:], ins[10:], turn(step))
        blocks[fold.slot(step)] = fifth_product(taken[0], ginner[step], taken[1])
        fold.step(step, early=1)

    fifth_begin(*ins[6:10], giw, small)

    @pl.loop(0, 2)
    def _(step):
        conv_step(step)
        block_step(step)

    for i, (o, (near_core, on)) in enumerate(zip((*CHIPS, 0), state)):
        near_core.wait()
        both = gstate[:, h.mate(o)[1]] + state_in[i]
        if on is None:
            ssum[...] = both
        else:
            state_low[i] = both.astype(bf16)
            on.start()

    pl.loop(2, 4)(conv_step)
    fold.settle(0)
    pl.loop(4, spans)(conv_step)

    giw_low[...] = giw[...].astype(bf16)
    inner_planes = Planes(h, w, 16, giw, giw_low, lanes_at, None, far_inner)
    inner_planes.start()
    for up in range(1, 4):
        w.send(small, rsmall.at[h.z], 20 + up, h.plane(up)[0])
    keep_small = w.keep(small, rsmall.at[h.z])
    pl.loop(2, spans)(block_step)
    fold.last()

    for _, on in state[:3]:
        on.wait()
    ssum[...] = ssum[...] + jnp.sum(state_got[...].astype(f32), axis=0)
    for up in range(1, 4):
        device, z = h.plane(up)
        w.send(ssum.at[z], ps.at[h.z], 32 + up, device)
    keep.append(w.keep(ssum.at[h.z], ps.at[h.z]))

    keep_small.wait()
    for up in range(1, 4):
        device, z = h.plane(4 - up)
        w.arrived(rsmall.at[z], 20 + up, device)
    smallsum[...] = jnp.sum(rsmall[...], axis=0)
    for i, o in enumerate((*CHIPS, CORE)):
        w.send(smallsum, psmall.at[h.t], 36 + i, h.mate(o)[0])
    keep.append(w.keep(smallsum, psmall.at[h.t]))

    inner_planes.wait()
    zsum[...] = (giw[:, lanes] + jnp.sum(far_inner[...].astype(f32), axis=0)).T
    for o in range(1, 8):
        device, place = h.mate(o)
        w.send(rows_at(zsum, place, 32), pinner.at[h.t], 52 + o, device)
    keep.append(w.keep(rows_at(zsum, h.t, 32), pinner.at[h.t]))
    chips.last()
    seventh_kernel(0, 2, 2, chip, rgp, *rest, mixed, gtok, gain)

    for i, o in enumerate(CHIPS):
        device, place = h.mate(o)
        w.arrived(psmall.at[place], 36 + i, device)
        w.send(psmall.at[place], psmall.at[place], 40 + i, mate)
    w.arrived(psmall.at[h.mate(CORE)[1]], 39, mate)
    for i, o in enumerate(CHIPS):
        w.arrived(psmall.at[h.mate(o ^ CORE)[1]], 40 + i, mate)
    for o in range(1, 8):
        device, place = h.mate(o)
        w.arrived(pgate.at[place], 44 + o, device)
        w.arrived(pinner.at[place], 52 + o, device)
    for up in range(1, 4):
        device, z = h.plane(4 - up)
        w.arrived(ps.at[z], 32 + up, device)
    out_planes.wait()
    for copy in keep:
        copy.wait()
    w.finish()


def view(block, ref, step):
    if block.block_shape is None:
        return ref
    cuts, full = [], True
    for at, size, total in zip(block.index_map(step), block.block_shape, ref.shape):
        if size is pl.squeezed:
            cuts.append(at)
        elif size == total:
            cuts.append(slice(None))
            continue
        else:
            cuts.append(pl.ds(at * size if isinstance(at, int) else pl.multiple_of(at * size, size), size))
        full = False
    return ref if full else ref.at[tuple(cuts)]


def views(blocks, refs, step):
    return [view(block, ref, step) for block, ref in zip(blocks, refs)]


class Rows:
    def __init__(self, ref):
        self.ref = ref

    def __getitem__(self, span):
        return self.ref[pl.ds(pl.multiple_of(span * SPAN, SPAN), SPAN), :]

    def __setitem__(self, span, value):
        pass


def kept(dims, dtype=f32):
    return pltpu.VMEM(dims, dtype)


def flat(kernel, number, name, work, ins, outs, scratch, far=()):
    shapes = [*[kept(a.shape, a.dtype) for a in work.outs], *outs]
    return pl.pallas_call(
        functools.partial(kernel, work),
        in_specs=[IN_VMEM] * (len(work.ins) + len(ins)) + [IN_HBM] * len(far),
        out_specs=[IN_VMEM] * len(shapes),
        out_shape=shapes,
        scratch_shapes=scratch,
        compiler_params=pltpu.CompilerParams(
            collective_id=number, has_side_effects=True, vmem_limit_bytes=SMALL_LIMIT
        ),
        name=name,
    )(*work.ins, *ins, *[pltpu.with_memory_space_constraint(a, pltpu.HBM) for a in far])


def total_kernel(mine, every, planes, lines, send, recv, local):
    h = Here()
    w = Wires(send, recv, local)
    greet(near(h) + line(h))
    keep = w.keep(mine, planes.at[h.z])
    for up in range(1, 4):
        w.send(mine, planes.at[h.z], up, h.plane(up)[0])
    keep.wait()
    for up in range(1, 4):
        device, z = h.plane(4 - up)
        w.arrived(planes.at[z], up, device)
    lines[...] = jnp.sum(planes[...], axis=0)
    for o in range(1, 8):
        w.send(lines, every.at[h.t], 3 + o, h.mate(o)[0])
    keep = w.keep(lines, every.at[h.t])
    for o in range(1, 8):
        device, place = h.mate(o)
        w.arrived(every.at[place], 3 + o, device)
    keep.wait()
    w.finish()


def vmem(*dims, dtype=f32):
    return pltpu.VMEM(dims, dtype)


class Direct:
    @staticmethod
    def start(in_weight, out_weight, tokens, docs, conv, head, gain, norm):
        rows = PLANE * SPAN
        outs = [kept((D, MAIN), bf16), kept((4, PLANE, 32, SHARED), bf16), kept((rows, D), bf16), kept((16, D), bf16),
                kept((8, LOCAL)), kept((1, 128)), kept((1, 128)), kept((1, WIDE)), kept((1, WIDE)),
                kept((128, 128), bf16), kept((4, 1, WIDE)), kept((4, 1, WIDE)), kept((rows + 8, 8)),
                kept((PLANE, 1, SPAN)), kept(out_weight.shape, bf16), kept((1, D))]
        ins = [in_weight, out_weight, tokens, docs.reshape(-1, 128), conv, head, gain, norm]
        ins = [pltpu.with_memory_space_constraint(a, pltpu.HBM) for a in ins]
        loaded = [ins[i] for i in (0, 1, 3, 4, 5, 6)]
        wm, ws, x, halo, *prepared, flags, doc_rows, out_low, norm = pl.pallas_call(
            start_kernel,
            in_specs=[IN_HBM] * len(ins),
            out_specs=[IN_VMEM] * len(outs),
            out_shape=outs,
            scratch_shapes=[*[pltpu.VMEM(a.shape, a.dtype) for a in loaded], vmem(PLANE, 32, MAIN, dtype=bf16),
                            vmem(32, SHARED, dtype=bf16)] + wires(51, 10),
            compiler_params=pltpu.CompilerParams(collective_id=0, has_side_effects=True, vmem_limit_bytes=SMALL_LIMIT),
            name="gather_start",
        )(*ins)
        return wm, ws.reshape(D, SHARED), x, halo, prepared, flags, doc_rows, out_low, norm

    @staticmethod
    def first(spans, work, cotangent, out):
        rows = spans * SPAN
        return flat(
            first_direct, 1, "project_scan", work, [out],
            [kept((NSTATE, WIDE)), kept((rows, D), bf16), kept((WIDE, D), bf16)],
            [*work.scratch[:3], vmem(4, PACK, WIDE), vmem(PACK, WIDE, dtype=bf16), vmem(4, PACK, WIDE, dtype=bf16)]
            + wires(16, 2), [cotangent],
        )

    @staticmethod
    def second(spans, work):
        return work, None, None

    @staticmethod
    def third(spans, work):
        work.second, normed = work.ins[0], work.ins[10]
        work.ins = [*work.second.ins, normed]
        *outs, gout, ggw, ends, chip, held = flat(
            third_direct, 4, "carry_gate_back", work, [],
            [kept((4, PACK, WIDE)), kept((SPAN, D)), kept((2, SPAN, D), bf16)],
            [vmem(4, SPAN, D), vmem(4, SPAN, D), *work.scratch[:3], vmem(PLANE, spans, 2, SPAN),
             vmem(PACK, WIDE, dtype=bf16), vmem(4, PACK, WIDE, dtype=bf16)] + wires(18, 1),
        )
        return *outs, gout, ggw, ends, (chip, held)

    @staticmethod
    def fourth(spans, work, gout, ggw, mix):
        chip, held = mix
        gpre, hsum, rmix, near_gate, far_gate, parts, own, tails, steps = flat(
            fourth_direct, 5, "scan_back", work, [held, ggw],
            [kept((2, SPAN, D), bf16), kept((2, WIDE, SPAN)),
             kept((3, WIDE, SPAN), bf16), kept((2, SPAN, STATES), bf16), kept((SPAN, STATES)), kept((PLANE, 8, STATES)),
             kept((PLANE, 8, SPAN))],
            [*work.scratch, vmem(PLANE, SPAN, STATES), vmem(4, SPAN, STATES), vmem(2, SPAN, STATES, dtype=bf16), vmem(spans, 8, SPAN),
             vmem(8, WIDE), vmem(SPAN, STATES, dtype=bf16), vmem(SPAN // 2, STATES, dtype=bf16),
             vmem(SPAN // 2, STATES, dtype=bf16), vmem(WIDE, D, dtype=bf16)] + wires(36, 3),
        )
        ggw = [ggw, near_gate, far_gate]
        return gpre, hsum, [parts, own], tails, steps, gout, [chip, rmix], ggw

    @staticmethod
    def fifth(spans, work, ggw, grad_state, gout, rest):
        piece = vmem(4, 4, 32, SHARED)
        mix, *rest = rest
        pgate, pinner, ps, psmall, near_out, far_out, *tokens_back = flat(
            fifth_direct, 6, "conv_back_reduce", work, [*ggw, grad_state.reshape(4, PLANE, 32, SHARED), gout, *mix, *rest],
            [kept((PLANE, 32, WIDE)), kept((PLANE, 32, WIDE)), kept((4, 32, SHARED)), kept((PLANE, SMALL, WIDE)),
             kept((2, HEAD_DIM, D)), kept((3, HEAD_DIM, D), bf16), kept((SPAN, D), bf16), kept((SPAN, D)),
             kept((D // 128, 128)), kept((4, SPAN, D)), kept((4, SPAN, D)), kept((2, SPAN, D), bf16),
             kept((2, SPAN, D), bf16), kept((SPAN, D))],
            [*work.scratch, vmem(spans, SPAN, WIDE, dtype=bf16), vmem(WIDE, D), vmem(WIDE, D, dtype=bf16),
             vmem(SMALL, WIDE), vmem(3, SPAN, WIDE, dtype=bf16),
             vmem(SPAN, WIDE), vmem(SPAN, WIDE), piece, vmem(3, 4, 32, SHARED, dtype=bf16),
             vmem(3, 4, 32, SHARED, dtype=bf16), vmem(4, 32, SHARED),
             vmem(4, SMALL, WIDE), vmem(SMALL, WIDE), vmem(SPAN, D, dtype=bf16), vmem(SPAN // 2, D, dtype=bf16),
             vmem(SPAN // 2, D, dtype=bf16), vmem(WIDE, D, dtype=bf16)] + wires(60, 5),
        )
        return pgate, pinner, ps, tokens_back[:3], psmall, tokens_back[3:], [gout, near_out, far_out]

    @staticmethod
    def total(part):
        return talk(
            total_kernel, 9, "sum_all", [kept((PLANE, *part.shape))], [part],
            [vmem(4, *part.shape), vmem(*part.shape)] + wires(11, 2),
        )[0]


class Plain:
    @staticmethod
    def start(in_weight, out_weight, tokens, docs, conv, head, gain, norm):
        main, shared, out_low = run_pack(in_weight, out_weight)
        rows = main.shape[1]
        main = lax.all_to_all(main, TP, split_axis=0, concat_axis=0, tiled=True)
        main = lax.all_gather(main.reshape(PLANE * rows, MAIN), "grp", axis=0, tiled=True)
        shared = lax.all_gather(shared, ALL, axis=0, tiled=True)
        x = lax.all_gather(tokens, TP, axis=0, tiled=True)
        groups, group = lax.axis_size("grp"), lax.axis_index("grp")
        halo = lax.ppermute(x[x.shape[0] - 16 :], "grp", [(g, (g + 1) % groups) for g in range(groups)])
        at = jnp.stack([group, lax.axis_index(TP)])
        flags = plain_flags(docs, group, x.shape[0])
        return main, shared, x, halo, run_prep(groups, at, conv, head, gain), *flags, out_low, norm

    @staticmethod
    def first(spans, work, cotangent, out):
        *outs, end = launch(
            functools.partial(first_plain, spans), "project_scan", 2 * spans, work.in_specs, work.ins,
            [*work.out_specs, whole(PACK, WIDE)], [*work.outs, shape(PACK, WIDE)], work.scratch,
        )
        groups, group = lax.axis_size("grp"), lax.axis_index("grp")
        ends = lax.all_gather(end, "grp")

        def one(g, carried):
            return jnp.where(g < group, ends[g, NSTATE : NSTATE + 1] * carried + ends[g, :NSTATE], carried)

        inc = lax.fori_loop(0, groups, one, jnp.zeros((NSTATE, WIDE), f32))
        every = lax.all_gather(out, ALL, axis=0, tiled=True).reshape(HERE, PLANE, HEAD_DIM, D)
        wo = lax.dynamic_index_in_dim(every, lax.axis_index(TP), 1, False).reshape(WIDE, D)
        return *outs, inc, lax.all_gather(cotangent, TP, axis=0, tiled=True), wo

    @staticmethod
    def second(spans, work):
        y, gno, sums = launch(
            second_kernel, "scan_carry", spans, work.in_specs, work.ins,
            [*work.out_specs, spec((1, 2, SPAN), lambda s: (s, 0, 0))], [*work.outs, shape(spans, 2, SPAN)],
        )
        return y, gno, lax.all_gather(sums, TP)

    @staticmethod
    def third(spans, work):
        start = (whole(PACK, WIDE), shape(PACK, WIDE))
        mix = (work.later(D), shape(spans * SPAN, D))
        *outs, start, mix = launch(
            functools.partial(third_plain, spans), "gate_norm_back", 2 * spans, work.in_specs, work.ins,
            [*work.out_specs, start[0], mix[0]], [*work.outs, start[1], mix[1]], work.scratch,
        )
        return *outs, lax.all_gather(start, "grp"), lax.psum_scatter(mix, TP, scatter_dimension=0, tiled=True)

    @staticmethod
    def fourth(spans, work, gout, ggw, mix):
        rows = spans * SPAN
        gpre, hsum, gst, gstep = launch(
            fourth_plain, "scan_back", spans, work.in_specs, work.ins,
            [*work.out_specs, spec((SPAN, STATES), lambda s: (s, 0)), spec((8, SPAN), lambda s: (0, s))],
            [shape(rows, WIDE), work.outs[1], shape(rows, STATES), shape(8, rows)], work.scratch,
        )
        groups = lax.axis_size("grp")
        back = [(g, (g - 1) % groups) for g in range(groups)]
        swap = lambda a: lax.all_to_all(a, TP, split_axis=0, concat_axis=0, tiled=True)
        blocks = gst.reshape(PLANE, SPAN, STATES)
        tails = jnp.concatenate([blocks[1:, 0:8], lax.ppermute(gst[0:8], "grp", back)[None]], axis=0)
        steps = gstep.reshape(8, PLANE, SPAN).transpose(1, 0, 2)
        empty = jnp.zeros((HERE, PLANE, HEAD_DIM, D), f32)
        mine = gout.reshape(HERE, HEAD_DIM, D)
        every = lax.dynamic_update_index_in_dim(empty, mine, lax.axis_index(TP), 1).reshape(INNER, D)
        out = lax.psum_scatter(every, ALL, scatter_dimension=0, tiled=True)
        gpre = jnp.concatenate([gpre, lax.ppermute(gpre[0:8], "grp", back)], axis=0)
        return gpre, hsum, [swap(blocks)], swap(tails), swap(steps), [out], [mix], ggw

    @staticmethod
    def fifth(spans, work, ggw, grad_state, gout, rest):
        gp, giw, small = launch(
            functools.partial(fifth_plain, spans), "conv_back", spans, work.in_specs, work.ins,
            [spec((SPAN, D), lambda s: (s, 0)), whole(WIDE, D), whole(SMALL, WIDE)],
            [shape(spans * SPAN, D), shape(WIDE, D), shape(SMALL, WIDE)],
            [*work.scratch, pltpu.VMEM((SPAN, WIDE), bf16)],
        )
        inner_z = lax.psum_scatter(giw.T, "grp", scatter_dimension=0, tiled=True)
        gate_z = lax.psum_scatter(ggw.T, "grp", scatter_dimension=0, tiled=True)
        rows = inner_z.shape[0] // PLANE
        home = lambda a: lax.all_to_all(a.reshape(PLANE, rows, WIDE), TP, split_axis=0, concat_axis=0, tiled=True)
        state = lax.psum_scatter(grad_state, ALL, scatter_dimension=0, tiled=True)
        small = lax.all_gather(lax.psum(small, "grp"), TP)
        gp = lax.psum_scatter(gp, TP, scatter_dimension=0, tiled=True)
        return home(gate_z), home(inner_z), state[None], run_seventh([gp], *rest), small, [], gout

    @staticmethod
    def total(part):
        return lax.psum(part, ALL)[None]


def run_pack(in_weight, out_weight):
    rows = in_weight.shape[0]
    return pl.pallas_call(
        pack_kernel,
        out_shape=[shape(PLANE, rows, MAIN, dtype=bf16), shape(rows, SHARED, dtype=bf16),
                   shape(*out_weight.shape, dtype=bf16)],
        compiler_params=pltpu.CompilerParams(vmem_limit_bytes=SMALL_LIMIT),
        name="pack_weights",
    )(in_weight, out_weight)


def plain_flags(doc_ids, group, rows):
    spans = rows // SPAN
    padded = jnp.concatenate([jnp.full((8,), -1, jnp.int32), doc_ids, jnp.full((8,), -2, jnp.int32)])
    window = lax.dynamic_slice(padded, (group * rows,), (rows + 16,))
    now = window[8:]
    lags = [now == window[8 - k : rows + 16 - k] for k in range(1, CONV)]
    by_span = window[8 : rows + 8].reshape(spans, SPAN)
    rise = by_span == window[7 : rows + 7 : SPAN][:, None]
    tail = by_span == by_span[:, SPAN - 1 :]
    fill = lambda a: jnp.pad(a.reshape(rows), (0, 8))
    zero = jnp.zeros_like(now)
    flags = jnp.stack([a.astype(f32) for a in (*lags, fill(rise), fill(tail), now, zero, zero)], axis=1)
    return flags, by_span.astype(f32).reshape(spans, 1, SPAN)


def shards(
    plan,
    tokens, cotangent, doc_ids, norm_gain, in_weight, conv_params, head_params, out_gain, out_weight,
    norm_first, norm_second, in_first, in_second, conv_first, conv_second, head_first, head_second,
    gain_first, gain_second, out_first, out_second,
):
    groups = lax.axis_size("grp")
    group = lax.axis_index("grp")
    place = lax.axis_index(TP)
    tok_rows = tokens.shape[0]
    rows = PLANE * tok_rows
    spans = rows // SPAN

    wm, ws, x, halo, prepared, flags, doc_rows, out_low, norm_row = plan.start(
        in_weight, out_weight, tokens, doc_ids, conv_params, head_params, out_gain.reshape(INNER // 128, 128),
        norm_gain.reshape(1, D),
    )
    conv, bias, rate, skip, gain, pick, before_us, behind_us = prepared

    normed, gate, chan, pre, act, dt, cum, held, pref, edge, part, incoming, cot, wo = plan.first(
        spans, First(spans, x, halo, norm_row, wm, ws, pick, conv, bias, rate, flags, doc_rows, skip, before_us),
        cotangent, out_low,
    )
    y, gno, sums = plan.second(spans, Second(spans, act, cum, flags, held, pref, incoming, part, gate, cot, wo, gain))
    gy, ggate, behind, suff, gog, gskip, gout, ggw, starts, mix = plan.third(
        spans, Third(spans, y, gate, gno, sums, act, cum, flags, gain, cot, wo, normed)
    )
    gpre, hsum, parts, tails, steps, gout, mix, ggw = plan.fourth(
        spans,
        Fourth(spans, act, dt, cum, flags, doc_rows, held, pref, incoming, behind, suff, starts, behind_us, gy, pre,
               skip, rate),
        gout, ggw, mix,
    )
    gs, gconv_state, grad_state = run_sixth(parts, tails, steps, flags, chan, edge, conv, tokens, norm_row)
    g_gate, g_inner, g_shared, tokens_back, small, spare, grads_out = plan.fifth(
        spans,
        Fifth(spans, gpre, flags, chan, edge, conv, normed, gconv_state, gog, gskip, hsum, ggate, wm),
        ggw, grad_state, gout, (mix, gs, ws, tokens, cotangent, norm_row),
    )
    *results, grad_norm_gain = tokens_back
    in_f, in_s, in_u, out_f, out_s, out_u, sums, mixed, grad_tokens = run_adam(
        results, g_gate, g_inner, g_shared, grad_norm_gain, in_weight, in_first, in_second,
        out_weight, out_first, out_second, grads_out, spare,
    )
    norm3 = [a.reshape(D // 128, 128) for a in (norm_gain, norm_first, norm_second)]
    gain3 = [a.reshape(INNER // 128, 128) for a in (out_gain, gain_first, gain_second)]
    params = [*norm3, conv_params, conv_first, conv_second, head_params, head_first, head_second, *gain3]
    in_w, out_w, *rest = run_last(plan.total(sums), small, [in_weight, in_u, out_weight, out_u], params)
    rest[0:3] = [a.reshape(D) for a in rest[0:3]]
    rest[9:12] = [a.reshape(INNER) for a in rest[9:12]]
    return (mixed, grad_tokens, *rest[0:3], in_f, in_s, in_w, *rest[3:12], out_f, out_s, out_w)


def solution(mesh):
    seq = mesh.shape["seq"]
    sub = PLANE // seq
    groups = mesh.shape["fsdp"] // sub
    cut = Mesh(mesh.devices.reshape(groups, sub, seq), ALL)
    plan = Direct if (groups, sub, seq) == (4, 4, 2) else Plain
    split = P(ALL, None)
    none = P()
    return jax.shard_map(
        functools.partial(shards, plan),
        mesh=cut,
        in_specs=(split, split, none, none, split, none, none, none, split, none, none, split, split)
        + (none,) * 6
        + (split, split),
        out_specs=(split, split) + (none,) * 3 + (split,) * 3 + (none,) * 9 + (split,) * 3,
        check_vma=False,
    )
```
